32 devices in a mesh: batch: 8 (over y, x, core), head: 4 (over z).
Axes of the slice: x: 2, y: 2, z: 4, core: 2. Of those that a mesh axis runs over, the one named last changes fastest.
Arguments:
- stream: bfloat16 [32768, 512], P(('batch', 'head')), may hold values from -3 to 3
- accumulator: float32 [32768, 512], P(('batch', 'head')), may hold values from -3 to 3
- inward: bfloat16 [3, 512, 512], P(None, None, 'head'), may hold values from -0.375 to 0.375
- inward_bias: bfloat16 [2, 512], P(None, 'head'), may hold values from -2.5 to 2.5
- outward: bfloat16 [512, 512], replicated, may hold values from -0.75 to 0.75
- outward_bias: float32 [512], replicated, may hold values from -2.5 to 2.5
- first_gain: float32 [512], replicated, may hold values from 0.25 to 1.75
- first_shift: float32 [512], replicated, may hold values from -2.5 to 2.5
- up_weight: bfloat16 [512, 2048], replicated, may hold values from -0.25 to 0.25
- up_bias: float32 [2048], replicated, may hold values from -2.5 to 2.5
- down_weight: bfloat16 [2048, 512], replicated, may hold values from -0.125 to 0.125
- down_bias: float32 [512], replicated, may hold values from -2.5 to 2.5
- second_gain: float32 [512], replicated, may hold values from 0.25 to 1.75
- second_shift: float32 [512], replicated, may hold values from -2.5 to 2.5
- long_count: int32 [8], P('batch'), may hold values from 0 to 4, as said below
- stream_cotangent: float32 [32768, 512], P(('batch', 'head')), may hold values from -3 to 3
- accumulator_cotangent: float32 [32768, 512], P(('batch', 'head')), may hold values from -3 to 3
Outputs:
- next_stream: bfloat16 [32768, 512], P(('batch', 'head'))
- next_accumulator: float32 [32768, 512], P(('batch', 'head'))
- stream_gradient: float32 [32768, 512], P(('batch', 'head'))
- inward_gradient: float32 [3, 512, 512], P(None, None, 'head')
- inward_bias_gradient: float32 [2, 512], P(None, 'head')
- outward_gradient: float32 [512, 512], replicated
- outward_bias_gradient: float32 [512], replicated
- first_gain_gradient: float32 [512], replicated
- first_shift_gradient: float32 [512], replicated
- up_weight_gradient: float32 [512, 2048], replicated
- up_bias_gradient: float32 [2048], replicated
- down_weight_gradient: float32 [2048, 512], replicated
- down_bias_gradient: float32 [512], replicated
- second_gain_gradient: float32 [512], replicated
- second_shift_gradient: float32 [512], replicated
The draws below stay inside these ranges and needn't reach their ends.
Inputs may be any that keep to these rules, and one draw needn't show every extreme that they name: `long_count`: long sequences of 1024 tokens come first in their group, then sequences of 256 tokens fill it. Some group holds only long sequences and some holds none.
All inputs are finite; a program needn't handle non-finite values.
Results may differ from the reference program's by a relative error of at most 0.015.
Values may be sent and summed in bfloat16 or wider, within the bound.
No kernel may reach another device: no remote copies, remote signals or barrier semaphores. Data moves between devices by JAX's collectives and lax.ppermute only.
A program may use at most 128 MiB of HBM per device.

```python
import math
import jax
import jax.numpy as jnp
from jax import lax

D = 512
HEADS = 8
HEAD_DIM = 64
FF = 2048
LONG = 1024
SHORT = 256
GROUP = 4096
TOKENS = 32768
N_BATCH = 8


def draw_long_count(key, part):
    key = jax.random.fold_in(key, 7)
    key_one, key_two, key_three = jax.random.split(key, 3)
    most_long = GROUP // LONG
    counts = jax.random.randint(key_one, (N_BATCH,), 0, most_long + 1)
    first_pick = jax.random.randint(key_two, (), 0, N_BATCH)
    other_pick = (first_pick + 1 + jax.random.randint(key_three, (), 0, N_BATCH - 1)) % N_BATCH
    return counts.at[first_pick].set(most_long).at[other_pick].set(0).astype(jnp.int32)


def draw_stream(key, part):
    key = jax.random.fold_in(key, 11)
    values = jax.random.normal(key, (TOKENS, D), jnp.float32)
    return jnp.clip(values, -3.0, 3.0).astype(jnp.bfloat16)


def steps_of(stream_key, extent, cuts, least, largest):
    def one(axis_at, blocks):
        heights = jax.random.uniform(jax.random.fold_in(jax.random.fold_in(stream_key, 6), axis_at), (blocks,), jnp.float32, least / len(cuts), largest / len(cuts))
        return jnp.repeat(jnp.exp(heights), extent[axis_at] // blocks).reshape((-1,) + (1,) * (len(extent) - axis_at - 1))

    level = one(*cuts[0])
    for cut in cuts[1:]:
        level = level * one(*cut)
    return level


def bell_draw(rng, extent, deviation, most, cuts=(), held_as=jnp.bfloat16):
    result = jax.random.normal(rng, extent, jnp.float32) * deviation
    if len(cuts) > 0:
        result = steps_of(rng, extent, cuts, -0.22, 0.18) * result
    return jnp.clip(result, min=-most, max=most).astype(held_as)


def setup_inputs(seed: int = 0) -> dict:
    splits = jax.random.split(jax.random.key(seed), 18)
    stream = draw_stream(jax.random.fold_in(splits[17], 71), 0)
    accumulator = bell_draw(splits[1], (TOKENS, D), 1.0, 3.0, ((0, 32),), jnp.float32)
    inward = bell_draw(splits[2], (3, D, D), (D // 2) ** -0.5, 0.375, ((2, 4),))
    inward_bias = bell_draw(splits[3], (2, D), 0.5, 2.5, ((1, 4),))
    outward = bell_draw(splits[4], (D, D), (D // 8) ** -0.5, 0.75)
    outward_bias = bell_draw(splits[5], (D,), 0.5, 2.5, (), jnp.float32)
    first_gain = jnp.clip(1.0 + 0.15 * jax.random.normal(splits[6], (D,), jnp.float32), 0.25, 1.75)
    first_shift = bell_draw(splits[7], (D,), 0.5, 2.5, (), jnp.float32)
    up_weight = bell_draw(splits[8], (D, FF), D ** -0.5, 0.25)
    up_bias = bell_draw(splits[9], (FF,), 0.5, 2.5, (), jnp.float32)
    down_weight = bell_draw(splits[10], (FF, D), FF ** -0.5, 0.125)
    down_bias = bell_draw(splits[11], (D,), 0.5, 2.5, (), jnp.float32)
    second_gain = jnp.clip(1.0 + 0.15 * jax.random.normal(splits[12], (D,), jnp.float32), 0.25, 1.75)
    second_shift = bell_draw(splits[13], (D,), 0.5, 2.5, (), jnp.float32)
    long_count = draw_long_count(jax.random.fold_in(splits[17], 71), 0)
    stream_cotangent = bell_draw(splits[15], (TOKENS, D), 1.0, 3.0, ((0, 32),), jnp.float32)
    accumulator_cotangent = bell_draw(splits[16], (TOKENS, D), 1.0, 3.0, ((0, 32),), jnp.float32)
    return dict(stream=stream, accumulator=accumulator, inward=inward, inward_bias=inward_bias, outward=outward, outward_bias=outward_bias, first_gain=first_gain, first_shift=first_shift, up_weight=up_weight, up_bias=up_bias, down_weight=down_weight, down_bias=down_bias, second_gain=second_gain, second_shift=second_shift, long_count=long_count, stream_cotangent=stream_cotangent, accumulator_cotangent=accumulator_cotangent)


@jax.custom_vjp
def low(v):
    return lax.optimization_barrier(v.astype(jnp.bfloat16)).astype(jnp.float32)

@jax.custom_vjp
def low_back(v):
    return v

def low_keep(v):
    return (low(v), None)

def low_pass(kept, grad):
    return (grad,)

def back_keep(v):
    return (v, None)

def back_low(kept, grad):
    return (low(grad),)
low.defvjp(low_keep, low_pass)
low_back.defvjp(back_keep, back_low)
HIGHEST = lax.Precision.HIGHEST

def layer_norm(hidden, norm_gain, norm_shift):
    average = lax.optimization_barrier(jnp.mean(hidden, -1, keepdims=True))
    centered = hidden - average
    variance = lax.optimization_barrier(jnp.mean(centered * centered, -1, keepdims=True))
    return centered * lax.rsqrt(variance + 1e-05) * norm_gain + norm_shift

def smooth_act(values):
    return jax.nn.gelu(values, approximate=False)

def segment_keys(positions, limit_rows):
    return jnp.where(positions < limit_rows, -1 - positions // LONG, positions // SHORT)

def attend_block(operands):
    query_rows, key_rows, value_rows, segment = operands
    scores = low_back(jnp.einsum('qhe,khe->hqk', query_rows, key_rows, precision=HIGHEST) * (1.0 / math.sqrt(HEAD_DIM)))
    allowed = segment[:, None] == segment[None, :]
    scores = jnp.where(allowed[None], scores, -1e+30)
    attend_full = jax.nn.softmax(scores, axis=-1)
    return jnp.einsum('hqk,khe->qhe', low(attend_full), value_rows, precision=HIGHEST)

def forward(params, segment):
    stream, accumulator, inward, inward_bias, outward, outward_bias, first_gain, first_shift, up_weight, up_bias, down_weight, down_bias, second_gain, second_shift = params
    projected = jnp.einsum('td,cde->cte', stream, inward, precision=HIGHEST)
    queries = low_back(low(projected[0] + inward_bias[0]))
    key_vectors = low_back(low(projected[1]))
    value_vectors = low_back(low(projected[2] + inward_bias[1]))
    blocks = stream.shape[0] // LONG
    block_shape = (blocks, LONG, HEADS, HEAD_DIM)
    head_output = lax.map(jax.checkpoint(attend_block), (queries.reshape(block_shape), key_vectors.reshape(block_shape), value_vectors.reshape(block_shape), segment.reshape(blocks, LONG)))
    head_output = low_back(low(head_output.reshape(stream.shape)))
    attention = low_back(jnp.dot(head_output, outward, precision=HIGHEST) + outward_bias)
    first_norm = layer_norm(stream + attention, first_gain, first_shift)
    preactivation = low_back(jnp.dot(low(first_norm), up_weight, precision=HIGHEST) + up_bias)
    hidden = low(smooth_act(preactivation))
    branch = low_back(jnp.dot(hidden, down_weight, precision=HIGHEST) + down_bias)
    second_norm = layer_norm(first_norm + branch, second_gain, second_shift)
    return (second_norm, accumulator + attention + branch)

def reference(stream, accumulator, inward, inward_bias, outward, outward_bias, first_gain, first_shift, up_weight, up_bias, down_weight, down_bias, second_gain, second_shift, long_count, stream_cotangent, accumulator_cotangent):
    positions = jnp.arange(stream.shape[0], dtype=jnp.int32)
    within = (positions % GROUP).astype(jnp.int32)
    limit_rows = (long_count[positions // GROUP] * LONG).astype(jnp.int32)
    segment = segment_keys(within, limit_rows)
    floats = tuple((element.astype(jnp.float32) for element in (stream, accumulator, inward, inward_bias, outward, outward_bias, first_gain, first_shift, up_weight, up_bias, down_weight, down_bias, second_gain, second_shift)))

    def run_layer(params):
        return forward(params, segment)
    outputs, pullback = jax.vjp(run_layer, floats)
    grads = pullback((stream_cotangent.astype(jnp.float32), accumulator_cotangent.astype(jnp.float32)))[0]
    return (outputs[0].astype(jnp.bfloat16), outputs[1], grads[0], grads[2], grads[3], grads[4], grads[5], grads[6], grads[7], grads[8], grads[9], grads[10], grads[11], grads[12], grads[13])
```

```python
import math

import jax
import jax.numpy as jnp
from jax import lax
from jax.experimental import pallas as pl
from jax.experimental.pallas import tpu as pltpu
from jax.sharding import PartitionSpec as P

F32, BF = jnp.float32, jnp.bfloat16
ROWS, D, FF, PAIR, HD, SHORT = 1024, 512, 2048, 128, 64, 256
QB = 256
VMEM = 60 << 20
def dot(a, b): return lax.dot_general(a, b, (((1,), (0,)), ((), ())), preferred_element_type=F32)
def dot_nt(a, b): return lax.dot_general(a, b, (((1,), (1,)), ((), ())), preferred_element_type=F32)
def dot_tn(a, b): return lax.dot_general(a, b, (((0,), (0,)), ((), ())), preferred_element_type=F32)
def cp(n=1, **k): return pltpu.CompilerParams(dimension_semantics=("arbitrary",) * n, vmem_limit_bytes=VMEM, **k)

def fwd_kernel(flag, x, w, bias, e, o, qkv, rl, vt):
    wc = jnp.concatenate([w[0, 0], w[0, 1], w[0, 2]], axis=1)
    p = dot(x[...], wc)
    bq = bias[0, 0:1].astype(F32); bv = bias[0, 1:2].astype(F32)
    q = ((p[:, :PAIR] + bq).astype(BF).astype(F32) * (1.0 / math.sqrt(HD))).astype(BF)
    k = p[:, PAIR:2 * PAIR].astype(BF)
    v = (p[:, 2 * PAIR:] + bv)
    qkv[:, :PAIR] = q
    qkv[:, PAIR:2 * PAIR] = k
    qkv[:, 2 * PAIR:] = v.astype(BF)
    lane = lax.broadcasted_iota(jnp.int32, (1, PAIR), 1)
    vT = v.T.astype(BF)
    for h in range(2):
        vt[h, :HD] = vT[h * HD:(h + 1) * HD]
        vt[h, HD:] = jnp.ones((16, ROWS), BF)
    def block(qb, k0, kn):
        qs = slice(qb * QB, (qb + 1) * QB)
        parts, inv = [], []
        for h in range(2):
            qh = jnp.where(lane // HD == h, qkv[qs, :PAIR], jnp.zeros((), BF))
            s = dot_nt(qkv[k0:k0 + kn, PAIR:2 * PAIR], qh)
            m = jnp.max(s, axis=0, keepdims=True)
            ex = jnp.exp(s - m).astype(BF)
            e[0, h, 0:kn, qs] = ex
            ot = dot(vt[h, :, k0:k0 + kn], ex)
            r = 1.0 / ot[HD:HD + 1]
            parts.append(ot[:HD] * r)
            inv.append(jnp.broadcast_to(r, (HD, QB)))
        o[qs, :] = jnp.concatenate(parts, 0).T.astype(BF)
        rl[0, qs, :] = jnp.concatenate(inv, 0).T
    @pl.when(flag[0] == 1)
    def _():
        for qb in range(ROWS // QB): block(qb, 0, ROWS)
    @pl.when(flag[0] == 0)
    def _():
        for qb in range(ROWS // QB): block(qb, qb * QB, QB)

def attention_forward(flag, x, w, bias):
    n = w.shape[0]
    return pl.pallas_call(
        fwd_kernel, grid=(n,),
        in_specs=[pl.BlockSpec(memory_space=pltpu.SMEM),
                  pl.BlockSpec((ROWS, D), lambda i: (0, 0)),
                  pl.BlockSpec((1, 3, D, PAIR), lambda i: (i, 0, 0, 0)),
                  pl.BlockSpec((1, 2, PAIR), lambda i: (i, 0, 0))],
        out_specs=[pl.BlockSpec((1, 2, ROWS, ROWS), lambda i: (i, 0, 0, 0)),
                   pl.BlockSpec((ROWS, PAIR), lambda i: (0, i)),
                   pl.BlockSpec((ROWS, 3 * PAIR), lambda i: (0, i)),
                   pl.BlockSpec((1, ROWS, PAIR), lambda i: (i, 0, 0))],
        out_shape=[jax.ShapeDtypeStruct((n, 2, ROWS, ROWS), BF),
                   jax.ShapeDtypeStruct((ROWS, n * PAIR), BF),
                   jax.ShapeDtypeStruct((ROWS, n * 3 * PAIR), BF),
                   jax.ShapeDtypeStruct((n, ROWS, PAIR), F32)],
        scratch_shapes=[pltpu.VMEM((2, HD + 16, ROWS), BF)],
        compiler_params=cp(),
    )(flag, x, w, bias)

def bwd_kernel(flag, x, e, qkv, o, do, rl, g, wg, bg, vaug, doaug, ds, kt):
    lane = lax.broadcasted_iota(jnp.int32, (1, PAIR), 1)
    zero = jnp.zeros((), BF)
    dof = do[...].astype(F32) * rl[0]
    dob = dof.astype(BF)
    t = dof * o[...].astype(F32)
    th = t.astype(BF)
    tl = (t - th.astype(F32)).astype(BF)
    row = lax.broadcasted_iota(jnp.int32, (PAIR, PAIR), 0)
    col = lax.broadcasted_iota(jnp.int32, (PAIR, PAIR), 1)
    pick = jnp.where((row // HD != col // HD) & (col % HD < 2), 1.0, 0.0).astype(BF)
    delta = -(dot(th, pick) + dot(tl, pick))
    dh = delta.astype(BF)
    dl = (delta - dh.astype(F32)).astype(BF)
    dd = jnp.where(lane % HD == 0, dh, dl)
    v = qkv[:, 2 * PAIR:]
    one = jnp.ones((), BF)
    for h in range(2):
        own = lane // HD == h
        aug = (lane // HD != h) & (lane % HD < 2)
        vaug[h] = jnp.where(own, v, jnp.where(aug, one, zero))
        doaug[h] = jnp.where(own, dob, jnp.where(aug, dd, zero))
    kt[...] = qkv[:, PAIR:2 * PAIR].astype(F32).T.astype(BF)
    def score_grad(h, qs, k0, kn):
        dp = dot_nt(vaug[h, k0:k0 + kn], doaug[h, qs])
        return (e[0, h, 0:kn, qs].astype(F32) * dp).astype(BF)
    @pl.when(flag[0] == 1)
    def _():
        for qb in range(ROWS // QB):
            qs = slice(qb * QB, (qb + 1) * QB)
            dq = []
            for h in range(2):
                d = score_grad(h, qs, 0, ROWS)
                ds[h, :, qs] = d
                dq.append(dot(kt[h * HD:(h + 1) * HD], d))
            g[qs, :PAIR] = (jnp.concatenate(dq, 0).T * (1.0 / math.sqrt(HD))).astype(BF)
        q0 = [jnp.where(lane // HD == h, qkv[:, :PAIR], zero) for h in range(2)]
        d0 = [jnp.where(lane // HD == h, doaug[h], zero) for h in range(2)]
        for kb in range(ROWS // QB):
            ks = slice(kb * QB, (kb + 1) * QB)
            dk = dot(ds[0, ks], q0[0]) + dot(ds[1, ks], q0[1])
            dv = dot(e[0, 0, ks], d0[0]) + dot(e[0, 1, ks], d0[1])
            g[ks, PAIR:2 * PAIR] = dk.astype(BF)
            g[ks, 2 * PAIR:] = dv.astype(BF)
    @pl.when(flag[0] == 0)
    def _():
        for qb in range(ROWS // QB):
            qs = slice(qb * QB, (qb + 1) * QB)
            dq, dk, dv = [], 0.0, 0.0
            for h in range(2):
                own = lane // HD == h
                d = score_grad(h, qs, qb * QB, QB)
                dq.append(dot(kt[h * HD:(h + 1) * HD, qs], d))
                dk = dk + dot(d, jnp.where(own, qkv[qs, :PAIR], zero))
                dv = dv + dot(e[0, h, 0:QB, qs], jnp.where(own, doaug[h, qs], zero))
            g[qs, :PAIR] = (jnp.concatenate(dq, 0).T * (1.0 / math.sqrt(HD))).astype(BF)
            g[qs, PAIR:2 * PAIR] = dk.astype(BF)
            g[qs, 2 * PAIR:] = dv.astype(BF)
    gr = dot_tn(x[...], g[...])
    for c in range(3):
        wg[0, c] = gr[:, c * PAIR:(c + 1) * PAIR].astype(BF)
    bg[0, 0:1] = jnp.sum(g[:, :PAIR].astype(F32), 0, keepdims=True)
    bg[0, 1:2] = jnp.sum(g[:, 2 * PAIR:].astype(F32), 0, keepdims=True)

def attention_backward(flag, x, e, qkv, o, do, rl):
    n = e.shape[0]
    return pl.pallas_call(
        bwd_kernel, grid=(n,),
        in_specs=[pl.BlockSpec(memory_space=pltpu.SMEM),
                  pl.BlockSpec((ROWS, D), lambda i: (0, 0)),
                  pl.BlockSpec((1, 2, ROWS, ROWS), lambda i: (i, 0, 0, 0)),
                  pl.BlockSpec((ROWS, 3 * PAIR), lambda i: (0, i)),
                  pl.BlockSpec((ROWS, PAIR), lambda i: (0, i)),
                  pl.BlockSpec((ROWS, PAIR), lambda i: (0, i)),
                  pl.BlockSpec((1, ROWS, PAIR), lambda i: (i, 0, 0))],
        out_specs=[pl.BlockSpec((ROWS, 3 * PAIR), lambda i: (0, i)),
                   pl.BlockSpec((1, 3, D, PAIR), lambda i: (i, 0, 0, 0)),
                   pl.BlockSpec((1, 2, PAIR), lambda i: (i, 0, 0))],
        out_shape=[jax.ShapeDtypeStruct((ROWS, n * 3 * PAIR), BF),
                   jax.ShapeDtypeStruct((n, 3, D, PAIR), BF),
                   jax.ShapeDtypeStruct((n, 2, PAIR), F32)],
        scratch_shapes=[pltpu.VMEM((2, ROWS, PAIR), BF), pltpu.VMEM((2, ROWS, PAIR), BF),
                        pltpu.VMEM((2, ROWS, ROWS), BF), pltpu.VMEM((PAIR, ROWS), BF)],
        compiler_params=cp(),
    )(flag, x, e, qkv, o, do, rl)

TILE = 256
def gelu_parts(u):
    t = 1.0 / (1.0 + (0.3275911 * 0.7071067811865476) * jnp.abs(u))
    g = jnp.exp(u * u * -0.5)
    poly = t * (0.127414796 + t * (-0.142248368 + t * (0.7107068705 + t * (-0.7265760135 + t * 0.5307027145))))
    tail = poly * g
    cdf = jnp.where(u >= 0, 1.0 - tail, tail)
    return u * cdf, cdf + u * g * 0.3989422804014327

def norm_parts(h):
    m = jnp.mean(h, -1, keepdims=True)
    c = h - m
    v = jnp.mean(c * c, -1, keepdims=True)
    r = lax.rsqrt(v + 1e-5)
    return c * r, r
def norm_back(e, gain, z, r):
    eg = e * gain
    return r * (eg - jnp.mean(eg, -1, keepdims=True) - z * jnp.mean(eg * z, -1, keepdims=True))
def colsum(a): return jnp.sum(a, 0, keepdims=True)

def ffn_kernel(x, acc, oh, wo, bo, g1, s1, wu, bu, wd, bd, g2, s2, sc, ac,
               ns, na, fg, hg, dwo, dwu, dwd, vec, vup,
               low, hid, bgr, pgr, agr):
    i = pl.program_id(0)
    n = pl.num_programs(0)
    rs = pl.ds(pl.multiple_of(i * TILE, TILE), TILE)
    ot = oh[rs, :]
    att = dot(ot, wo[...]) + bo[...]
    z1, r1 = norm_parts(x[...].astype(F32) + att)
    first = z1 * g1[...] + s1[...]
    fl = first.astype(BF)
    low[rs, :] = fl
    u = dot(fl, wu[...]) + bu[...]
    a, ap = gelu_parts(u)
    ab = a.astype(BF)
    hid[rs, :] = ab
    br = dot(ab, wd[...]) + bd[...]
    na[...] = acc[...] + att + br
    z2, r2 = norm_parts(first + br)
    ns[...] = (z2 * g2[...] + s2[...]).astype(BF)
    e2 = sc[...]
    si = norm_back(e2, g2[...], z2, r2)
    bg = (si + ac[...]).astype(BF)
    bgr[rs, :] = bg
    pg = (dot_nt(bg, wd[...]) * ap).astype(BF)
    pgr[rs, :] = pg
    e1 = dot_nt(pg, wu[...]) + si
    fi = norm_back(e1, g1[...], z1, r1)
    fg[...] = fi
    ag = (fi + ac[...]).astype(BF)
    agr[rs, :] = ag
    hg[...] = dot_nt(ag, wo[...]).astype(BF)
    sums = [colsum(ag.astype(F32)), colsum(e1 * z1), colsum(e1), colsum(bg.astype(F32)), colsum(e2 * z2), colsum(e2)]
    @pl.when(i == 0)
    def _():
        vec[...] = jnp.zeros_like(vec)
        vup[...] = jnp.zeros_like(vup)
    for j, s in enumerate(sums): vec[j:j + 1, :] += s
    vup[0:1, :] += colsum(pg.astype(F32))
    @pl.when(i == n - 1)
    def _():
        dwd[...] = dot_tn(hid[...], bgr[...]).astype(BF)
        dwu[...] = dot_tn(low[...], pgr[...]).astype(BF)
        dwo[...] = dot_tn(oh[...], agr[...]).astype(BF)

def ffn(x, acc, oh, wo, bo, g1, s1, wu, bu, wd, bd, g2, s2, sc, ac):
    full = lambda a: pl.BlockSpec(a.shape, lambda i: (0,) * a.ndim)
    tile = pl.BlockSpec((TILE, D), lambda i: (i, 0))
    vs = [v.reshape(1, -1) for v in (bo, g1, s1, bu, bd, g2, s2)]
    bo, g1, s1, bu, bd, g2, s2 = vs
    S = jax.ShapeDtypeStruct
    outs = [S((ROWS, D), BF), S((ROWS, D), F32), S((ROWS, D), F32), S((ROWS, D), BF), S((D, D), BF), S((D, FF), BF), S((FF, D), BF), S((8, D), F32), S((8, FF), F32)]
    return pl.pallas_call(
        ffn_kernel, grid=(ROWS // TILE,),
        in_specs=[tile, tile, full(oh), full(wo), full(bo), full(g1), full(s1), full(wu), full(bu), full(wd), full(bd), full(g2), full(s2), tile, tile],
        out_specs=[tile, tile, tile, tile] + [full(s) for s in outs[4:]],
        out_shape=outs,
        scratch_shapes=[pltpu.VMEM((ROWS, D), BF), pltpu.VMEM((ROWS, FF), BF), pltpu.VMEM((ROWS, D), BF), pltpu.VMEM((ROWS, FF), BF), pltpu.VMEM((ROWS, D), BF)],
        compiler_params=cp(),
    )(x, acc, oh, wo, bo, g1, s1, wu, bu, wd, bd, g2, s2, sc, ac)

def back_stream_kernel(fg, g, w, out):
    t = fg[...]
    n = w.shape[0]
    for s in range(n):
        wc = jnp.concatenate([w[s, 0], w[s, 1], w[s, 2]], axis=1)
        t = t + dot_nt(g[:, s * 3 * PAIR:(s + 1) * 3 * PAIR], wc)
    out[...] = t
def back_stream(fg, g, w):
    T = 256
    return pl.pallas_call(
        back_stream_kernel, grid=(ROWS // T,),
        in_specs=[pl.BlockSpec((T, D), lambda i: (i, 0)), pl.BlockSpec((T, g.shape[1]), lambda i: (i, 0)),
                  pl.BlockSpec(w.shape, lambda i: (0, 0, 0, 0))],
        out_specs=pl.BlockSpec((T, D), lambda i: (i, 0)),
        out_shape=jax.ShapeDtypeStruct((ROWS, D), F32),
        compiler_params=cp(),
    )(fg, g, w)


def body(stream, accumulator, inward, inward_bias, outward, outward_bias, first_gain, first_shift, up_weight, up_bias,
         down_weight, down_bias, second_gain, second_shift, long_count, stream_cotangent, accumulator_cotangent):
    assert stream.shape == (ROWS, D)
    both = ("batch", "head")
    me = lax.axis_index("head")
    n_head, width = lax.axis_size("head"), inward.shape[2]
    pairs = D // PAIR
    flag = (me < long_count).astype(jnp.int32)
    full = lax.all_gather(inward, "head", axis=2, tiled=True)
    full_bias = lax.all_gather(inward_bias, "head", axis=1, tiled=True)
    w = full.reshape(3, D, pairs, PAIR).transpose(2, 0, 1, 3)
    b = full_bias.reshape(2, pairs, PAIR).transpose(1, 0, 2)
    e, o, qkv, rl = attention_forward(flag, stream, w, b)
    ns, na, fg, hg, dwo, dwu, dwd, vec, vup = ffn(
        stream, accumulator, o, outward, outward_bias, first_gain, first_shift, up_weight, up_bias, down_weight, down_bias,
        second_gain, second_shift, stream_cotangent, accumulator_cotangent)
    dwo, dwu, dwd, vec, vup = lax.psum((dwo, dwu, dwd, vec.astype(BF), vup.astype(BF)), both)
    g, wg, bg = attention_backward(flag, stream, e, qkv, o, hg, rl)
    sg = back_stream(fg, g, w)
    wg = wg.transpose(1, 2, 0, 3).reshape(3, D, D)
    bg = bg.astype(BF).transpose(1, 0, 2).reshape(2, D)
    wg = lax.psum(lax.psum_scatter(wg, "head", scatter_dimension=2, tiled=True), "batch").astype(F32)
    bg = lax.psum(lax.psum_scatter(bg, "head", scatter_dimension=1, tiled=True), "batch").astype(F32)
    dwo, dwu, dwd, vec, vup = (a.astype(F32) for a in (dwo, dwu, dwd, vec, vup))
    return (ns, na, sg, wg, bg, dwo, vec[0], vec[1], vec[2], dwu, vup[0], dwd, vec[3], vec[4], vec[5])


def solution(mesh):
    tokens = P(("batch", "head"), None)
    in_specs = (tokens, tokens, P(None, None, "head"), P(None, "head")) + (P(),) * 10 + (P("batch"), tokens, tokens)
    out_specs = (tokens,) * 3 + (P(None, None, "head"), P(None, "head")) + (P(),) * 10
    return jax.shard_map(body, mesh=mesh, in_specs=in_specs, out_specs=out_specs, check_vma=False)
```

```python
import math

import jax
import jax.numpy as jnp
from jax import lax
from jax.experimental import pallas as pl
from jax.experimental.pallas import tpu as pltpu
from jax.sharding import PartitionSpec as P

F32, BF = jnp.float32, jnp.bfloat16
ROWS, D, FF, PAIR, HD, SHORT = 1024, 512, 2048, 128, 64, 256
QB = 256
SCALE = 1.0 / math.sqrt(HD)


def dot(a, b):
    return lax.dot_general(a, b, (((1,), (0,)), ((), ())), preferred_element_type=F32)


def dot_nt(a, b):
    return lax.dot_general(a, b, (((1,), (1,)), ((), ())), preferred_element_type=F32)


def dot_tn(a, b):
    return lax.dot_general(a, b, (((0,), (0,)), ((), ())), preferred_element_type=F32)


def params(n=1, mib=60):
    return pltpu.CompilerParams(dimension_semantics=("arbitrary",) * n or None, vmem_limit_bytes=mib << 20)


def cost(flops, nbytes):
    return pl.CostEstimate(flops=int(flops), bytes_accessed=int(nbytes), transcendentals=0)


SMEM = pl.BlockSpec(memory_space=pltpu.SMEM)
VM = pl.BlockSpec(memory_space=pltpu.VMEM)
ANY = pl.BlockSpec(memory_space=pl.ANY)


def whole(shape):
    return pl.BlockSpec(shape, lambda *_: (0,) * len(shape))


HALF = D // 2
PACK = 3 * HALF + 16


def side(w):
    return jnp.concatenate([w[c * HALF : (c + 1) * HALF] for c in range(3)], axis=1)


def fwd_kernel(n_pairs, code, x, *refs):
    was, wbs = refs[:n_pairs], refs[n_pairs : 2 * n_pairs]
    e, o, qkv, rl, es, qs_, sems, qsems = refs[2 * n_pairs :]
    ca = pl.multiple_of(code[0] * HALF, HALF)
    cb = pl.multiple_of(HALF - code[0] * HALF, HALF)
    lane = lax.broadcasted_iota(jnp.int32, (1, PAIR), 1)

    def run(short):
        n = QB if short else ROWS
        copies = []

        def keys(qb):
            return slice(qb * QB, (qb + 1) * QB) if short else slice(0, ROWS)

        def project(a):
            wa, wb = was[a], wbs[a]
            p = dot(x[:, pl.ds(ca, HALF)], side(wa)) + dot(x[:, pl.ds(cb, HALF)], side(wb))
            bq, bv = wa[3 * HALF : 3 * HALF + 1].astype(F32), wa[3 * HALF + 1 : 3 * HALF + 2].astype(F32)
            q = ((p[:, :PAIR] + bq).astype(BF).astype(F32) * SCALE).astype(BF)
            k = p[:, PAIR : 2 * PAIR].astype(BF)
            v = (p[:, 2 * PAIR :] + bv).astype(BF)
            qs_[a, :, :PAIR] = q
            qs_[a, :, PAIR : 2 * PAIR] = k
            qs_[a, :, 2 * PAIR :] = v
            copies.append(pltpu.make_async_copy(qs_.at[a], qkv.at[a], qsems.at[a]))
            copies[-1].start()
            return q, k, [jnp.where(lane // HD == h, v, jnp.ones((), BF)) for h in range(2)]

        ready = {0: project(0)}

        def score(item):
            a, qb, h = item
            q, k, _ = ready[a]
            qh = jnp.where(lane // HD == h, q[qb * QB : (qb + 1) * QB], jnp.zeros((), BF))
            return dot_nt(qh, k[keys(qb)])

        done = {}

        def product(item, ex):
            a, qb, h = item
            qs = slice(qb * QB, (qb + 1) * QB)
            u = dot(ex, ready[a][2][h][keys(qb)])
            r = 1.0 / pltpu.roll(u, HD, 1)
            done[h] = (u * r, r)
            if h == 1:
                o[qs, a * PAIR : (a + 1) * PAIR] = jnp.where(lane < HD, done[0][0], done[1][0]).astype(BF)
                rl[a, qs, :] = jnp.where(lane < HD, done[0][1], done[1][1])

        items = [(a, qb, h) for a in range(n_pairs) for qb in range(ROWS // QB) for h in range(2)]
        ahead, last = score(items[0]), None
        for i, item in enumerate(items):
            s = ahead
            if i + 1 < len(items):
                if items[i + 1][0] not in ready:
                    ready[items[i + 1][0]] = project(items[i + 1][0])
                ahead = score(items[i + 1])
            ex = jnp.exp(s - jnp.max(s, axis=1, keepdims=True)).astype(BF)
            a, qb, h = item
            at = (a, h, pl.ds(qb * QB, QB), pl.ds(0, n))
            es[at] = ex
            copies.append(pltpu.make_async_copy(es.at[at], e.at[at], sems.at[i]))
            copies[-1].start()
            if last is not None:
                product(*last)
            last = (item, ex)
        product(*last)
        for c in copies:
            c.wait()

    pl.when(code[1] == 1)(lambda: run(False))
    pl.when(code[1] == 0)(lambda: run(True))


def attention_forward(code, x, was, wbs):
    S, n = jax.ShapeDtypeStruct, len(was)
    return pl.pallas_call(
        lambda *refs: fwd_kernel(n, *refs),
        in_specs=[SMEM, VM] + [VM] * (2 * n),
        out_specs=[ANY, VM, ANY, VM],
        out_shape=[S((n, 2, ROWS, ROWS), BF), S((ROWS, n * PAIR), BF), S((n, ROWS, 3 * PAIR), BF), S((n, ROWS, PAIR), F32)],
        scratch_shapes=[pltpu.VMEM((n, 2, ROWS, ROWS), BF), pltpu.VMEM((n, ROWS, 3 * PAIR), BF),
                        pltpu.SemaphoreType.DMA((8 * n,)), pltpu.SemaphoreType.DMA((n,))],
        compiler_params=params(0),
        cost_estimate=cost(n * 6e9, n * 7 << 20),
    )(code, x, *was, *wbs)


PART, VROWS = 192, 64


def bwd_kernel(slots, at_o, last, code, x_, hg_, *refs):
    n = len(slots)
    es_, qkvs_, os_, rls_ = (refs[k * n : (k + 1) * n] for k in range(4))
    refs = refs[4 * n :]
    if last:
        (vec, vup, bg_in), refs = refs[:3], refs[3:]
        g_, keep, send, v_out, x, e, qkv, o, do, rl, ds, g, gsum, vrow, sems, gsems = refs
    else:
        g_, keep, send, bg_out, x, e, qkv, o, do, rl, ds, g, gsum, vrow, sems, gsems = refs
    lane = lax.broadcasted_iota(jnp.int32, (1, PAIR), 1)
    zero, one = jnp.zeros((), BF), jnp.ones((), BF)
    row = lax.broadcasted_iota(jnp.int32, (PAIR, PAIR), 0)
    col = lax.broadcasted_iota(jnp.int32, (PAIR, PAIR), 1)
    own = [lane // HD == h for h in range(2)]
    aug = [(lane // HD != h) & (lane % HD < 2) for h in range(2)]

    def run(short):
        n_keys = SHORT if short else ROWS
        tile = SHORT if short else 512
        items = [(qb, h) for qb in range(ROWS // tile) for h in range(2)]
        loads, stores = {}, []

        def load(key, src, dst):
            loads[key] = pltpu.make_async_copy(src, dst, sems.at[len(loads)])
            loads[key].start()

        for a, slot in enumerate(slots):
            load((a, "do"), hg_.at[:, pl.ds(slot * PAIR, PAIR)], do.at[a])
            load((a, "rl"), rls_[a].at[at_o[a]], rl.at[a])
            load((a, "o"), os_[a].at[:, pl.ds(at_o[a] * PAIR, PAIR)], o.at[a])
            load((a, "qkv"), qkvs_[a].at[at_o[a]], qkv.at[a])
            for qb, h in items:
                at = (h, pl.ds(qb * tile, tile), pl.ds(0, n_keys))
                load((a, qb, h), es_[a].at[(at_o[a], *at)], e.at[(a, *at)])
        load("x", x_, x)

        def keys(qb):
            return slice(qb * tile, (qb + 1) * tile) if short else slice(0, ROWS)

        for a in range(n):
            for k in ("do", "rl", "o", "qkv"):
                loads[a, k].wait()
            dof = do[a].astype(F32) * rl[a]
            dob = dof.astype(BF)
            t = dof * o[a].astype(F32)
            th = t.astype(BF)
            tl = (t - th.astype(F32)).astype(BF)
            pick = jnp.where((row // HD != col // HD) & (col % HD < 2), 1.0, 0.0).astype(BF)
            delta = -(dot(th, pick) + dot(tl, pick))
            dh = delta.astype(BF)
            dd = jnp.where(lane % HD == 0, dh, (delta - dh.astype(F32)).astype(BF))
            q, k, v = qkv[a, :, :PAIR], qkv[a, :, PAIR : 2 * PAIR], qkv[a, :, 2 * PAIR :]
            va = [jnp.where(own[h], v, jnp.where(aug[h], one, zero)) for h in range(2)]
            da = [jnp.where(own[h], dob, jnp.where(aug[h], dd, zero)) for h in range(2)]
            km = [jnp.where(own[h], k, zero) for h in range(2)]
            qt = q.astype(F32).T.astype(BF)
            dt = dof.T.astype(BF)

            def weights(item):
                qb, h = item
                return dot_nt(da[h][qb * tile : (qb + 1) * tile], va[h][keys(qb)])

            ahead = weights(items[0])
            for i, item in enumerate(items):
                dp = ahead
                if i + 1 < len(items):
                    ahead = weights(items[i + 1])
                qb, h = item
                qs = slice(qb * tile, (qb + 1) * tile)
                loads[a, qb, h].wait()
                ds[a, h, qs, 0:n_keys] = e[a, h, qs, 0:n_keys] * dp.astype(BF)
            for ks in [slice(b * tile, (b + 1) * tile) for b in range(ROWS // tile)] if short else [slice(0, ROWS)]:
                dq = dot(ds[a, 0, ks, 0:n_keys], km[0][ks]) + dot(ds[a, 1, ks, 0:n_keys], km[1][ks])
                g[a, ks, :PAIR] = (dq * SCALE).astype(BF)
                hs = [slice(h * HD, (h + 1) * HD) for h in range(2)]
                vt = [dot(dt[hs[h], ks], e[a, h, ks, 0:n_keys]) for h in range(2)]
                kt = [dot(qt[hs[h], ks], ds[a, h, ks, 0:n_keys]) for h in range(2)]
                g[a, ks, 2 * PAIR :] = jnp.concatenate(vt, 0).T.astype(BF)
                g[a, ks, PAIR : 2 * PAIR] = jnp.concatenate(kt, 0).T.astype(BF)
            stores.append(pltpu.make_async_copy(g.at[a], g_.at[a], gsems.at[a]))
            stores[-1].start()
            if a == 0:
                loads["x"].wait()
            gr = dot_tn(x[...], g[a])
            for c in range(3):
                gsum[a, c * D : (c + 1) * D, :] = gr[:, c * PAIR : (c + 1) * PAIR].astype(BF)
        for c in stores:
            c.wait()

    pl.when(code[1] == 1)(lambda: run(False))
    pl.when(code[1] == 0)(lambda: run(True))
    for a in range(n):
        for j in range(8):

            def put(out, low, j=j, a=a):
                at = (((j % 4) ^ low) * n + a) * PART
                out[pl.ds(pl.multiple_of(at, PART), PART), :] = gsum[a, j * PART : (j + 1) * PART, :]

            pl.when(code[0] == j // 4)(lambda: put(keep, code[5]))
            pl.when(code[0] != j // 4)(lambda: put(send, code[6]))
    bgs = [jnp.concatenate([colsum(g[a, :, :PAIR].astype(F32)), colsum(g[a, :, 2 * PAIR :].astype(F32))], 0) for a in range(n)]
    if not last:
        bg_out[...] = jnp.concatenate(bgs + [jnp.zeros((4, PAIR), F32)], 0)
        return
    for i in range(6):
        for c in range(4):
            vrow[i * 4 + c : i * 4 + c + 1, :] = vec[i : i + 1, c * PAIR : (c + 1) * PAIR]
    for c in range(16):
        vrow[24 + c : 25 + c, :] = vup[0:1, c * PAIR : (c + 1) * PAIR]
    known = [bg_in[0:2], bg_in[2:4]] + bgs
    for p in range(4):
        vrow[40 + 2 * p : 42 + 2 * p, :] = sum(jnp.where((code[4] ^ s) == p, b, 0.0) for s, b in enumerate(known))
    vrow[48:, :] = jnp.zeros((VROWS - 48, PAIR), F32)
    v_out[...] = vrow[...].astype(BF)
    send[8 * PART :, :] = v_out[...]


def attention_backward(code, x, hg, slots, at_o, es, qkvs, os, rls, small=None):
    S, n, last = jax.ShapeDtypeStruct, len(slots), small is not None
    ins = [code, x, hg, *es, *qkvs, *os, *rls] + list(small or ())
    rows = 4 * n * PART
    outs = [S((n, ROWS, 3 * PAIR), BF), S((rows, PAIR), BF), S((rows + VROWS * last, PAIR), BF), S((VROWS, PAIR), BF) if last else S((8, PAIR), F32)]
    scratch = [((ROWS, D), BF), ((n, 2, ROWS, ROWS), BF), ((n, ROWS, 3 * PAIR), BF), ((n, ROWS, PAIR), BF), ((n, ROWS, PAIR), BF),
               ((n, ROWS, PAIR), F32), ((n, 2, ROWS, ROWS), BF), ((n, ROWS, 3 * PAIR), BF), ((n, 3 * D, PAIR), BF), ((VROWS, PAIR), F32)]
    return pl.pallas_call(
        lambda *refs: bwd_kernel(slots, at_o, last, *refs),
        in_specs=[SMEM] + [ANY] * (2 + 4 * n) + [VM] * (3 * last),
        out_specs=[ANY, VM, VM, VM],
        out_shape=outs,
        scratch_shapes=[pltpu.VMEM(*a) for a in scratch] + [pltpu.SemaphoreType.DMA((12 * n + 1,)), pltpu.SemaphoreType.DMA((n,))],
        compiler_params=params(0),
        cost_estimate=cost(n * 8e9, n * 8 << 20),
    )(*ins)


def gelu_parts(u):
    cdf = 0.5 + 0.5 * lax.erf(u * math.sqrt(0.5))
    density = jnp.exp2(u * u * (-0.5 * math.log2(math.e))) * (1.0 / math.sqrt(2.0 * math.pi))
    return u * cdf, cdf + u * density


def norm_parts(h):
    m = jnp.mean(h, -1, keepdims=True)
    c = h - m
    r = lax.rsqrt(jnp.mean(c * c, -1, keepdims=True) + 1e-5)
    return c * r, r


def norm_back(e, gain, z, r):
    eg = e * gain
    return r * (eg - jnp.mean(eg, -1, keepdims=True) - z * jnp.mean(eg * z, -1, keepdims=True))


def colsum(a):
    return jnp.sum(a, 0, keepdims=True)


BLOCKS, BLOCK = 16, 144


def place(block, size, base, first, half, code, out):
    low = code[2 + half]
    for s in range(block.shape[0] // size):
        out[(first + s) ^ low, base : base + size, :] = block[s * size : (s + 1) * size].astype(BF)


def ffn_kernel(code, x_, acc_, oa_, ob_, oc_, wo, bo, g1, s1, wu_, bu, wd_, bd, g2, s2, sc_, ac_,
               ns_, na_, fg_, hg_, keep0, keep1, send0, send1, vec, vup,
               x, acc, oa, ob, oc, sc, ac, wu, wd, ns, na, fg, hg, keep, send, wp, hid, bfull, lfull, pfull, ofull, afull, isem, osem):
    tiles = [slice(t * QB, (t + 1) * QB) for t in range(ROWS // QB)]
    loads, stores = {}, []

    def load(name, src, dst, t=None):
        at = pl.ds(t * QB, QB) if t is not None else pl.ds(0, src.shape[0])
        loads[name, t] = pltpu.make_async_copy(src.at[at], dst.at[at], isem.at[len(loads)])
        loads[name, t].start()

    def store(src, dst, *at):
        stores.append(pltpu.make_async_copy(src.at[at], dst.at[at], osem.at[len(stores)]))
        stores[-1].start()

    by_tile = (("oa", oa_, oa), ("ob", ob_, ob), ("oc", oc_, oc), ("x", x_, x), ("acc", acc_, acc), ("sc", sc_, sc), ("ac", ac_, ac))
    for t in (0, 1):
        for name, src, dst in by_tile[:4]:
            load(name, src, dst, t)
    load("wu", wu_, wu)
    load("wd", wd_, wd)
    for name, src, dst in by_tile[4:]:
        for t in (0, 1):
            load(name, src, dst, t)
    for t in (2, 3):
        for name, src, dst in by_tile:
            load(name, src, dst, t)

    for s in range(D // PAIR):
        at = pl.multiple_of((code[4] ^ s) * PAIR, PAIR)
        wp[s * PAIR : (s + 1) * PAIR, :] = wo[pl.ds(at, PAIR), :]

    def wait(t, *names):
        for name in names:
            loads[name, t].wait()

    sums, up_sum = [0.0] * 6, 0.0
    for group in ((0, 1), (2, 3)):
        att, z1, r1, first, hidden, slope, si, bgs, pgs, ags = {}, {}, {}, {}, {}, {}, {}, {}, {}, {}
        for t in group:
            wait(t, "oa", "ob", "oc")
            ofull[tiles[t], :] = jnp.concatenate([oa[tiles[t]], ob[tiles[t]], oc[tiles[t]]], axis=1)
            att[t] = dot(ofull[tiles[t], :], wp[...]) + bo[...]
        for t in group:
            wait(t, "x")
            z1[t], r1[t] = norm_parts(x[tiles[t]].astype(F32) + att[t])
            first[t] = z1[t] * g1[...] + s1[...]
            lfull[tiles[t], :] = first[t].astype(BF)
        if group[0] == 0:
            wait(None, "wu")
        ups = {t: dot(first[t].astype(BF), wu[...]) for t in group}
        for t in group:
            a, slope[t] = gelu_parts(ups[t] + bu[...])
            hidden[t] = a.astype(BF)
            hid[tiles[t], :] = hidden[t]
        if group[0] == 0:
            wait(None, "wd")
        branch = {t: dot(hidden[t], wd[...]) + bd[...] for t in group}
        for t in group:
            wait(t, "acc", "sc", "ac")
            na[tiles[t]] = acc[tiles[t]] + att[t] + branch[t]
            store(na, na_, pl.ds(t * QB, QB))
            z2, r2 = norm_parts(first[t] + branch[t])
            ns[tiles[t]] = (z2 * g2[...] + s2[...]).astype(BF)
            store(ns, ns_, pl.ds(t * QB, QB))
            e2 = sc[tiles[t]]
            si[t] = norm_back(e2, g2[...], z2, r2)
            bgs[t] = (si[t] + ac[tiles[t]]).astype(BF)
            bfull[tiles[t], :] = bgs[t]
            sums[3:] = [a + colsum(b) for a, b in zip(sums[3:], (bgs[t].astype(F32), e2 * z2, e2))]
        hgs = {t: dot_nt(bgs[t], wd[...]) for t in group}
        for t in group:
            pgs[t] = (hgs[t] * slope[t]).astype(BF)
            pfull[tiles[t], :] = pgs[t]
            up_sum += colsum(pgs[t].astype(F32))
        es = {t: dot_nt(pgs[t], wu[...]) for t in group}
        for t in group:
            e1 = es[t] + si[t]
            fi = norm_back(e1, g1[...], z1[t], r1[t])
            fg[tiles[t]] = fi
            store(fg, fg_, pl.ds(t * QB, QB))
            ags[t] = (fi + ac[tiles[t]]).astype(BF)
            afull[tiles[t], :] = ags[t]
            sums[:3] = [a + colsum(b) for a, b in zip(sums[:3], (ags[t].astype(F32), e1 * z1[t], e1))]
        for t in group:
            hg[tiles[t]] = dot_nt(ags[t], wp[...]).astype(BF)
            store(hg, hg_, pl.ds(t * QB, QB))
    for j, s in enumerate(sums):
        vec[j : j + 1, :] = s
    vec[6:8, :] = jnp.zeros((2, D), F32)
    vup[0:1, :] = up_sum
    quarter = BLOCKS // 2
    for half, out, dsts in ((1, send, (send0, send1)), (0, keep, (keep0, keep1))):

        def ship(base, size):
            for k in (1, 0):
                src = out.at[pl.ds(k * quarter, quarter), pl.ds(base, size)]
                stores.append(pltpu.make_async_copy(src, dsts[k].at[:, pl.ds(base, size)], osem.at[len(stores)]))
                stores[-1].start()

        mine = code[0] ^ half
        for b in range(4):
            at = pl.multiple_of(mine * 1024 + b * 256, 256)
            place(dot_tn(hid[:, pl.ds(at, 256)], bfull[...]), 64, 0, b * 4, half, code, out)
        ship(0, 64)
        for c in range(2):
            at = pl.multiple_of(mine * 1024 + c * 512, 512)
            place(dot_tn(lfull[...], pfull[:, pl.ds(at, 512)]), 64, 64, c * 8, half, code, out)
        ship(64, 64)
        for p in range(2):
            at = pl.multiple_of(((mine * 2 + p) ^ code[4]) * PAIR, PAIR)
            place(dot_tn(ofull[:, pl.ds(at, PAIR)], afull[...]), 16, 128, p * 8, half, code, out)
        ship(128, 16)
    for c in stores:
        c.wait()


def ffn(code, x, acc, os, wo, bo, g1, s1, wu, bu, wd, bd, g2, s2, sc, ac):
    S = jax.ShapeDtypeStruct
    bo, g1, s1, bu, bd, g2, s2 = (v.reshape(1, -1) for v in (bo, g1, s1, bu, bd, g2, s2))
    ins = (code, x, acc, *os, wo, bo, g1, s1, wu, bu, wd, bd, g2, s2, sc, ac)
    specs = [SMEM] + [ANY] * 5 + [VM] * 4 + [ANY, VM, ANY] + [VM] * 3 + [ANY] * 2
    outs = [S((ROWS, D), BF), S((ROWS, D), F32), S((ROWS, D), F32), S((ROWS, D), BF)]
    outs += [S((BLOCKS // 2, BLOCK, D), BF)] * 4 + [S((8, D), F32), S((1, FF), F32)]
    buffers = [x, acc, *os, sc, ac, wu, wd] + outs[:4] + [S((BLOCKS, BLOCK, D), BF)] * 2
    scratch = [pltpu.VMEM(a.shape, a.dtype) for a in buffers]
    scratch += [pltpu.VMEM(s, BF) for s in ((D, D), (ROWS, FF), (ROWS, D), (ROWS, D), (ROWS, FF), (ROWS, D), (ROWS, D))]
    return pl.pallas_call(
        ffn_kernel,
        in_specs=specs,
        out_specs=[ANY] * 8 + [VM] * 2,
        out_shape=outs,
        scratch_shapes=scratch + [pltpu.SemaphoreType.DMA((30,)), pltpu.SemaphoreType.DMA((28,))],
        compiler_params=params(0),
        cost_estimate=cost(25e9, 20 << 20),
    )(*ins)


def back_stream_kernel(code, fg, ga, gb, *refs):
    was, wbs, out = refs[:4], refs[4:8], refs[8]
    ca = pl.multiple_of(code[0] * HALF, HALF)
    cb = pl.multiple_of(HALF - code[0] * HALF, HALF)
    for at, ws in ((ca, was), (cb, wbs)):
        t = fg[:, pl.ds(at, HALF)]
        for s, w in enumerate(ws):
            t = t + dot_nt((ga if s < 2 else gb)[s % 2], side(w))
        out[:, pl.ds(at, HALF)] = t


def back_stream(code, fg, ga, gb, was, wbs):
    return pl.pallas_call(
        back_stream_kernel,
        grid=(ROWS // QB,),
        in_specs=[SMEM, pl.BlockSpec((QB, D), lambda i: (i, 0))] + [pl.BlockSpec((2, QB, 3 * PAIR), lambda i: (0, i, 0))] * 2 + [whole((PACK, PAIR))] * 8,
        out_specs=pl.BlockSpec((QB, D), lambda i: (i, 0)),
        out_shape=jax.ShapeDtypeStruct((ROWS, D), F32),
        compiler_params=params(1, 16),
        cost_estimate=cost(4e9, 8 << 20),
    )(code, fg, ga, gb, *was, *wbs)


def general_gather(inward, inward_bias):
    full = lax.all_gather(inward, "head", axis=2, tiled=True)
    bias = lax.all_gather(inward_bias, "head", axis=1, tiled=True)
    was, wbs = [], []
    for p in range(D // PAIR):
        cols = slice(p * PAIR, (p + 1) * PAIR)
        tail = jnp.pad(bias[:, cols], ((0, 14), (0, 0)))
        was.append(jnp.concatenate([full[:, :HALF, cols].reshape(3 * HALF, PAIR), tail], 0))
        wbs.append(jnp.concatenate([full[:, HALF:, cols].reshape(3 * HALF, PAIR), tail], 0))
    return was, wbs


def general_sums(blocks, pair_parts, vectors):
    both = ("batch", "head")
    whole_half, vectors = lax.psum((blocks, vectors), both)
    wide = whole_half.astype(F32)
    dwd = wide[:, :64].reshape(FF, D)
    dwu = wide[:, 64:128].reshape(4, D, D).transpose(1, 0, 2).reshape(D, FF)
    dwo = wide[:, 128:].reshape(D, D)
    wg = []
    for k, n in pair_parts:
        t = jnp.concatenate([k[: 8 * PART].reshape(4, 2, PART, PAIR), n[: 8 * PART].reshape(4, 2, PART, PAIR)], 0)
        wg += [t[:, a].reshape(3, D, PAIR) for a in range(2)]
    wg = lax.psum(lax.psum_scatter(jnp.concatenate(wg, 2), "head", scatter_dimension=2, tiled=True), "batch")
    rows = vectors[:48].astype(F32).reshape(-1)
    bias = rows[5120:].reshape(D // PAIR, 2, PAIR).transpose(1, 0, 2).reshape(2, D)
    width = D // lax.axis_size("head")
    bias = lax.dynamic_slice_in_dim(bias, lax.axis_index("head") * width, width, 1)
    return wg.astype(F32), bias, dwo, dwu, dwd, rows


def swap(x, masks):
    n_batch, n_head = lax.axis_size("batch"), lax.axis_size("head")
    pairs = []
    for b in range(n_batch):
        for h in range(n_head):
            axis, mask = masks[b & 1]
            to = (b ^ mask, h) if axis == "batch" else (b, h ^ mask)
            pairs.append((b * n_head + h, to[0] * n_head + to[1]))
    return lax.ppermute(x, ("batch", "head"), pairs)


CORE = (("batch", 1), ("batch", 1))
X, Y, NEAR, FAR = ("batch", 2), ("batch", 4), ("head", 1), ("head", 2)
STEPS = ((X, NEAR), (NEAR, X), (Y, FAR), (FAR, Y))
PAIR_STEPS = ((X, Y), (Y, X), (FAR, FAR), (NEAR, NEAR))


def place_code(steps, core, index):
    code = 0
    for masks in steps:
        bits = []
        for axis, mask in masks:
            bits.append(((index[axis] & mask) > 0).astype(jnp.int32))
        code = code * 2 + jnp.where(core == 0, bits[0], bits[1])
    return code


def add(a, b):
    return (a.astype(F32) + b.astype(F32)).astype(BF)


def after(x, *others):
    return lax.optimization_barrier((x, *others))[0]


def combine_kernel(n_keep, *refs):
    keeps, gots, v = refs[:n_keep], refs[n_keep : 2 * n_keep], refs[2 * n_keep]
    keep, send, v_out = refs[2 * n_keep + 1 :]
    half = keep.shape[0]
    step = half // (2 * n_keep) if n_keep > 1 else half
    for b in range(4 if n_keep > 1 else 2):
        out, base = (keep, 0) if b < (2 if n_keep > 1 else 1) else (send, half)
        for a, (k, r) in enumerate(zip(keeps, gots)):
            at = b * step
            to = (b * n_keep + a) * step - base
            out[to : to + step, :] = add(k[at : at + step, :], r[at : at + step, :])
    total = add(v[...], gots[-1][-VROWS:, :])
    v_out[...] = total
    if send.shape[0] > half:
        send[half:, :] = total


def combine(keeps, gots, v):
    S, n = jax.ShapeDtypeStruct, len(keeps)
    half = sum(k.shape[0] for k in keeps) // 2
    return pl.pallas_call(
        lambda *refs: combine_kernel(n, *refs),
        in_specs=[VM] * (2 * n + 1),
        out_specs=[VM] * 3,
        out_shape=[S((half, PAIR), BF), S((half + VROWS, PAIR), BF), S((VROWS, PAIR), BF)],
        compiler_params=pltpu.CompilerParams(vmem_limit_bytes=16 << 20),
        cost_estimate=cost(1e6, 2 << 20),
    )(*keeps, *gots, v)


def widen_kernel(code, src, *refs):
    dwd, dwu, dwo = refs[-3:]
    for s in range(4):
        at = (pl.program_id(0) * 4 + s) ^ (code[1] & 7)
        dwd[s * 64 : (s + 1) * 64, :] = src[at, 0:64].astype(F32)
        dwu[s * 64 : (s + 1) * 64, :] = src[at, 64:128].astype(F32)
        dwo[s * 16 : (s + 1) * 16, :] = src[at, 128:144].astype(F32)


def widen(quarter, low, src, before=()):
    S = jax.ShapeDtypeStruct
    spec = pltpu.PrefetchScalarGridSpec(
        num_scalar_prefetch=1,
        grid=(2,),
        in_specs=[pl.BlockSpec((BLOCKS // 2, BLOCK, D), lambda i, c: (0, 0, 0))] + [ANY] * len(before),
        out_specs=[
            pl.BlockSpec((256, D), lambda i, c: (c[0] * 2 + i, 0)),
            pl.BlockSpec((256, D), lambda i, c: (i, c[0])),
            pl.BlockSpec((64, D), lambda i, c: (c[0] * 2 + i, 0)),
        ],
    )
    return pl.pallas_call(
        widen_kernel,
        grid_spec=spec,
        out_shape=[S((FF, D), F32), S((D, FF), F32), S((D, D), F32)],
        input_output_aliases={2 + k: k for k in range(len(before))},
        compiler_params=params(1, 16),
        cost_estimate=cost(1e6, 4 << 20),
    )(jnp.stack([quarter, low]), src, *before)


def finish_kernel(code, own, other, v, wg, bg, *outs):
    for j in range(8):
        for half, src, low in ((code[0], own, code[5]), (1 - code[0], other, code[6])):

            @pl.when(half == j // 4)
            def _():
                block = src[pl.ds(pl.multiple_of(((j % 4) ^ low) * PART, PART), PART), :].astype(F32)
                for r in range(0, PART, 64):
                    at = j * PART + r
                    wg[at // D, at % D : at % D + 64] = block[r : r + 64]

    rows = v[...].astype(F32)
    for i in range(6):
        for c in range(4):
            outs[i][0:1, c * PAIR : (c + 1) * PAIR] = rows[i * 4 + c : i * 4 + c + 1]
    for c in range(16):
        outs[6][0:1, c * PAIR : (c + 1) * PAIR] = rows[24 + c : 25 + c]
    for p in range(4):

        @pl.when(code[4] == p)
        def _():
            bg[...] = rows[40 + 2 * p : 42 + 2 * p]


def finish(code, own, other, v):
    S = jax.ShapeDtypeStruct
    return pl.pallas_call(
        finish_kernel,
        in_specs=[SMEM, VM, VM, VM],
        out_specs=[VM] * 9,
        out_shape=[S((3, D, PAIR), F32), S((2, PAIR), F32)] + [S((1, D), F32)] * 6 + [S((1, FF), F32)],
        compiler_params=pltpu.CompilerParams(vmem_limit_bytes=16 << 20),
        cost_estimate=cost(1e6, 3 << 20),
    )(code, own, other, v)


def body(stream, accumulator, inward, inward_bias, outward, outward_bias, first_gain, first_shift, up_weight, up_bias,
         down_weight, down_bias, second_gain, second_shift, long_count, stream_cotangent, accumulator_cotangent):
    assert stream.shape == (ROWS, D)
    b, h = lax.axis_index("batch"), lax.axis_index("head")
    tuned = (lax.axis_size("batch"), lax.axis_size("head")) == (8, 4)
    flag = (h < long_count[0]).astype(jnp.int32)
    zero = jnp.zeros((), jnp.int32)
    if tuned:
        core, index = b & 1, {"batch": b, "head": h}
        low, other = (place_code(STEPS, c, index) for c in (core, 1 - core))
        pair_low, pair_other = (place_code(PAIR_STEPS[:2], c, index) for c in (core, 1 - core))
        code = jnp.stack([core, flag, low, other, h, pair_low, pair_other, zero])
        rows = inward.reshape(3, 2, HALF, PAIR)
        bias = jnp.pad(inward_bias, ((0, 14), (0, 0)))
        wa = jnp.concatenate([lax.dynamic_index_in_dim(rows, core, 1, False).reshape(3 * HALF, PAIR), bias], 0)
        wb = jnp.concatenate([lax.dynamic_index_in_dim(rows, 1 - core, 1, False).reshape(3 * HALF, PAIR), bias], 0)
        was = [wa] + [swap(wa, (("head", s),) * 2) for s in (1, 2, 3)]
        wbs = [wb]
    else:
        code = jnp.stack([zero, flag] + [zero] * 6)
        was, wbs = general_gather(inward, inward_bias)

    cuts = ((0, 1), (1, 2), (2, 4))
    heads = []
    for i, j in cuts:
        if tuned and i > 0:
            was[i:j] = [after(w, heads[-1][1]) for w in was[i:j]]
            wbs += [swap(w, CORE) for w in was[i:j]]
        heads.append(attention_forward(code, stream, was[i:j], wbs[i:j]))
    ns, na, fg, hg, *halves, vec, vup = ffn(
        code, stream, accumulator, [t[1] for t in heads], outward, outward_bias, first_gain, first_shift, up_weight, up_bias,
        down_weight, down_bias, second_gain, second_shift, stream_cotangent, accumulator_cotangent)

    def backward(slots, x, small=None):
        t = [heads[min(s, 2)] for s in slots]
        at = [max(s - 2, 0) for s in slots]
        return attention_backward(code, x, hg, slots, at, [a[0] for a in t], [a[2] for a in t], [a[1] for a in t], [a[3] for a in t], small)

    if not tuned:
        ga, ka, na_, bg = backward((0, 1), stream)
        gb, kb, nb_, v = backward((2, 3), stream, (vec, vup, bg))
        wg, bias, dwo, dwu, dwd, rows = general_sums(jnp.concatenate(halves, 0), ((ka, na_), (kb, nb_)), v)
        sg = back_stream(code, fg, ga, gb, was, wbs)
        vecs, vup = [rows[i * D : (i + 1) * D] for i in range(6)], rows[6 * D : 6 * D + FF]
    else:
        keep0, keep1, send0, send1 = halves
        out = add(keep1, swap(send1, CORE))
        got0 = swap(send0, CORE)
        got = swap(out, STEPS[0])
        cur = add(keep0, got0)
        ga, ka, sa, bg = backward((0, 1), after(stream, out, cur))
        ra = swap(sa, CORE)
        cur = add(after(cur, ka), got)
        out = cur[4:]
        got = swap(out, STEPS[1])
        gb, kb, sb, v = backward((2, 3), after(stream, out), (vec, vup, bg))
        rb = swap(sb, CORE)
        cur = add(after(cur[:4], kb), got)
        out = cur[2:]
        got = swap(out, STEPS[2])
        k, s, v = combine([ka, kb], [ra, rb], after(v, out))
        got2 = swap(s, PAIR_STEPS[0])
        cur = add(after(cur[:2], k), got)
        out = cur[1:]
        got = swap(out, STEPS[3])
        sg = back_stream(code, after(fg, s, out), ga, gb, was, wbs)
        cur = add(after(cur[:1], sg), got)
        got = swap(cur, STEPS[3])
        k, s, v = combine([k], [got2], after(v, cur))
        got2 = swap(s, PAIR_STEPS[1])
        cur = jnp.concatenate([after(cur, k), got], 0)
        got = swap(cur, STEPS[2])
        k, s, v = combine([k], [got2], after(v, cur))
        got2 = swap(s, PAIR_STEPS[2])
        cur = jnp.concatenate([after(cur, k), got], 0)
        got = swap(cur, STEPS[1])
        k, s, v = combine([k], [got2], after(v, cur))
        got2 = swap(s, PAIR_STEPS[3])
        v = add(v, got2[PART:])
        k = add(k, got2[:PART])
        got2 = swap(k, PAIR_STEPS[1])
        cur = jnp.concatenate([after(cur, k), got], 0)
        got = swap(cur, STEPS[0])
        other_cur = swap(cur, CORE)
        k = jnp.concatenate([after(k, cur), got2], 0)
        got2 = swap(k, PAIR_STEPS[0])
        mine, theirs = core * 2 + (low >> 3), (1 - core) * 2 + (other >> 3)
        wide = widen(mine, low, cur)
        k = jnp.concatenate([k, got2], 0)
        got2 = swap(k, CORE)
        wide = widen(theirs, other, other_cur, wide)
        wg, bias, *vecs, vup = finish(code, k, got2, v)
        vecs, vup = [t[0] for t in vecs], vup[0]
        got = after(got, bias, wide[0])
        other_got = swap(got, CORE)
        wide = widen(mine ^ 1, low, got, wide)
        dwd, dwu, dwo = widen(theirs ^ 1, other, other_got, wide)
    return (ns, na, sg, wg, bias, dwo, vecs[0], vecs[1], vecs[2], dwu, vup, dwd, vecs[3], vecs[4], vecs[5])


def solution(mesh):
    tokens = P(("batch", "head"), None)
    in_specs = (tokens, tokens, P(None, None, "head"), P(None, "head")) + (P(),) * 10 + (P("batch"), tokens, tokens)
    out_specs = (tokens,) * 3 + (P(None, None, "head"), P(None, "head")) + (P(),) * 10
    return jax.shard_map(body, mesh=mesh, in_specs=in_specs, out_specs=out_specs, check_vma=False)
```

```python
import math

import jax
import jax.numpy as jnp
from jax import lax
from jax.experimental import pallas as pl
from jax.experimental.pallas import tpu as pltpu
from jax.sharding import PartitionSpec as P

F32, BF = jnp.float32, jnp.bfloat16
ROWS, D, FF, PAIR, HD, SHORT = 1024, 512, 2048, 128, 64, 256
QB = 256
SCALE = 1.0 / math.sqrt(HD)


def dot(a, b):
    return lax.dot_general(a, b, (((1,), (0,)), ((), ())), preferred_element_type=F32)


def dot_nt(a, b):
    return lax.dot_general(a, b, (((1,), (1,)), ((), ())), preferred_element_type=F32)


def dot_tn(a, b):
    return lax.dot_general(a, b, (((0,), (0,)), ((), ())), preferred_element_type=F32)


def params(n=1, mib=60):
    return pltpu.CompilerParams(dimension_semantics=("arbitrary",) * n or None, vmem_limit_bytes=mib << 20)


def cost(flops, nbytes):
    return pl.CostEstimate(flops=int(flops), bytes_accessed=int(nbytes), transcendentals=0)


SMEM = pl.BlockSpec(memory_space=pltpu.SMEM)
VM = pl.BlockSpec(memory_space=pltpu.VMEM)
HBM = pl.BlockSpec(memory_space=pltpu.HBM)


def whole(shape):
    return pl.BlockSpec(shape, lambda *_: (0,) * len(shape))


HALF = D // 2
PACK = 3 * HALF + 16


def side(w):
    return jnp.concatenate([w[c * HALF : (c + 1) * HALF] for c in range(3)], axis=1)


def fwd_kernel(n_pairs, code, x, *refs):
    was, wbs = refs[:n_pairs], refs[n_pairs : 2 * n_pairs]
    e, o, qkv, rl, es, qs_, va, sems, qsems = refs[2 * n_pairs :]
    ca = pl.multiple_of(code[0] * HALF, HALF)
    cb = pl.multiple_of(HALF - code[0] * HALF, HALF)
    lane = lax.broadcasted_iota(jnp.int32, (1, PAIR), 1)

    def run(short):
        copies = []

        def project(a):
            wa, wb = was[a], wbs[a]
            p = dot(x[:, pl.ds(ca, HALF)], side(wa)) + dot(x[:, pl.ds(cb, HALF)], side(wb))
            bq, bv = wa[3 * HALF : 3 * HALF + 1].astype(F32), wa[3 * HALF + 1 : 3 * HALF + 2].astype(F32)
            q = ((p[:, :PAIR] + bq).astype(BF).astype(F32) * SCALE).astype(BF)
            k = p[:, PAIR : 2 * PAIR].astype(BF)
            v = (p[:, 2 * PAIR :] + bv).astype(BF)
            qs_[a, :, :PAIR] = q
            qs_[a, :, PAIR : 2 * PAIR] = k
            qs_[a, :, 2 * PAIR :] = v
            copies.append(pltpu.make_async_copy(qs_.at[a], qkv.at[a], qsems.at[a]))
            copies[-1].start()
            return q, k, [jnp.where((lane < HD) == (h == 0), v, jnp.ones((), BF)) for h in range(2)]

        if short:
            for a in range(n_pairs):
                for h, v in enumerate(project(a)[2]):
                    va[a, h] = v

            def block(i, carry):
                a, t = i // (ROWS // SHORT), i % (ROWS // SHORT)
                rows = pl.ds(pl.multiple_of(t * SHORT, SHORT), SHORT)
                q, k = qs_[a, rows, :PAIR], qs_[a, rows, PAIR : 2 * PAIR]
                outs = []
                for h in range(2):
                    sc = dot_nt(jnp.where((lane < HD) == (h == 0), q, jnp.zeros((), BF)), k)
                    ex = jnp.exp(sc - jnp.max(sc, axis=1, keepdims=True)).astype(BF)
                    es[a, h, rows, 0:SHORT] = ex
                    u = dot(ex, va[a, h, rows, :])
                    r = 1.0 / pltpu.roll(u, HD, 1)
                    outs.append((u * r, r))
                o[a, rows, :] = jnp.where(lane < HD, outs[0][0], outs[1][0]).astype(BF)
                rl[a, rows, :] = jnp.where(lane < HD, outs[0][1], outs[1][1])
                return carry

            lax.fori_loop(0, n_pairs * (ROWS // SHORT), block, 0)
            at = (slice(None), slice(None), slice(None), pl.ds(0, SHORT))
            copies.append(pltpu.make_async_copy(es.at[at], e.at[at], sems.at[0]))
            copies[-1].start()
            for c in copies:
                c.wait()
            return

        ready = {0: project(0)}

        def score(item):
            a, qb, h = item
            q, k, _ = ready[a]
            qh = jnp.where((lane < HD) == (h == 0), q[qb * QB : (qb + 1) * QB], jnp.zeros((), BF))
            return dot_nt(qh, k)

        done = {}

        def product(item, ex):
            a, qb, h = item
            qs = slice(qb * QB, (qb + 1) * QB)
            u = dot(ex, ready[a][2][h])
            r = 1.0 / pltpu.roll(u, HD, 1)
            done[h] = (u * r, r)
            if h == 1:
                o[a, qs, :] = jnp.where(lane < HD, done[0][0], done[1][0]).astype(BF)
                rl[a, qs, :] = jnp.where(lane < HD, done[0][1], done[1][1])

        items = [(a, qb, h) for a in range(n_pairs) for qb in range(ROWS // QB) for h in range(2)]
        ahead, last = score(items[0]), None
        for i, item in enumerate(items):
            s = ahead
            if i + 1 < len(items):
                if items[i + 1][0] not in ready:
                    ready[items[i + 1][0]] = project(items[i + 1][0])
                ahead = score(items[i + 1])
            ex = jnp.exp(s - jnp.max(s, axis=1, keepdims=True)).astype(BF)
            a, qb, h = item
            at = (a, h, pl.ds(qb * QB, QB))
            es[at] = ex
            copies.append(pltpu.make_async_copy(es.at[at], e.at[at], sems.at[i]))
            copies[-1].start()
            if last is not None:
                product(*last)
            last = (item, ex)
        product(*last)
        for c in copies:
            c.wait()

    pl.when(code[1] == 1)(lambda: run(False))
    pl.when(code[1] == 0)(lambda: run(True))


def attention_forward(code, x, was, wbs):
    S, n = jax.ShapeDtypeStruct, len(was)
    return pl.pallas_call(
        lambda *refs: fwd_kernel(n, *refs),
        in_specs=[SMEM, VM] + [VM] * (2 * n),
        out_specs=[HBM, VM, HBM, VM],
        out_shape=[S((n, 2, ROWS, ROWS), BF), S((n, ROWS, PAIR), BF), S((n, ROWS, 3 * PAIR), BF), S((n, ROWS, PAIR), F32)],
        scratch_shapes=[pltpu.VMEM((n, 2, ROWS, ROWS), BF), pltpu.VMEM((n, ROWS, 3 * PAIR), BF), pltpu.VMEM((n, 2, ROWS, PAIR), BF),
                        pltpu.SemaphoreType.DMA((8 * n,)), pltpu.SemaphoreType.DMA((n,))],
        compiler_params=params(0),
        cost_estimate=cost(1e6, 1 << 10),
    )(code, x, *was, *wbs)


PART, VROWS = 192, 64


def bwd_kernel(slots, at_o, last, code, x_, hg_, *refs):
    n = len(slots)
    es_, qkvs_, os_, rls_ = (refs[k * n : (k + 1) * n] for k in range(4))
    refs = refs[4 * n :]
    if last:
        (vec, vup, bg_in), refs = refs[:3], refs[3:]
        g_, keep, send, v_out, x, e, qkv, o, do, rl, ds, g, gsum, vrow, sva, sda, skm, sqt, sdt, sems, gsems = refs
    else:
        g_, keep, send, bg_out, x, e, qkv, o, do, rl, ds, g, gsum, vrow, sva, sda, skm, sqt, sdt, sems, gsems = refs
    lane = lax.broadcasted_iota(jnp.int32, (1, PAIR), 1)
    first, zero, one = lane < HD, jnp.zeros((), BF), jnp.ones((), BF)
    row = lax.broadcasted_iota(jnp.int32, (PAIR, PAIR), 0)
    col = lax.broadcasted_iota(jnp.int32, (PAIR, PAIR), 1)
    pick = jnp.where(((row < HD) != (col < HD)) & ((col & (HD - 1)) < 2), 1.0, 0.0).astype(BF)
    hs = [slice(h * HD, (h + 1) * HD) for h in range(2)]
    tile = 512
    items = [(t, h) for t in range(ROWS // tile) for h in range(2)]

    def small_loads(a):
        pairs = ((hg_.at[:, pl.ds(slots[a] * PAIR, PAIR)], do), (rls_[a].at[at_o[a]], rl), (os_[a].at[at_o[a]], o), (qkvs_[a].at[at_o[a]], qkv))
        return [pltpu.make_async_copy(src, dst.at[a], sems.at[8 * a + k]) for k, (src, dst) in enumerate(pairs)]

    def e_load(a, i):
        t, h = items[i]
        at = (h, pl.ds(t * tile, tile))
        return pltpu.make_async_copy(es_[a].at[(at_o[a], *at)], e.at[(a, *at)], sems.at[8 * a + 4 + i])

    def e_load_short(a):
        at = (slice(None), slice(None), pl.ds(0, SHORT))
        return pltpu.make_async_copy(es_[a].at[(at_o[a], *at)], e.at[(a, *at)], sems.at[8 * a + 4])

    def store_g(a):
        return pltpu.make_async_copy(g.at[a], g_.at[a], gsems.at[a])

    x_load = pltpu.make_async_copy(x_, x, sems.at[8 * n])

    def prepare(a):
        dof = do[a].astype(F32) * rl[a]
        dob = dof.astype(BF)
        t = dof * o[a].astype(F32)
        th = t.astype(BF)
        tl = (t - th.astype(F32)).astype(BF)
        delta = -(dot(th, pick) + dot(tl, pick))
        dh = delta.astype(BF)
        dd = jnp.where((lane & (HD - 1)) == 0, dh, (delta - dh.astype(F32)).astype(BF))
        q, k, v = qkv[a, :, :PAIR], qkv[a, :, PAIR : 2 * PAIR], qkv[a, :, 2 * PAIR :]
        own = [first == (h == 0) for h in range(2)]
        aug = [jnp.logical_not(own[h]) & ((lane & (HD - 1)) < 2) for h in range(2)]
        va = [jnp.where(own[h], v, jnp.where(aug[h], one, zero)) for h in range(2)]
        da = [jnp.where(own[h], dob, jnp.where(aug[h], dd, zero)) for h in range(2)]
        km = [jnp.where(own[h], k, zero) for h in range(2)]
        return va, da, km, q.astype(F32).T.astype(BF), dof.T.astype(BF)

    def project_back(a):
        gr = dot_tn(x[...], g[a])
        for c in range(3):
            gsum[a, c * D : (c + 1) * D, :] = gr[:, c * PAIR : (c + 1) * PAIR].astype(BF)

    def long():
        for a in range(n):
            for c in small_loads(a) + [e_load(a, i) for i in range(4)]:
                c.start()
        x_load.start()
        for a in range(n):
            for c in small_loads(a):
                c.wait()
            va, da, km, qt, dt = prepare(a)

            def weights(item):
                t, h = item
                return dot_nt(da[h][t * tile : (t + 1) * tile], va[h])

            ahead = weights(items[0])
            for i, item in enumerate(items):
                dp = ahead
                if i + 1 < len(items):
                    ahead = weights(items[i + 1])
                t, h = item
                rows = slice(t * tile, (t + 1) * tile)
                e_load(a, i).wait()
                ds[a, h, rows, :] = e[a, h, rows, :] * dp.astype(BF)
            dq = dot(ds[a, 0], km[0]) + dot(ds[a, 1], km[1])
            g[a, :, :PAIR] = (dq * SCALE).astype(BF)
            vt = [dot(dt[hs[h]], e[a, h]) for h in range(2)]
            kt = [dot(qt[hs[h]], ds[a, h]) for h in range(2)]
            g[a, :, 2 * PAIR :] = jnp.concatenate(vt, 0).T.astype(BF)
            g[a, :, PAIR : 2 * PAIR] = jnp.concatenate(kt, 0).T.astype(BF)
            store_g(a).start()
            if a == 0:
                x_load.wait()
            project_back(a)

    def short():
        for a in range(n):
            for c in small_loads(a) + [e_load_short(a)]:
                c.start()
        x_load.start()
        for a in range(n):
            for c in small_loads(a) + [e_load_short(a)]:
                c.wait()
        x_load.wait()

        def pair(a, carry):
            va, da, km, qt, dt = prepare(a)
            for h in range(2):
                sva[h], sda[h], skm[h] = va[h], da[h], km[h]
            sqt[...] = qt
            sdt[...] = dt

            def block(t, carry):
                rows = pl.ds(pl.multiple_of(t * SHORT, SHORT), SHORT)
                dq, vt, kt = 0.0, [], []
                for h in range(2):
                    ex = e[a, h, rows, 0:SHORT]
                    d = ex * dot_nt(sda[h, rows, :], sva[h, rows, :]).astype(BF)
                    dq = dq + dot(d, skm[h, rows, :])
                    vt.append(dot(sdt[hs[h], rows], ex))
                    kt.append(dot(sqt[hs[h], rows], d))
                g[a, rows, :PAIR] = (dq * SCALE).astype(BF)
                g[a, rows, 2 * PAIR :] = jnp.concatenate(vt, 0).T.astype(BF)
                g[a, rows, PAIR : 2 * PAIR] = jnp.concatenate(kt, 0).T.astype(BF)
                return carry

            lax.fori_loop(0, ROWS // SHORT, block, 0)
            store_g(a).start()
            project_back(a)
            return carry

        lax.fori_loop(0, n, pair, 0)

    pl.when(code[1] == 1)(long)
    pl.when(code[1] == 0)(short)

    def put(i, carry):
        a, j = i // 8, i % 8
        block = gsum[a, pl.ds(pl.multiple_of(j * PART, PART), PART), :]
        rel = (j % 4) ^ code[5]
        at = (rel & 1) + jnp.where(j // 4 == 0, (rel >> 1) * 4 + a * 2, (rel >> 1) * 2 + a * 4)
        rows = pl.ds(pl.multiple_of(at * PART, PART), PART)

        @pl.when(code[0] == j // 4)
        def _():
            keep[rows, :] = block

        @pl.when(code[0] != j // 4)
        def _():
            send[rows, :] = block

        return carry

    lax.fori_loop(0, 8 * n, put, 0)
    for a in range(n):
        store_g(a).wait()
    bgs = [jnp.concatenate([colsum(g[a, :, :PAIR].astype(F32)), colsum(g[a, :, 2 * PAIR :].astype(F32))], 0) for a in range(n)]
    if not last:
        bg_out[...] = jnp.concatenate(bgs + [jnp.zeros((4, PAIR), F32)], 0)
        return
    for i in range(6):
        for c in range(4):
            vrow[i * 4 + c : i * 4 + c + 1, :] = vec[i : i + 1, c * PAIR : (c + 1) * PAIR]
    for c in range(16):
        vrow[24 + c : 25 + c, :] = vup[0:1, c * PAIR : (c + 1) * PAIR]
    known = [bg_in[0:2], bg_in[2:4]] + bgs
    for p in range(4):
        vrow[40 + 2 * p : 42 + 2 * p, :] = sum(jnp.where((code[4] ^ s) == p, b, 0.0) for s, b in enumerate(known))
    vrow[48:, :] = jnp.zeros((VROWS - 48, PAIR), F32)
    v_out[...] = vrow[...].astype(BF)
    send[8 * PART :, :] = v_out[...]


def attention_backward(code, x, hg, slots, at_o, es, qkvs, os, rls, small=None):
    S, n, last = jax.ShapeDtypeStruct, len(slots), small is not None
    ins = [code, x, hg, *es, *qkvs, *os, *rls] + list(small or ())
    rows = 4 * n * PART
    outs = [S((n, ROWS, 3 * PAIR), BF), S((rows, PAIR), BF), S((rows + VROWS * last, PAIR), BF), S((VROWS, PAIR), BF) if last else S((8, PAIR), F32)]
    scratch = [((ROWS, D), BF), ((n, 2, ROWS, ROWS), BF), ((n, ROWS, 3 * PAIR), BF), ((n, ROWS, PAIR), BF), ((n, ROWS, PAIR), BF),
               ((n, ROWS, PAIR), F32), ((n, 2, ROWS, ROWS), BF), ((n, ROWS, 3 * PAIR), BF), ((n, 3 * D, PAIR), BF), ((VROWS, PAIR), F32)]
    scratch += [((2, ROWS, PAIR), BF)] * 3 + [((PAIR, ROWS), BF)] * 2
    return pl.pallas_call(
        lambda *refs: bwd_kernel(slots, at_o, last, *refs),
        in_specs=[SMEM] + [HBM] * (2 + 4 * n) + [VM] * (3 * last),
        out_specs=[HBM, VM, VM, VM],
        out_shape=outs,
        scratch_shapes=[pltpu.VMEM(*a) for a in scratch] + [pltpu.SemaphoreType.DMA((8 * n + 1,)), pltpu.SemaphoreType.DMA((n,))],
        compiler_params=params(0),
        cost_estimate=cost(n * 8e9, n * 8 << 20),
    )(*ins)


def gelu_parts(u):
    cdf = 0.5 + 0.5 * lax.erf(u * math.sqrt(0.5))
    density = jnp.exp2(u * u * (-0.5 * math.log2(math.e))) * (1.0 / math.sqrt(2.0 * math.pi))
    return u * cdf, cdf + u * density


def norm_parts(h):
    m = jnp.mean(h, -1, keepdims=True)
    c = h - m
    r = lax.rsqrt(jnp.mean(c * c, -1, keepdims=True) + 1e-5)
    return c * r, r


def norm_back(e, gain, z, r):
    eg = e * gain
    return r * (eg - jnp.mean(eg, -1, keepdims=True) - z * jnp.mean(eg * z, -1, keepdims=True))


def colsum(a):
    return jnp.sum(a, 0, keepdims=True)


BLOCKS, BLOCK = 16, 144


def place(block, size, base, first, half, code, out):
    low = code[2 + half]
    for s in range(block.shape[0] // size):
        out[(first + s) ^ low, base : base + size, :] = block[s * size : (s + 1) * size].astype(BF)


def ffn_kernel(code, x_, acc_, oa_, ob_, oc_, wo, bo, g1, s1, wu_, bu, wd_, bd, g2, s2, sc_, ac_,
               ns_, na_, fg_, hg_, keep0, keep1, send0, send1, vec, vup,
               x, acc, oa, ob, oc, od, sc, ac, wu, wd, ns, na, fg, hg, keep, send, wp, hid, bfull, lfull, pfull, ofull, afull, isem, osem):
    tiles = [slice(t * QB, (t + 1) * QB) for t in range(ROWS // QB)]
    loads, stores = {}, []

    def load(name, src, dst, t=None):
        at = pl.ds(t * QB, QB) if t is not None else pl.ds(0, src.shape[0])
        loads[name, t] = pltpu.make_async_copy(src.at[at], dst.at[at], isem.at[len(loads)])
        loads[name, t].start()

    def store(src, dst, *at):
        stores.append(pltpu.make_async_copy(src.at[at], dst.at[at], osem.at[len(stores)]))
        stores[-1].start()

    by_tile = (("oa", oa_.at[0], oa), ("ob", oc_.at[0], ob), ("oc", ob_.at[0], oc), ("od", oc_.at[1], od), ("x", x_, x), ("acc", acc_, acc), ("sc", sc_, sc), ("ac", ac_, ac))
    for t in (0, 1):
        for name, src, dst in by_tile[:5]:
            load(name, src, dst, t)
    load("wu", wu_, wu)
    load("wd", wd_, wd)
    for name, src, dst in by_tile[5:]:
        for t in (0, 1):
            load(name, src, dst, t)
    for t in (2, 3):
        for name, src, dst in by_tile:
            load(name, src, dst, t)

    for s in range(D // PAIR):
        at = pl.multiple_of((code[4] ^ s) * PAIR, PAIR)
        wp[s * PAIR : (s + 1) * PAIR, :] = wo[pl.ds(at, PAIR), :]

    def wait(t, *names):
        for name in names:
            loads[name, t].wait()

    sums, up_sum = [0.0] * 6, 0.0
    for group in ((0, 1), (2, 3)):
        att, z1, r1, first, hidden, slope, si, bgs, pgs, ags = {}, {}, {}, {}, {}, {}, {}, {}, {}, {}
        for t in group:
            wait(t, "oa", "ob", "oc", "od")
            ofull[tiles[t], :] = jnp.concatenate([oa[tiles[t]], ob[tiles[t]], oc[tiles[t]], od[tiles[t]]], axis=1)
            att[t] = dot(ofull[tiles[t], :], wp[...]) + bo[...]
        for t in group:
            wait(t, "x")
            z1[t], r1[t] = norm_parts(x[tiles[t]].astype(F32) + att[t])
            first[t] = z1[t] * g1[...] + s1[...]
            lfull[tiles[t], :] = first[t].astype(BF)
        if group[0] == 0:
            wait(None, "wu")
        ups = {t: dot(first[t].astype(BF), wu[...]) for t in group}
        for t in group:
            a, slope[t] = gelu_parts(ups[t] + bu[...])
            hidden[t] = a.astype(BF)
            hid[tiles[t], :] = hidden[t]
        if group[0] == 0:
            wait(None, "wd")
        branch = {t: dot(hidden[t], wd[...]) + bd[...] for t in group}
        for t in group:
            wait(t, "acc", "sc", "ac")
            na[tiles[t]] = acc[tiles[t]] + att[t] + branch[t]
            store(na, na_, pl.ds(t * QB, QB))
            z2, r2 = norm_parts(first[t] + branch[t])
            ns[tiles[t]] = (z2 * g2[...] + s2[...]).astype(BF)
            store(ns, ns_, pl.ds(t * QB, QB))
            e2 = sc[tiles[t]]
            si[t] = norm_back(e2, g2[...], z2, r2)
            bgs[t] = (si[t] + ac[tiles[t]]).astype(BF)
            bfull[tiles[t], :] = bgs[t]
            sums[3:] = [a + colsum(b) for a, b in zip(sums[3:], (bgs[t].astype(F32), e2 * z2, e2))]
        hgs = {t: dot_nt(bgs[t], wd[...]) for t in group}
        for t in group:
            pgs[t] = (hgs[t] * slope[t]).astype(BF)
            pfull[tiles[t], :] = pgs[t]
            up_sum += colsum(pgs[t].astype(F32))
        es = {t: dot_nt(pgs[t], wu[...]) for t in group}
        for t in group:
            e1 = es[t] + si[t]
            fi = norm_back(e1, g1[...], z1[t], r1[t])
            fg[tiles[t]] = fi
            store(fg, fg_, pl.ds(t * QB, QB))
            ags[t] = (fi + ac[tiles[t]]).astype(BF)
            afull[tiles[t], :] = ags[t]
            sums[:3] = [a + colsum(b) for a, b in zip(sums[:3], (ags[t].astype(F32), e1 * z1[t], e1))]
        for t in group:
            hg[tiles[t]] = dot_nt(ags[t], wp[...]).astype(BF)
            store(hg, hg_, pl.ds(t * QB, QB))
    for j, s in enumerate(sums):
        vec[j : j + 1, :] = s
    vec[6:8, :] = jnp.zeros((2, D), F32)
    vup[0:1, :] = up_sum
    quarter = BLOCKS // 2
    for half, out, dsts in ((1, send, (send0, send1)), (0, keep, (keep0, keep1))):

        def ship(base, size):
            for k in (1, 0):
                src = out.at[pl.ds(k * quarter, quarter), pl.ds(base, size)]
                stores.append(pltpu.make_async_copy(src, dsts[k].at[:, pl.ds(base, size)], osem.at[len(stores)]))
                stores[-1].start()

        mine = code[0] ^ half
        for b in range(4):
            at = pl.multiple_of(mine * 1024 + b * 256, 256)
            place(dot_tn(hid[:, pl.ds(at, 256)], bfull[...]), 64, 0, b * 4, half, code, out)
        ship(0, 64)
        for c in range(2):
            at = pl.multiple_of(mine * 1024 + c * 512, 512)
            place(dot_tn(lfull[...], pfull[:, pl.ds(at, 512)]), 64, 64, c * 8, half, code, out)
        ship(64, 64)
        for p in range(2):
            at = pl.multiple_of(((mine * 2 + p) ^ code[4]) * PAIR, PAIR)
            place(dot_tn(ofull[:, pl.ds(at, PAIR)], afull[...]), 16, 128, p * 8, half, code, out)
        ship(128, 16)
    for c in stores:
        c.wait()


def ffn(code, x, acc, os, wo, bo, g1, s1, wu, bu, wd, bd, g2, s2, sc, ac):
    S = jax.ShapeDtypeStruct
    bo, g1, s1, bu, bd, g2, s2 = (v.reshape(1, -1) for v in (bo, g1, s1, bu, bd, g2, s2))
    ins = (code, x, acc, *os, wo, bo, g1, s1, wu, bu, wd, bd, g2, s2, sc, ac)
    specs = [SMEM] + [HBM] * 5 + [VM] * 4 + [HBM, VM, HBM] + [VM] * 3 + [HBM] * 2
    outs = [S((ROWS, D), BF), S((ROWS, D), F32), S((ROWS, D), F32), S((ROWS, D), BF)]
    outs += [S((BLOCKS // 2, BLOCK, D), BF)] * 4 + [S((8, D), F32), S((1, FF), F32)]
    buffers = [x, acc] + [S((ROWS, PAIR), BF)] * 4 + [sc, ac, wu, wd] + outs[:4] + [S((BLOCKS, BLOCK, D), BF)] * 2
    scratch = [pltpu.VMEM(a.shape, a.dtype) for a in buffers]
    scratch += [pltpu.VMEM(s, BF) for s in ((D, D), (ROWS, FF), (ROWS, D), (ROWS, D), (ROWS, FF), (ROWS, D), (ROWS, D))]
    return pl.pallas_call(
        ffn_kernel,
        in_specs=specs,
        out_specs=[HBM] * 8 + [VM] * 2,
        out_shape=outs,
        scratch_shapes=scratch + [pltpu.SemaphoreType.DMA((34,)), pltpu.SemaphoreType.DMA((28,))],
        compiler_params=params(0),
        cost_estimate=cost(25e9, 20 << 20),
    )(*ins)


def back_stream_kernel(code, fg, ga, gb, *refs):
    was, wbs, out = refs[:4], refs[4:8], refs[8]
    ca = pl.multiple_of(code[0] * HALF, HALF)
    cb = pl.multiple_of(HALF - code[0] * HALF, HALF)
    for at, ws in ((ca, was), (cb, wbs)):
        t = fg[:, pl.ds(at, HALF)]
        for s, w in enumerate(ws):
            t = t + dot_nt((ga if s < 2 else gb)[s % 2], side(w))
        out[:, pl.ds(at, HALF)] = t


def back_stream(code, fg, ga, gb, was, wbs):
    return pl.pallas_call(
        back_stream_kernel,
        grid=(ROWS // QB,),
        in_specs=[SMEM, pl.BlockSpec((QB, D), lambda i: (i, 0))] + [pl.BlockSpec((2, QB, 3 * PAIR), lambda i: (0, i, 0))] * 2 + [whole((PACK, PAIR))] * 8,
        out_specs=pl.BlockSpec((QB, D), lambda i: (i, 0)),
        out_shape=jax.ShapeDtypeStruct((ROWS, D), F32),
        compiler_params=params(1, 16),
        cost_estimate=cost(4e9, 8 << 20),
    )(code, fg, ga, gb, *was, *wbs)


def general_gather(inward, inward_bias):
    full = lax.all_gather(inward, "head", axis=2, tiled=True)
    bias = lax.all_gather(inward_bias, "head", axis=1, tiled=True)
    was, wbs = [], []
    for p in range(D // PAIR):
        cols = slice(p * PAIR, (p + 1) * PAIR)
        tail = jnp.pad(bias[:, cols], ((0, 14), (0, 0)))
        was.append(jnp.concatenate([full[:, :HALF, cols].reshape(3 * HALF, PAIR), tail], 0))
        wbs.append(jnp.concatenate([full[:, HALF:, cols].reshape(3 * HALF, PAIR), tail], 0))
    return was, wbs


def general_sums(blocks, pair_parts, vectors):
    both = ("batch", "head")
    whole_half, vectors = lax.psum((blocks, vectors), both)
    wide = whole_half.astype(F32)
    dwd = wide[:, :64].reshape(FF, D)
    dwu = wide[:, 64:128].reshape(4, D, D).transpose(1, 0, 2).reshape(D, FF)
    dwo = wide[:, 128:].reshape(D, D)
    wg = []
    for k, n in pair_parts:
        k = k[: 8 * PART].reshape(2, 2, 2 * PART, PAIR).swapaxes(0, 1)
        n = n[: 8 * PART].reshape(2, 2, 2 * PART, PAIR)
        wg += [jnp.concatenate([k[a], n[a]], 0).reshape(3, D, PAIR) for a in range(2)]
    wg = lax.psum(lax.psum_scatter(jnp.concatenate(wg, 2), "head", scatter_dimension=2, tiled=True), "batch")
    rows = vectors[:48].astype(F32).reshape(-1)
    bias = rows[5120:].reshape(D // PAIR, 2, PAIR).transpose(1, 0, 2).reshape(2, D)
    width = D // lax.axis_size("head")
    bias = lax.dynamic_slice_in_dim(bias, lax.axis_index("head") * width, width, 1)
    return wg.astype(F32), bias, dwo, dwu, dwd, rows


def swap(x, masks):
    n_batch, n_head = lax.axis_size("batch"), lax.axis_size("head")
    pairs = []
    for b in range(n_batch):
        for h in range(n_head):
            axis, mask = masks[b & 1]
            to = (b ^ mask, h) if axis == "batch" else (b, h ^ mask)
            pairs.append((b * n_head + h, to[0] * n_head + to[1]))
    return lax.ppermute(x, ("batch", "head"), pairs)


CORE = (("batch", 1), ("batch", 1))
X, Y, NEAR, FAR = ("batch", 2), ("batch", 4), ("head", 1), ("head", 2)
STEPS = ((X, NEAR), (NEAR, X), (Y, FAR), (FAR, Y))
PAIR_STEPS = ((X, NEAR), (NEAR, X), (Y, Y), (FAR, FAR))


def place_code(steps, core, index):
    code = 0
    for masks in steps:
        bits = []
        for axis, mask in masks:
            bits.append(((index[axis] & mask) > 0).astype(jnp.int32))
        code = code * 2 + jnp.where(core == 0, bits[0], bits[1])
    return code


def add(a, b):
    return (a.astype(F32) + b.astype(F32)).astype(BF)


def after(x, *others):
    return lax.optimization_barrier((x, *others))[0]


def combine_kernel(n_keep, *refs):
    keeps, gots, v = refs[:n_keep], refs[n_keep : 2 * n_keep], refs[2 * n_keep]
    keep, send, v_out = refs[2 * n_keep + 1 :]
    half = keep.shape[0]
    step = PART if n_keep > 1 else half
    for b in range(keeps[0].shape[0] // step):
        for a, (k, r) in enumerate(zip(keeps, gots)):
            at, to = b * step, (b * n_keep + a) * step
            total = add(k[at : at + step, :], r[at : at + step, :])
            if to < half:
                keep[to : to + step, :] = total
            else:
                send[to - half : to - half + step, :] = total
    total = add(v[...], gots[-1][-VROWS:, :])
    v_out[...] = total
    if send.shape[0] > half:
        send[half:, :] = total


def combine(keeps, gots, v):
    S, n = jax.ShapeDtypeStruct, len(keeps)
    half = sum(k.shape[0] for k in keeps) // 2
    return pl.pallas_call(
        lambda *refs: combine_kernel(n, *refs),
        in_specs=[VM] * (2 * n + 1),
        out_specs=[VM] * 3,
        out_shape=[S((half, PAIR), BF), S((half + VROWS, PAIR), BF), S((VROWS, PAIR), BF)],
        compiler_params=pltpu.CompilerParams(vmem_limit_bytes=16 << 20),
        cost_estimate=cost(1e6, 2 << 20),
    )(*keeps, *gots, v)


def widen_kernel(code, src, *refs):
    dwd, dwu, dwo = refs[-3:]
    for s in range(4):
        at = (pl.program_id(0) * 4 + s) ^ (code[1] & 7)
        dwd[s * 64 : (s + 1) * 64, :] = src[at, 0:64].astype(F32)
        dwu[s * 64 : (s + 1) * 64, :] = src[at, 64:128].astype(F32)
        dwo[s * 16 : (s + 1) * 16, :] = src[at, 128:144].astype(F32)


def widen(quarter, low, src, before=()):
    S = jax.ShapeDtypeStruct
    spec = pltpu.PrefetchScalarGridSpec(
        num_scalar_prefetch=1,
        grid=(2,),
        in_specs=[pl.BlockSpec((BLOCKS // 2, BLOCK, D), lambda i, c: (0, 0, 0))] + [HBM] * len(before),
        out_specs=[
            pl.BlockSpec((256, D), lambda i, c: (c[0] * 2 + i, 0)),
            pl.BlockSpec((256, D), lambda i, c: (i, c[0])),
            pl.BlockSpec((64, D), lambda i, c: (c[0] * 2 + i, 0)),
        ],
    )
    return pl.pallas_call(
        widen_kernel,
        grid_spec=spec,
        out_shape=[S((FF, D), F32), S((D, FF), F32), S((D, D), F32)],
        input_output_aliases={2 + k: k for k in range(len(before))},
        compiler_params=params(1, 16),
        cost_estimate=cost(1e6, 4 << 20),
    )(jnp.stack([quarter, low]), src, *before)


def finish_kernel(code, own, other, v, wg, bg, *outs):
    for j in range(8):
        rel = (j % 4) ^ code[5]
        at = pl.multiple_of(((rel & 1) * 2 + (rel >> 1)) * PART, PART)

        def put(src, j=j, at=at):
            block = src[pl.ds(at, PART), :].astype(F32)
            for r in range(0, PART, 64):
                to = j * PART + r
                wg[to // D, to % D : to % D + 64] = block[r : r + 64]

        pl.when(code[0] == j // 4)(lambda: put(own))
        pl.when(code[0] != j // 4)(lambda: put(other))

    rows = v[...].astype(F32)
    for i in range(6):
        for c in range(4):
            outs[i][0:1, c * PAIR : (c + 1) * PAIR] = rows[i * 4 + c : i * 4 + c + 1]
    for c in range(16):
        outs[6][0:1, c * PAIR : (c + 1) * PAIR] = rows[24 + c : 25 + c]
    for p in range(4):

        @pl.when(code[4] == p)
        def _():
            bg[...] = rows[40 + 2 * p : 42 + 2 * p]


def finish(code, own, other, v):
    S = jax.ShapeDtypeStruct
    return pl.pallas_call(
        finish_kernel,
        in_specs=[SMEM, VM, VM, VM],
        out_specs=[VM] * 9,
        out_shape=[S((3, D, PAIR), F32), S((2, PAIR), F32)] + [S((1, D), F32)] * 6 + [S((1, FF), F32)],
        compiler_params=pltpu.CompilerParams(vmem_limit_bytes=16 << 20),
        cost_estimate=cost(1e6, 3 << 20),
    )(code, own, other, v)


def body(stream, accumulator, inward, inward_bias, outward, outward_bias, first_gain, first_shift, up_weight, up_bias,
         down_weight, down_bias, second_gain, second_shift, long_count, stream_cotangent, accumulator_cotangent):
    assert stream.shape == (ROWS, D)
    b, h = lax.axis_index("batch"), lax.axis_index("head")
    tuned = (lax.axis_size("batch"), lax.axis_size("head")) == (8, 4)
    flag = (h < long_count[0]).astype(jnp.int32)
    zero = jnp.zeros((), jnp.int32)
    if tuned:
        core, index = b & 1, {"batch": b, "head": h}
        low, other = (place_code(STEPS, c, index) for c in (core, 1 - core))
        across = place_code(((X, X), (Y, Y)), core, index)
        code = jnp.stack([core, flag, low, other, h, across, zero, zero])
        rows = inward.reshape(3, 2, HALF, PAIR)
        bias = jnp.pad(inward_bias, ((0, 14), (0, 0)))
        wa = jnp.concatenate([lax.dynamic_index_in_dim(rows, core, 1, False).reshape(3 * HALF, PAIR), bias], 0)
        wb = jnp.concatenate([lax.dynamic_index_in_dim(rows, 1 - core, 1, False).reshape(3 * HALF, PAIR), bias], 0)
        was, wbs = [wa], [wb]
    else:
        code = jnp.stack([zero, flag] + [zero] * 6)
        was, wbs = general_gather(inward, inward_bias)

    heads = [attention_forward(code, stream, was[:1], wbs[:1])]
    if tuned:
        far = after(swap(wa, (FAR, FAR)), heads[0][1])
        other_far = swap(far, CORE)
        heads.append(attention_forward(code, stream, [far], [other_far]))
        two = [after(swap(w, (NEAR, NEAR)), heads[1][1]) for w in (wa, far)]
        other_two = [swap(w, CORE) for w in two]
        was, wbs = [wa, two[0], far, two[1]], [wb, other_two[0], other_far, other_two[1]]
    else:
        heads.append(attention_forward(code, stream, was[2:3], wbs[2:3]))
    heads.append(attention_forward(code, stream, was[1::2], wbs[1::2]))
    place_of = ((0, 0), (2, 0), (1, 0), (2, 1))
    ns, na, fg, hg, *halves, vec, vup = ffn(
        code, stream, accumulator, [t[1] for t in heads], outward, outward_bias, first_gain, first_shift, up_weight, up_bias,
        down_weight, down_bias, second_gain, second_shift, stream_cotangent, accumulator_cotangent)

    def backward(slots, x, small=None):
        t = [heads[place_of[s][0]] for s in slots]
        at = [place_of[s][1] for s in slots]
        return attention_backward(code, x, hg, slots, at, [a[0] for a in t], [a[2] for a in t], [a[1] for a in t], [a[3] for a in t], small)

    if not tuned:
        ga, ka, na_, bg = backward((0, 1), stream)
        gb, kb, nb_, v = backward((2, 3), stream, (vec, vup, bg))
        wg, bias, dwo, dwu, dwd, rows = general_sums(jnp.concatenate(halves, 0), ((ka, na_), (kb, nb_)), v)
        sg = back_stream(code, fg, ga, gb, was, wbs)
        vecs, vup = [rows[i * D : (i + 1) * D] for i in range(6)], rows[6 * D : 6 * D + FF]
    else:
        keep0, keep1, send0, send1 = halves
        out = add(keep1, swap(send1, CORE))
        got0 = swap(send0, CORE)
        got = swap(out, STEPS[0])
        cur = add(keep0, got0)
        ga, ka, sa, bg = backward((0, 1), after(stream, out, cur))
        ra = swap(sa, CORE)
        cur = add(after(cur, ka), got)
        out = cur[4:]
        got = swap(out, STEPS[1])
        gb, kb, sb, v = backward((2, 3), after(stream, out), (vec, vup, bg))
        rb = swap(sb, CORE)
        cur = add(after(cur[:4], kb), got)
        out = cur[2:]
        got = swap(out, STEPS[2])
        k, s, v = combine([ka, kb], [ra, rb], after(v, out))
        got2 = swap(s, PAIR_STEPS[0])
        cur = add(after(cur[:2], k), got)
        out = cur[1:]
        got = swap(out, STEPS[3])
        k, s, v = combine([k], [got2], after(v, out))
        got2 = swap(s, PAIR_STEPS[1])
        sg = back_stream(code, after(fg, s), ga, gb, was, wbs)
        cur = add(after(cur[:1], sg), got)
        got = swap(cur, STEPS[3])
        k, s, v = combine([k], [got2], after(v, cur))
        got2 = swap(s, PAIR_STEPS[2])
        cur = jnp.concatenate([after(cur, k), got], 0)
        got = swap(cur, STEPS[2])
        k, s, v = combine([k], [got2], after(v, cur))
        got2 = swap(s, PAIR_STEPS[3])
        v = add(v, got2[PART:])
        k = add(k, got2[:PART])
        got2 = swap(k, (X, X))
        cur = jnp.concatenate([after(cur, k), got], 0)
        got = swap(cur, STEPS[1])
        k = jnp.concatenate([after(k, cur), got2], 0)
        got2 = swap(k, (Y, Y))
        cur = jnp.concatenate([after(cur, k), got], 0)
        got = swap(cur, STEPS[0])
        other_cur = swap(cur, CORE)
        k = after(k, cur)
        mine, theirs = core * 2 + (low >> 3), (1 - core) * 2 + (other >> 3)
        wide = widen(theirs, other, other_cur, widen(mine, low, cur))
        k = jnp.concatenate([after(k, wide[0]), got2], 0)
        got2 = swap(k, CORE)
        wg, bias, *vecs, vup = finish(code, k, got2, v)
        vecs, vup = [t[0] for t in vecs], vup[0]
        got = after(got, bias)
        other_got = swap(got, CORE)
        wide = widen(mine ^ 1, low, got, wide)
        dwd, dwu, dwo = widen(theirs ^ 1, other, other_got, wide)
    return (ns, na, sg, wg, bias, dwo, vecs[0], vecs[1], vecs[2], dwu, vup, dwd, vecs[3], vecs[4], vecs[5])


def solution(mesh):
    tokens = P(("batch", "head"), None)
    in_specs = (tokens, tokens, P(None, None, "head"), P(None, "head")) + (P(),) * 10 + (P("batch"), tokens, tokens)
    out_specs = (tokens,) * 3 + (P(None, None, "head"), P(None, "head")) + (P(),) * 10
    return jax.shard_map(body, mesh=mesh, in_specs=in_specs, out_specs=out_specs, check_vma=False)
```

```python
import math

import jax
import jax.numpy as jnp
from jax import lax
from jax.experimental import pallas as pl
from jax.experimental.pallas import tpu as pltpu
from jax.sharding import PartitionSpec as P

F32, BF = jnp.float32, jnp.bfloat16
ROWS, D, FF, PAIR, HD, SHORT = 1024, 512, 2048, 128, 64, 256
QB = 256
SCALE = 1.0 / math.sqrt(HD)


def dot(a, b):
    return lax.dot_general(a, b, (((1,), (0,)), ((), ())), preferred_element_type=F32)


def dot_nt(a, b):
    return lax.dot_general(a, b, (((1,), (1,)), ((), ())), preferred_element_type=F32)


def dot_tn(a, b):
    return lax.dot_general(a, b, (((0,), (0,)), ((), ())), preferred_element_type=F32)


def params(n=1, mib=60):
    return pltpu.CompilerParams(dimension_semantics=("arbitrary",) * n or None, vmem_limit_bytes=mib << 20)


def cost(flops, nbytes):
    return pl.CostEstimate(flops=int(flops), bytes_accessed=int(nbytes), transcendentals=0)


SMEM = pl.BlockSpec(memory_space=pltpu.SMEM)
VM = pl.BlockSpec(memory_space=pltpu.VMEM)
HBM = pl.BlockSpec(memory_space=pltpu.HBM)


def whole(shape):
    return pl.BlockSpec(shape, lambda *_: (0,) * len(shape))


HALF = D // 2
PACK = 3 * HALF + 16


def side(w):
    return jnp.concatenate([w[c * HALF : (c + 1) * HALF] for c in range(3)], axis=1)


def fwd_kernel(n_pairs, code, x, *refs):
    was, wbs = refs[:n_pairs], refs[n_pairs : 2 * n_pairs]
    e, o, qkv, rl, es, qs_, va, sems, qsems = refs[2 * n_pairs :]
    ca = pl.multiple_of(code[0] * HALF, HALF)
    cb = pl.multiple_of(HALF - code[0] * HALF, HALF)
    lane = lax.broadcasted_iota(jnp.int32, (1, PAIR), 1)

    def run(short):
        copies = []

        def project(a):
            wa, wb = was[a], wbs[a]
            p = dot(x[:, pl.ds(ca, HALF)], side(wa)) + dot(x[:, pl.ds(cb, HALF)], side(wb))
            bq, bv = wa[3 * HALF : 3 * HALF + 1].astype(F32), wa[3 * HALF + 1 : 3 * HALF + 2].astype(F32)
            q = ((p[:, :PAIR] + bq).astype(BF).astype(F32) * SCALE).astype(BF)
            k = p[:, PAIR : 2 * PAIR].astype(BF)
            v = (p[:, 2 * PAIR :] + bv).astype(BF)
            qs_[a, :, :PAIR] = q
            qs_[a, :, PAIR : 2 * PAIR] = k
            qs_[a, :, 2 * PAIR :] = v
            copies.append(pltpu.make_async_copy(qs_.at[a], qkv.at[a], qsems.at[a]))
            copies[-1].start()
            return q, k, [jnp.where((lane < HD) == (h == 0), v, jnp.ones((), BF)) for h in range(2)]

        if short:
            for a in range(n_pairs):
                for h, v in enumerate(project(a)[2]):
                    va[a, h] = v

            def block(i, carry):
                a, t = i // (ROWS // SHORT), i % (ROWS // SHORT)
                rows = pl.ds(pl.multiple_of(t * SHORT, SHORT), SHORT)
                q, k = qs_[a, rows, :PAIR], qs_[a, rows, PAIR : 2 * PAIR]
                outs = []
                for h in range(2):
                    sc = dot_nt(jnp.where((lane < HD) == (h == 0), q, jnp.zeros((), BF)), k)
                    ex = jnp.exp(sc - jnp.max(sc, axis=1, keepdims=True)).astype(BF)
                    es[a, h, rows, 0:SHORT] = ex
                    u = dot(ex, va[a, h, rows, :])
                    r = 1.0 / pltpu.roll(u, HD, 1)
                    outs.append((u * r, r))
                o[a, rows, :] = jnp.where(lane < HD, outs[0][0], outs[1][0]).astype(BF)
                rl[a, rows, :] = jnp.where(lane < HD, outs[0][1], outs[1][1])
                return carry

            lax.fori_loop(0, n_pairs * (ROWS // SHORT), block, 0)
            at = (slice(None), slice(None), slice(None), pl.ds(0, SHORT))
            copies.append(pltpu.make_async_copy(es.at[at], e.at[at], sems.at[0]))
            copies[-1].start()
            for c in copies:
                c.wait()
            return

        ready = {0: project(0)}

        def score(item):
            a, qb, h = item
            q, k, _ = ready[a]
            qh = jnp.where((lane < HD) == (h == 0), q[qb * QB : (qb + 1) * QB], jnp.zeros((), BF))
            return dot_nt(qh, k)

        done = {}

        def product(item, ex):
            a, qb, h = item
            qs = slice(qb * QB, (qb + 1) * QB)
            u = dot(ex, ready[a][2][h])
            r = 1.0 / pltpu.roll(u, HD, 1)
            done[h] = (u * r, r)
            if h == 1:
                o[a, qs, :] = jnp.where(lane < HD, done[0][0], done[1][0]).astype(BF)
                rl[a, qs, :] = jnp.where(lane < HD, done[0][1], done[1][1])

        items = [(a, qb, h) for a in range(n_pairs) for qb in range(ROWS // QB) for h in range(2)]
        ahead, last = score(items[0]), None
        for i, item in enumerate(items):
            s = ahead
            if i + 1 < len(items):
                if items[i + 1][0] not in ready:
                    ready[items[i + 1][0]] = project(items[i + 1][0])
                ahead = score(items[i + 1])
            ex = jnp.exp(s - jnp.max(s, axis=1, keepdims=True)).astype(BF)
            a, qb, h = item
            at = (a, h, pl.ds(qb * QB, QB))
            es[at] = ex
            copies.append(pltpu.make_async_copy(es.at[at], e.at[at], sems.at[i]))
            copies[-1].start()
            if last is not None:
                product(*last)
            last = (item, ex)
        product(*last)
        for c in copies:
            c.wait()

    pl.when(code[1] == 1)(lambda: run(False))
    pl.when(code[1] == 0)(lambda: run(True))


def attention_forward(code, x, was, wbs):
    S, n = jax.ShapeDtypeStruct, len(was)
    return pl.pallas_call(
        lambda *refs: fwd_kernel(n, *refs),
        in_specs=[SMEM, VM] + [VM] * (2 * n),
        out_specs=[HBM, VM, HBM, VM],
        out_shape=[S((n, 2, ROWS, ROWS), BF), S((n, ROWS, PAIR), BF), S((n, ROWS, 3 * PAIR), BF), S((n, ROWS, PAIR), F32)],
        scratch_shapes=[pltpu.VMEM((n, 2, ROWS, ROWS), BF), pltpu.VMEM((n, ROWS, 3 * PAIR), BF), pltpu.VMEM((n, 2, ROWS, PAIR), BF),
                        pltpu.SemaphoreType.DMA((8 * n,)), pltpu.SemaphoreType.DMA((n,))],
        compiler_params=params(0),
        cost_estimate=cost(1e6, 1 << 10),
    )(code, x, *was, *wbs)


PART, VROWS = 192, 64


def bwd_kernel(slots, at_o, last, code, x_, hg_, *refs):
    n = len(slots)
    es_, qkvs_, os_, rls_ = (refs[k * n : (k + 1) * n] for k in range(4))
    refs = refs[4 * n :]
    if last:
        (vec, vup, *bg_ins), refs = refs[:4], refs[4:]
        g_, keep, send, v_out, x, e, qkv, o, do, rl, ds, g, gsum, vrow, sva, sda, skm, sqt, sdt, sems, gsems = refs
    else:
        g_, keep, send, bg_out, x, e, qkv, o, do, rl, ds, g, gsum, vrow, sva, sda, skm, sqt, sdt, sems, gsems = refs
    lane = lax.broadcasted_iota(jnp.int32, (1, PAIR), 1)
    first, zero, one = lane < HD, jnp.zeros((), BF), jnp.ones((), BF)
    row = lax.broadcasted_iota(jnp.int32, (PAIR, PAIR), 0)
    col = lax.broadcasted_iota(jnp.int32, (PAIR, PAIR), 1)
    pick = jnp.where(((row < HD) != (col < HD)) & ((col & (HD - 1)) < 2), 1.0, 0.0).astype(BF)
    hs = [slice(h * HD, (h + 1) * HD) for h in range(2)]
    tile = 512
    items = [(t, h) for t in range(ROWS // tile) for h in range(2)]

    def small_loads(a):
        pairs = ((hg_.at[:, pl.ds(slots[a] * PAIR, PAIR)], do), (rls_[a].at[at_o[a]], rl), (os_[a].at[at_o[a]], o), (qkvs_[a].at[at_o[a]], qkv))
        return [pltpu.make_async_copy(src, dst.at[a], sems.at[8 * a + k]) for k, (src, dst) in enumerate(pairs)]

    def e_load(a, i):
        t, h = items[i]
        at = (h, pl.ds(t * tile, tile))
        return pltpu.make_async_copy(es_[a].at[(at_o[a], *at)], e.at[(a, *at)], sems.at[8 * a + 4 + i])

    def e_load_short(a):
        at = (slice(None), slice(None), pl.ds(0, SHORT))
        return pltpu.make_async_copy(es_[a].at[(at_o[a], *at)], e.at[(a, *at)], sems.at[8 * a + 4])

    def store_g(a):
        return pltpu.make_async_copy(g.at[a], g_.at[a], gsems.at[a])

    x_load = pltpu.make_async_copy(x_, x, sems.at[8 * n])

    def prepare(a):
        dof = do[a].astype(F32) * rl[a]
        dob = dof.astype(BF)
        t = dof * o[a].astype(F32)
        th = t.astype(BF)
        tl = (t - th.astype(F32)).astype(BF)
        delta = -(dot(th, pick) + dot(tl, pick))
        dh = delta.astype(BF)
        dd = jnp.where((lane & (HD - 1)) == 0, dh, (delta - dh.astype(F32)).astype(BF))
        q, k, v = qkv[a, :, :PAIR], qkv[a, :, PAIR : 2 * PAIR], qkv[a, :, 2 * PAIR :]
        own = [first == (h == 0) for h in range(2)]
        aug = [jnp.logical_not(own[h]) & ((lane & (HD - 1)) < 2) for h in range(2)]
        va = [jnp.where(own[h], v, jnp.where(aug[h], one, zero)) for h in range(2)]
        da = [jnp.where(own[h], dob, jnp.where(aug[h], dd, zero)) for h in range(2)]
        km = [jnp.where(own[h], k, zero) for h in range(2)]
        return va, da, km, q.astype(F32).T.astype(BF), dof.T.astype(BF)

    def project_back(a):
        gr = dot_tn(x[...], g[a])
        for c in range(3):
            gsum[a, c * D : (c + 1) * D, :] = gr[:, c * PAIR : (c + 1) * PAIR].astype(BF)

    def long():
        for a in range(n):
            for c in small_loads(a) + [e_load(a, i) for i in range(4)]:
                c.start()
        x_load.start()
        for a in range(n):
            for c in small_loads(a):
                c.wait()
            va, da, km, qt, dt = prepare(a)

            def weights(item):
                t, h = item
                return dot_nt(da[h][t * tile : (t + 1) * tile], va[h])

            ahead = weights(items[0])
            for i, item in enumerate(items):
                dp = ahead
                if i + 1 < len(items):
                    ahead = weights(items[i + 1])
                t, h = item
                rows = slice(t * tile, (t + 1) * tile)
                e_load(a, i).wait()
                ds[a, h, rows, :] = e[a, h, rows, :] * dp.astype(BF)
            dq = dot(ds[a, 0], km[0]) + dot(ds[a, 1], km[1])
            g[a, :, :PAIR] = (dq * SCALE).astype(BF)
            vt = [dot(dt[hs[h]], e[a, h]) for h in range(2)]
            kt = [dot(qt[hs[h]], ds[a, h]) for h in range(2)]
            g[a, :, 2 * PAIR :] = jnp.concatenate(vt, 0).T.astype(BF)
            g[a, :, PAIR : 2 * PAIR] = jnp.concatenate(kt, 0).T.astype(BF)
            store_g(a).start()
            if a == 0:
                x_load.wait()
            project_back(a)

    def short():
        for a in range(n):
            for c in small_loads(a) + [e_load_short(a)]:
                c.start()
        x_load.start()
        for a in range(n):
            for c in small_loads(a) + [e_load_short(a)]:
                c.wait()
        x_load.wait()

        def pair(a, carry):
            va, da, km, qt, dt = prepare(a)
            for h in range(2):
                sva[h], sda[h], skm[h] = va[h], da[h], km[h]
            sqt[...] = qt
            sdt[...] = dt

            def block(t, carry):
                rows = pl.ds(pl.multiple_of(t * SHORT, SHORT), SHORT)
                dq, vt, kt = 0.0, [], []
                for h in range(2):
                    ex = e[a, h, rows, 0:SHORT]
                    d = ex * dot_nt(sda[h, rows, :], sva[h, rows, :]).astype(BF)
                    dq = dq + dot(d, skm[h, rows, :])
                    vt.append(dot(sdt[hs[h], rows], ex))
                    kt.append(dot(sqt[hs[h], rows], d))
                g[a, rows, :PAIR] = (dq * SCALE).astype(BF)
                g[a, rows, 2 * PAIR :] = jnp.concatenate(vt, 0).T.astype(BF)
                g[a, rows, PAIR : 2 * PAIR] = jnp.concatenate(kt, 0).T.astype(BF)
                return carry

            lax.fori_loop(0, ROWS // SHORT, block, 0)
            store_g(a).start()
            project_back(a)
            return carry

        lax.fori_loop(0, n, pair, 0)

    pl.when(code[1] == 1)(long)
    pl.when(code[1] == 0)(short)

    def put(i, carry):
        a, j = i // 8, i % 8
        block = gsum[a, pl.ds(pl.multiple_of(j * PART, PART), PART), :]
        rel = (j % 4) ^ code[5]
        if n == 2:
            at = (rel >> 1) + jnp.where(j // 4 == 0, (rel & 1) * 4 + a * 2, (rel & 1) * 2 + a * 4)
        else:
            at = (rel >> 1) + (rel & 1) * 2
        rows = pl.ds(pl.multiple_of(at * PART, PART), PART)

        @pl.when(code[0] == j // 4)
        def _():
            keep[rows, :] = block

        @pl.when(code[0] != j // 4)
        def _():
            send[rows, :] = block

        return carry

    lax.fori_loop(0, 8 * n, put, 0)
    for a in range(n):
        store_g(a).wait()
    bgs = [jnp.concatenate([colsum(g[a, :, :PAIR].astype(F32)), colsum(g[a, :, 2 * PAIR :].astype(F32))], 0) for a in range(n)]
    if not last:
        bg_out[...] = jnp.concatenate(bgs + [jnp.zeros((8 - 2 * n, PAIR), F32)], 0)
        return
    for i in range(6):
        for c in range(4):
            vrow[i * 4 + c : i * 4 + c + 1, :] = vec[i : i + 1, c * PAIR : (c + 1) * PAIR]
    for c in range(16):
        vrow[24 + c : 25 + c, :] = vup[0:1, c * PAIR : (c + 1) * PAIR]
    known = [bg_ins[0][0:2], bg_ins[0][2:4], bg_ins[1][0:2]] + bgs
    for p in range(4):
        vrow[40 + 2 * p : 42 + 2 * p, :] = sum(jnp.where((code[4] ^ s) == p, b, 0.0) for s, b in enumerate(known))
    vrow[48:, :] = jnp.zeros((VROWS - 48, PAIR), F32)
    v_out[...] = vrow[...].astype(BF)
    send[4 * n * PART :, :] = v_out[...]


def attention_backward(code, x, hg, slots, at_o, es, qkvs, os, rls, small=None):
    S, n, last = jax.ShapeDtypeStruct, len(slots), small is not None
    ins = [code, x, hg, *es, *qkvs, *os, *rls] + list(small or ())
    rows = 4 * n * PART
    outs = [S((n, ROWS, 3 * PAIR), BF), S((rows, PAIR), BF), S((rows + VROWS * last, PAIR), BF), S((VROWS, PAIR), BF) if last else S((8, PAIR), F32)]
    scratch = [((ROWS, D), BF), ((n, 2, ROWS, ROWS), BF), ((n, ROWS, 3 * PAIR), BF), ((n, ROWS, PAIR), BF), ((n, ROWS, PAIR), BF),
               ((n, ROWS, PAIR), F32), ((n, 2, ROWS, ROWS), BF), ((n, ROWS, 3 * PAIR), BF), ((n, 3 * D, PAIR), BF), ((VROWS, PAIR), F32)]
    scratch += [((2, ROWS, PAIR), BF)] * 3 + [((PAIR, ROWS), BF)] * 2
    return pl.pallas_call(
        lambda *refs: bwd_kernel(slots, at_o, last, *refs),
        in_specs=[SMEM] + [HBM] * (2 + 4 * n) + [VM] * (4 * last),
        out_specs=[HBM, VM, VM, VM],
        out_shape=outs,
        scratch_shapes=[pltpu.VMEM(*a) for a in scratch] + [pltpu.SemaphoreType.DMA((8 * n + 1,)), pltpu.SemaphoreType.DMA((n,))],
        compiler_params=params(0, 44),
        cost_estimate=cost(n * 8e9, n * 8 << 20),
    )(*ins)


def gelu_parts(u):
    cdf = 0.5 + 0.5 * lax.erf(u * math.sqrt(0.5))
    density = jnp.exp2(u * u * (-0.5 * math.log2(math.e))) * (1.0 / math.sqrt(2.0 * math.pi))
    return u * cdf, cdf + u * density


def norm_parts(h):
    m = jnp.mean(h, -1, keepdims=True)
    c = h - m
    r = lax.rsqrt(jnp.mean(c * c, -1, keepdims=True) + 1e-5)
    return c * r, r


def norm_back(e, gain, z, r):
    eg = e * gain
    return r * (eg - jnp.mean(eg, -1, keepdims=True) - z * jnp.mean(eg * z, -1, keepdims=True))


def colsum(a):
    return jnp.sum(a, 0, keepdims=True)


BLOCKS, BLOCK = 16, 144


def place(block, size, base, first, half, code, out):
    low = code[2 + half]
    for s in range(block.shape[0] // size):
        out[(first + s) ^ low, base : base + size, :] = block[s * size : (s + 1) * size].astype(BF)


def ffn_kernel(code, x_, acc_, oa_, ob_, oc_, wo, bo, g1, s1, wu_, bu, wd_, bd, g2, s2, sc_, ac_,
               ns_, na_, fg_, hg_, keep0, keep1, send0, send1, vec, vup,
               x, acc, oa, ob, oc, od, sc, ac, wu, wd, ns, na, fg, hg, keep, send, wp, hid, bfull, lfull, pfull, ofull, afull, isem, osem):
    tiles = [slice(t * QB, (t + 1) * QB) for t in range(ROWS // QB)]
    loads, stores = {}, []

    def load(name, src, dst, t=None):
        at = pl.ds(t * QB, QB) if t is not None else pl.ds(0, src.shape[0])
        loads[name, t] = pltpu.make_async_copy(src.at[at], dst.at[at], isem.at[len(loads)])
        loads[name, t].start()

    def store(src, dst, *at):
        stores.append(pltpu.make_async_copy(src.at[at], dst.at[at], osem.at[len(stores)]))
        stores[-1].start()

    by_tile = (("oa", oa_.at[0], oa), ("ob", oc_.at[0], ob), ("oc", ob_.at[0], oc), ("od", oc_.at[1], od), ("x", x_, x), ("acc", acc_, acc), ("sc", sc_, sc), ("ac", ac_, ac))
    for t in (0, 1):
        for name, src, dst in by_tile[:5]:
            load(name, src, dst, t)
    load("wu", wu_, wu)
    load("wd", wd_, wd)
    for name, src, dst in by_tile[5:]:
        for t in (0, 1):
            load(name, src, dst, t)
    for t in (2, 3):
        for name, src, dst in by_tile:
            load(name, src, dst, t)

    for s in range(D // PAIR):
        at = pl.multiple_of((code[4] ^ s) * PAIR, PAIR)
        wp[s * PAIR : (s + 1) * PAIR, :] = wo[pl.ds(at, PAIR), :]

    def wait(t, *names):
        for name in names:
            loads[name, t].wait()

    sums, up_sum = [0.0] * 6, 0.0
    for group in ((0, 1), (2, 3)):
        att, z1, r1, first, hidden, slope, si, bgs, pgs, ags = {}, {}, {}, {}, {}, {}, {}, {}, {}, {}
        for t in group:
            wait(t, "oa", "ob", "oc", "od")
            ofull[tiles[t], :] = jnp.concatenate([oa[tiles[t]], ob[tiles[t]], oc[tiles[t]], od[tiles[t]]], axis=1)
            att[t] = dot(ofull[tiles[t], :], wp[...]) + bo[...]
        for t in group:
            wait(t, "x")
            z1[t], r1[t] = norm_parts(x[tiles[t]].astype(F32) + att[t])
            first[t] = z1[t] * g1[...] + s1[...]
            lfull[tiles[t], :] = first[t].astype(BF)
        if group[0] == 0:
            wait(None, "wu")
        ups = {t: dot(first[t].astype(BF), wu[...]) for t in group}
        for t in group:
            a, slope[t] = gelu_parts(ups[t] + bu[...])
            hidden[t] = a.astype(BF)
            hid[tiles[t], :] = hidden[t]
        if group[0] == 0:
            wait(None, "wd")
        branch = {t: dot(hidden[t], wd[...]) + bd[...] for t in group}
        for t in group:
            wait(t, "acc", "sc", "ac")
            na[tiles[t]] = acc[tiles[t]] + att[t] + branch[t]
            store(na, na_, pl.ds(t * QB, QB))
            z2, r2 = norm_parts(first[t] + branch[t])
            ns[tiles[t]] = (z2 * g2[...] + s2[...]).astype(BF)
            store(ns, ns_, pl.ds(t * QB, QB))
            e2 = sc[tiles[t]]
            si[t] = norm_back(e2, g2[...], z2, r2)
            bgs[t] = (si[t] + ac[tiles[t]]).astype(BF)
            bfull[tiles[t], :] = bgs[t]
            sums[3:] = [a + colsum(b) for a, b in zip(sums[3:], (bgs[t].astype(F32), e2 * z2, e2))]
        hgs = {t: dot_nt(bgs[t], wd[...]) for t in group}
        for t in group:
            pgs[t] = (hgs[t] * slope[t]).astype(BF)
            pfull[tiles[t], :] = pgs[t]
            up_sum += colsum(pgs[t].astype(F32))
        es = {t: dot_nt(pgs[t], wu[...]) for t in group}
        for t in group:
            e1 = es[t] + si[t]
            fi = norm_back(e1, g1[...], z1[t], r1[t])
            fg[tiles[t]] = fi
            store(fg, fg_, pl.ds(t * QB, QB))
            ags[t] = (fi + ac[tiles[t]]).astype(BF)
            afull[tiles[t], :] = ags[t]
            sums[:3] = [a + colsum(b) for a, b in zip(sums[:3], (ags[t].astype(F32), e1 * z1[t], e1))]
        for t in group:
            hg[tiles[t]] = dot_nt(ags[t], wp[...]).astype(BF)
            store(hg, hg_, pl.ds(t * QB, QB))
    for j, s in enumerate(sums):
        vec[j : j + 1, :] = s
    vec[6:8, :] = jnp.zeros((2, D), F32)
    vup[0:1, :] = up_sum
    quarter = BLOCKS // 2
    for half, out, dsts in ((1, send, (send0, send1)), (0, keep, (keep0, keep1))):

        def ship(base, size):
            for k in (1, 0):
                src = out.at[pl.ds(k * quarter, quarter), pl.ds(base, size)]
                stores.append(pltpu.make_async_copy(src, dsts[k].at[:, pl.ds(base, size)], osem.at[len(stores)]))
                stores[-1].start()

        mine = code[0] ^ half
        for b in range(4):
            at = pl.multiple_of(mine * 1024 + b * 256, 256)
            place(dot_tn(hid[:, pl.ds(at, 256)], bfull[...]), 64, 0, b * 4, half, code, out)
        ship(0, 64)
        for c in range(2):
            at = pl.multiple_of(mine * 1024 + c * 512, 512)
            place(dot_tn(lfull[...], pfull[:, pl.ds(at, 512)]), 64, 64, c * 8, half, code, out)
        ship(64, 64)
        for p in range(2):
            at = pl.multiple_of(((mine * 2 + p) ^ code[4]) * PAIR, PAIR)
            place(dot_tn(ofull[:, pl.ds(at, PAIR)], afull[...]), 16, 128, p * 8, half, code, out)
        ship(128, 16)
    for c in stores:
        c.wait()


def ffn(code, x, acc, os, wo, bo, g1, s1, wu, bu, wd, bd, g2, s2, sc, ac):
    S = jax.ShapeDtypeStruct
    bo, g1, s1, bu, bd, g2, s2 = (v.reshape(1, -1) for v in (bo, g1, s1, bu, bd, g2, s2))
    ins = (code, x, acc, *os, wo, bo, g1, s1, wu, bu, wd, bd, g2, s2, sc, ac)
    specs = [SMEM] + [HBM] * 5 + [VM] * 4 + [HBM, VM, HBM] + [VM] * 3 + [HBM] * 2
    outs = [S((ROWS, D), BF), S((ROWS, D), F32), S((ROWS, D), F32), S((ROWS, D), BF)]
    outs += [S((BLOCKS // 2, BLOCK, D), BF)] * 4 + [S((8, D), F32), S((1, FF), F32)]
    buffers = [x, acc] + [S((ROWS, PAIR), BF)] * 4 + [sc, ac, wu, wd] + outs[:4] + [S((BLOCKS, BLOCK, D), BF)] * 2
    scratch = [pltpu.VMEM(a.shape, a.dtype) for a in buffers]
    scratch += [pltpu.VMEM(s, BF) for s in ((D, D), (ROWS, FF), (ROWS, D), (ROWS, D), (ROWS, FF), (ROWS, D), (ROWS, D))]
    return pl.pallas_call(
        ffn_kernel,
        in_specs=specs,
        out_specs=[HBM] * 8 + [VM] * 2,
        out_shape=outs,
        scratch_shapes=scratch + [pltpu.SemaphoreType.DMA((34,)), pltpu.SemaphoreType.DMA((28,))],
        compiler_params=params(0),
        cost_estimate=cost(25e9, 20 << 20),
    )(*ins)


def back_stream_kernel(code, fg, ga, gb, gc, *refs):
    was, wbs, out = refs[:4], refs[4:8], refs[8]
    ca = pl.multiple_of(code[0] * HALF, HALF)
    cb = pl.multiple_of(HALF - code[0] * HALF, HALF)
    for at, ws in ((ca, was), (cb, wbs)):
        t = fg[:, pl.ds(at, HALF)]
        for s, w in enumerate(ws):
            t = t + dot_nt((ga[0], ga[1], gb[0], gc[0])[s], side(w))
        out[:, pl.ds(at, HALF)] = t


def back_stream(code, fg, gs, was, wbs):
    return pl.pallas_call(
        back_stream_kernel,
        grid=(ROWS // QB,),
        in_specs=[SMEM, pl.BlockSpec((QB, D), lambda i: (i, 0))] + [pl.BlockSpec((g.shape[0], QB, 3 * PAIR), lambda i: (0, i, 0)) for g in gs] + [whole((PACK, PAIR))] * 8,
        out_specs=pl.BlockSpec((QB, D), lambda i: (i, 0)),
        out_shape=jax.ShapeDtypeStruct((ROWS, D), F32),
        compiler_params=params(1, 56),
        cost_estimate=cost(4e9, 8 << 20),
    )(code, fg, *gs, *was, *wbs)


def general_gather(inward, inward_bias):
    full = lax.all_gather(inward, "head", axis=2, tiled=True)
    bias = lax.all_gather(inward_bias, "head", axis=1, tiled=True)
    was, wbs = [], []
    for p in range(D // PAIR):
        cols = slice(p * PAIR, (p + 1) * PAIR)
        tail = jnp.pad(bias[:, cols], ((0, 14), (0, 0)))
        was.append(jnp.concatenate([full[:, :HALF, cols].reshape(3 * HALF, PAIR), tail], 0))
        wbs.append(jnp.concatenate([full[:, HALF:, cols].reshape(3 * HALF, PAIR), tail], 0))
    return was, wbs


def general_sums(blocks, pair_parts, vectors):
    both = ("batch", "head")
    whole_half, vectors = lax.psum((blocks, vectors), both)
    wide = whole_half.astype(F32)
    dwd = wide[:, :64].reshape(FF, D)
    dwu = wide[:, 64:128].reshape(4, D, D).transpose(1, 0, 2).reshape(D, FF)
    dwo = wide[:, 128:].reshape(D, D)
    wg = []
    for k, n in pair_parts:
        if k.shape[0] == 8 * PART:
            k, n = k.reshape(2, 2, 2, PART, PAIR).swapaxes(0, 1), n.reshape(2, 2, 2, PART, PAIR)
        else:
            k, n = k.reshape(1, 2, 2, PART, PAIR), n[: 4 * PART].reshape(1, 2, 2, PART, PAIR)
        wg += [jnp.concatenate([t[a].swapaxes(0, 1).reshape(4 * PART, PAIR) for t in (k, n)], 0).reshape(3, D, PAIR) for a in range(k.shape[0])]
    wg = lax.psum(lax.psum_scatter(jnp.concatenate(wg, 2), "head", scatter_dimension=2, tiled=True), "batch")
    rows = vectors[:48].astype(F32).reshape(-1)
    bias = rows[5120:].reshape(D // PAIR, 2, PAIR).transpose(1, 0, 2).reshape(2, D)
    width = D // lax.axis_size("head")
    bias = lax.dynamic_slice_in_dim(bias, lax.axis_index("head") * width, width, 1)
    return wg.astype(F32), bias, dwo, dwu, dwd, rows


def swap(x, masks):
    n_batch, n_head = lax.axis_size("batch"), lax.axis_size("head")
    pairs = []
    for b in range(n_batch):
        for h in range(n_head):
            axis, mask = masks[b & 1]
            to = (b ^ mask, h) if axis == "batch" else (b, h ^ mask)
            pairs.append((b * n_head + h, to[0] * n_head + to[1]))
    return lax.ppermute(x, ("batch", "head"), pairs)


CORE = (("batch", 1), ("batch", 1))
X, Y, NEAR, FAR = ("batch", 2), ("batch", 4), ("head", 1), ("head", 2)
STEPS = ((X, NEAR), (NEAR, X), (Y, FAR), (FAR, Y))
PAIR_STEPS = ((Y, NEAR), (NEAR, Y), (FAR, FAR))


def place_code(steps, core, index):
    code = 0
    for masks in steps:
        bits = []
        for axis, mask in masks:
            bits.append(((index[axis] & mask) > 0).astype(jnp.int32))
        code = code * 2 + jnp.where(core == 0, bits[0], bits[1])
    return code


def add(a, b):
    return (a.astype(F32) + b.astype(F32)).astype(BF)


def after(x, *others):
    return lax.optimization_barrier((x, *others))[0]


def split_sum(total, to, keep, send):
    half = keep.shape[0]
    if to < half:
        keep[to : to + total.shape[0], :] = total
    else:
        send[to - half : to - half + total.shape[0], :] = total


def first_combine_kernel(code, ka, kb, kc, ra, rb, rc, v, keep, send, v_out):
    def place_at(q, far):
        return ((q >> 1) * 4 + far * 2 + (q & 1)) * PART

    for q in range(8):
        rows = slice(q * PART, (q + 1) * PART)
        split_sum(add(ka[rows, :], ra[rows, :]), place_at(q, 0), keep, send)
    for core in range(2):

        @pl.when(code[0] == core)
        def _():
            for k, r, near in ((kb, rb, 0), (kc, rc, 1)):
                for p in range(4):
                    rows = slice(p * PART, (p + 1) * PART)
                    q = (p & 1) + ((p >> 1) * 4 + near * 2 if core == 0 else (p >> 1) * 2 + near * 4)
                    split_sum(add(k[rows, :], r[rows, :]), place_at(q, 1), keep, send)

    v_out[...] = add(v[...], rc[-VROWS:, :])
    send[keep.shape[0] :, :] = v_out[...]


def combine_kernel(k, r, v, keep, send, v_out):
    half = keep.shape[0]
    for to in (0, half):
        split_sum(add(k[to : to + half, :], r[to : to + half, :]), to, keep, send)
    v_out[...] = add(v[...], r[-VROWS:, :])
    send[half:, :] = v_out[...]


def merge_kernel(k, r, v, out):
    n = k.shape[0]
    out[:n, :] = add(k[...], r[:n, :])
    out[n:, :] = add(v[...], r[n:, :])


def merge(k, r, v):
    return pl.pallas_call(
        merge_kernel,
        in_specs=[VM] * 3,
        out_specs=VM,
        out_shape=jax.ShapeDtypeStruct(r.shape, BF),
        compiler_params=pltpu.CompilerParams(vmem_limit_bytes=16 << 20),
        cost_estimate=cost(1e6, 1 << 18),
    )(k, r, v)


def combine(kernel, half, *args):
    S = jax.ShapeDtypeStruct
    return pl.pallas_call(
        kernel,
        in_specs=[SMEM] * (len(args) - 3 > 3) + [VM] * (len(args) - (len(args) - 3 > 3)),
        out_specs=[VM] * 3,
        out_shape=[S((half, PAIR), BF), S((half + VROWS, PAIR), BF), S((VROWS, PAIR), BF)],
        compiler_params=pltpu.CompilerParams(vmem_limit_bytes=16 << 20),
        cost_estimate=cost(1e6, 2 << 20),
    )(*args)


def widen_kernel(code, src, *refs):
    dwd, dwu, dwo = refs[-3:]
    for s in range(4):
        at = (pl.program_id(0) * 4 + s) ^ (code[1] & 7)
        dwd[s * 64 : (s + 1) * 64, :] = src[at, 0:64].astype(F32)
        dwu[s * 64 : (s + 1) * 64, :] = src[at, 64:128].astype(F32)
        dwo[s * 16 : (s + 1) * 16, :] = src[at, 128:144].astype(F32)


def widen(quarter, low, src, before=()):
    S = jax.ShapeDtypeStruct
    spec = pltpu.PrefetchScalarGridSpec(
        num_scalar_prefetch=1,
        grid=(2,),
        in_specs=[pl.BlockSpec((BLOCKS // 2, BLOCK, D), lambda i, c: (0, 0, 0))] + [HBM] * len(before),
        out_specs=[
            pl.BlockSpec((256, D), lambda i, c: (c[0] * 2 + i, 0)),
            pl.BlockSpec((256, D), lambda i, c: (i, c[0])),
            pl.BlockSpec((64, D), lambda i, c: (c[0] * 2 + i, 0)),
        ],
    )
    return pl.pallas_call(
        widen_kernel,
        grid_spec=spec,
        out_shape=[S((FF, D), F32), S((D, FF), F32), S((D, D), F32)],
        input_output_aliases={2 + k: k for k in range(len(before))},
        compiler_params=params(1, 16),
        cost_estimate=cost(1e6, 4 << 20),
    )(jnp.stack([quarter, low]), src, *before)


def finish_kernel(code, own, other, v, wg, bg, *outs):
    for j in range(8):
        rel = (j % 4) ^ code[5]
        at = pl.multiple_of(((rel & 1) * 2 + (rel >> 1)) * PART, PART)

        def put(src, j=j, at=at):
            block = src[pl.ds(at, PART), :].astype(F32)
            for r in range(0, PART, 64):
                to = j * PART + r
                wg[to // D, to % D : to % D + 64] = block[r : r + 64]

        pl.when(code[0] == j // 4)(lambda: put(own))
        pl.when(code[0] != j // 4)(lambda: put(other))

    rows = v[...].astype(F32)
    for i in range(6):
        for c in range(4):
            outs[i][0:1, c * PAIR : (c + 1) * PAIR] = rows[i * 4 + c : i * 4 + c + 1]
    for c in range(16):
        outs[6][0:1, c * PAIR : (c + 1) * PAIR] = rows[24 + c : 25 + c]
    for p in range(4):

        @pl.when(code[4] == p)
        def _():
            bg[...] = rows[40 + 2 * p : 42 + 2 * p]


def finish(code, own, other, v):
    S = jax.ShapeDtypeStruct
    return pl.pallas_call(
        finish_kernel,
        in_specs=[SMEM, VM, VM, VM],
        out_specs=[VM] * 9,
        out_shape=[S((3, D, PAIR), F32), S((2, PAIR), F32)] + [S((1, D), F32)] * 6 + [S((1, FF), F32)],
        compiler_params=pltpu.CompilerParams(vmem_limit_bytes=16 << 20),
        cost_estimate=cost(1e6, 3 << 20),
    )(code, own, other, v)


def body(stream, accumulator, inward, inward_bias, outward, outward_bias, first_gain, first_shift, up_weight, up_bias,
         down_weight, down_bias, second_gain, second_shift, long_count, stream_cotangent, accumulator_cotangent):
    assert stream.shape == (ROWS, D)
    b, h = lax.axis_index("batch"), lax.axis_index("head")
    tuned = (lax.axis_size("batch"), lax.axis_size("head")) == (8, 4)
    flag = (h < long_count[0]).astype(jnp.int32)
    zero = jnp.zeros((), jnp.int32)
    if tuned:
        core, index = b & 1, {"batch": b, "head": h}
        low, other = (2 * place_code(STEPS[:3], c, index) for c in (core, 1 - core))
        across = place_code(((Y, Y),), core, index)
        code = jnp.stack([core, flag, low, other, h, across, zero, zero])
        rows = inward.reshape(3, 2, HALF, PAIR)
        bias = jnp.pad(inward_bias, ((0, 14), (0, 0)))
        wa = jnp.concatenate([lax.dynamic_index_in_dim(rows, core, 1, False).reshape(3 * HALF, PAIR), bias], 0)
        wb = jnp.concatenate([lax.dynamic_index_in_dim(rows, 1 - core, 1, False).reshape(3 * HALF, PAIR), bias], 0)
        was, wbs = [wa], [wb]
    else:
        code = jnp.stack([zero, flag] + [zero] * 6)
        was, wbs = general_gather(inward, inward_bias)

    heads = [attention_forward(code, stream, was[:1], wbs[:1])]
    if tuned:
        far, near = lax.optimization_barrier((swap(wa, (FAR, FAR)), swap(wa, (NEAR, NEAR)), heads[0][1]))[:2]
        other_far, other_near, last = swap(far, CORE), swap(near, CORE), swap(far, (NEAR, NEAR))
        heads.append(attention_forward(code, stream, [far], [other_far]))
        two = [near, after(last, heads[1][1])]
        other_two = [other_near, swap(two[1], CORE)]
        was, wbs = [wa, two[0], far, two[1]], [wb, other_two[0], other_far, other_two[1]]
    else:
        heads.append(attention_forward(code, stream, was[2:3], wbs[2:3]))
    heads.append(attention_forward(code, stream, was[1::2], wbs[1::2]))
    place_of = ((0, 0), (2, 0), (1, 0), (2, 1))
    ns, na, fg, hg, *halves, vec, vup = ffn(
        code, stream, accumulator, [t[1] for t in heads], outward, outward_bias, first_gain, first_shift, up_weight, up_bias,
        down_weight, down_bias, second_gain, second_shift, stream_cotangent, accumulator_cotangent)

    def backward(slots, x, small=None):
        t = [heads[place_of[s][0]] for s in slots]
        at = [place_of[s][1] for s in slots]
        return attention_backward(code, x, hg, slots, at, [a[0] for a in t], [a[2] for a in t], [a[1] for a in t], [a[3] for a in t], small)

    if not tuned:
        ga, ka, sa, bga = backward((0, 1), stream)
        gb, kb, sb, bgb = backward((2,), stream)
        gc, kc, sc, v = backward((3,), stream, (vec, vup, bga, bgb))
        wg, bias, dwo, dwu, dwd, rows = general_sums(jnp.concatenate(halves, 0), ((ka, sa), (kb, sb), (kc, sc)), v)
        sg = back_stream(code, fg, [ga, gb, gc], was, wbs)
        vecs, vup = [rows[i * D : (i + 1) * D] for i in range(6)], rows[6 * D : 6 * D + FF]
    else:
        keep0, keep1, send0, send1 = halves
        out = add(keep1, swap(send1, CORE))
        got0 = swap(send0, CORE)
        got = swap(out, STEPS[0])
        cur = add(keep0, got0)
        ga, ka, sa, bga = backward((0, 1), after(stream, out, cur))
        ra = swap(sa, CORE)
        cur = add(after(cur, ka), got)
        out = cur[4:]
        got = swap(out, STEPS[1])
        gb, kb, sb, bgb = backward((2,), after(stream, out))
        rb = swap(sb, CORE)
        cur = add(after(cur[:4], kb), got)
        out = cur[2:]
        got = swap(out, STEPS[2])
        gc, kc, sc, v = backward((3,), after(stream, out), (vec, vup, bga, bgb))
        rc = swap(sc, CORE)
        cur = add(after(cur[:2], kc), got)
        got = swap(cur, STEPS[3])
        k, s, v = combine(first_combine_kernel, 8 * PART, code, ka, kb, kc, ra, rb, rc, after(v, cur))
        got2 = swap(s, PAIR_STEPS[0])
        sg = back_stream(code, after(fg, s), [ga, gb, gc], was, wbs)
        cur = add(after(cur, sg), got)
        got = swap(cur, STEPS[2])
        k, s, v = combine(combine_kernel, 4 * PART, k, got2, after(v, cur))
        got2 = swap(s, PAIR_STEPS[1])
        cur = jnp.concatenate([after(cur, s), got], 0)
        got = swap(cur, STEPS[1])
        k, s, v = combine(combine_kernel, 2 * PART, k, got2, after(v, cur))
        m = merge(k, swap(s, PAIR_STEPS[2]), v)
        m = add(m, swap(m, (X, X)))
        cur = jnp.concatenate([after(cur, m), got], 0)
        got = swap(cur, STEPS[0])
        other_cur = swap(cur, CORE)
        m = after(m, cur)
        k, v = m[: 2 * PART], m[2 * PART :]
        got2 = swap(k, (Y, Y))
        mine, theirs = core * 2 + (low >> 3), (1 - core) * 2 + (other >> 3)
        wide = widen(theirs, other, other_cur, widen(mine, low, cur))
        k = jnp.concatenate([after(k, wide[0]), got2], 0)
        got2 = swap(k, CORE)
        wg, bias, *vecs, vup = finish(code, k, got2, v)
        vecs, vup = [t[0] for t in vecs], vup[0]
        got = after(got, bias)
        other_got = swap(got, CORE)
        wide = widen(mine ^ 1, low, got, wide)
        dwd, dwu, dwo = widen(theirs ^ 1, other, other_got, wide)
    return (ns, na, sg, wg, bias, dwo, vecs[0], vecs[1], vecs[2], dwu, vup, dwd, vecs[3], vecs[4], vecs[5])


def solution(mesh):
    tokens = P(("batch", "head"), None)
    in_specs = (tokens, tokens, P(None, None, "head"), P(None, "head")) + (P(),) * 10 + (P("batch"), tokens, tokens)
    out_specs = (tokens,) * 3 + (P(None, None, "head"), P(None, "head")) + (P(),) * 10
    return jax.shard_map(body, mesh=mesh, in_specs=in_specs, out_specs=out_specs, check_vma=False)
```

```python
import math

import jax
import jax.numpy as jnp
from jax import lax
from jax.experimental import pallas as pl
from jax.experimental.pallas import tpu as pltpu
from jax.sharding import PartitionSpec as P

F32, BF = jnp.float32, jnp.bfloat16
ROWS, D, FF, PAIR, HD, SHORT = 1024, 512, 2048, 128, 64, 256
QB = 256
SCALE = 1.0 / math.sqrt(HD)


def dot(a, b):
    return lax.dot_general(a, b, (((1,), (0,)), ((), ())), preferred_element_type=F32)


def dot_nt(a, b):
    return lax.dot_general(a, b, (((1,), (1,)), ((), ())), preferred_element_type=F32)


def dot_tn(a, b):
    return lax.dot_general(a, b, (((0,), (0,)), ((), ())), preferred_element_type=F32)


def params(n=1, mib=60):
    return pltpu.CompilerParams(dimension_semantics=("arbitrary",) * n or None, vmem_limit_bytes=mib << 20)


def cost(flops, nbytes):
    return pl.CostEstimate(flops=int(flops), bytes_accessed=int(nbytes), transcendentals=0)


SMEM = pl.BlockSpec(memory_space=pltpu.SMEM)
VM = pl.BlockSpec(memory_space=pltpu.VMEM)
HBM = pl.BlockSpec(memory_space=pltpu.HBM)


def whole(shape):
    return pl.BlockSpec(shape, lambda *_: (0,) * len(shape))


HALF = D // 2
PACK = 3 * HALF + 16


def side(w):
    return jnp.concatenate([w[c * HALF : (c + 1) * HALF] for c in range(3)], axis=1)


def fwd_kernel(n_pairs, code, x, *refs):
    was, wbs = refs[:n_pairs], refs[n_pairs : 2 * n_pairs]
    e, o, qkv, rl, es, qs_, va, sems, qsems = refs[2 * n_pairs :]
    ca = pl.multiple_of(code[0] * HALF, HALF)
    cb = pl.multiple_of(HALF - code[0] * HALF, HALF)
    lane = lax.broadcasted_iota(jnp.int32, (1, PAIR), 1)

    def run(short):
        copies = []

        def project(a):
            wa, wb = was[a], wbs[a]
            p = dot(x[:, pl.ds(ca, HALF)], side(wa)) + dot(x[:, pl.ds(cb, HALF)], side(wb))
            bq, bv = wa[3 * HALF : 3 * HALF + 1].astype(F32), wa[3 * HALF + 1 : 3 * HALF + 2].astype(F32)
            q = ((p[:, :PAIR] + bq).astype(BF).astype(F32) * SCALE).astype(BF)
            k = p[:, PAIR : 2 * PAIR].astype(BF)
            v = (p[:, 2 * PAIR :] + bv).astype(BF)
            qs_[a, :, :PAIR] = q
            qs_[a, :, PAIR : 2 * PAIR] = k
            qs_[a, :, 2 * PAIR :] = v
            copies.append(pltpu.make_async_copy(qs_.at[a], qkv.at[a], qsems.at[a]))
            copies[-1].start()
            return q, k, [jnp.where((lane < HD) == (h == 0), v, jnp.ones((), BF)) for h in range(2)]

        if short:
            for a in range(n_pairs):
                for h, v in enumerate(project(a)[2]):
                    va[a, h] = v

            def block(i, carry):
                a, t = i // (ROWS // SHORT), i % (ROWS // SHORT)
                rows = pl.ds(pl.multiple_of(t * SHORT, SHORT), SHORT)
                q, k = qs_[a, rows, :PAIR], qs_[a, rows, PAIR : 2 * PAIR]
                outs = []
                for h in range(2):
                    sc = dot_nt(jnp.where((lane < HD) == (h == 0), q, jnp.zeros((), BF)), k)
                    ex = jnp.exp(sc - jnp.max(sc, axis=1, keepdims=True)).astype(BF)
                    es[a, h, rows, 0:SHORT] = ex
                    u = dot(ex, va[a, h, rows, :])
                    r = 1.0 / pltpu.roll(u, HD, 1)
                    outs.append((u * r, r))
                o[a, rows, :] = jnp.where(lane < HD, outs[0][0], outs[1][0]).astype(BF)
                rl[a, rows, :] = jnp.where(lane < HD, outs[0][1], outs[1][1])
                return carry

            lax.fori_loop(0, n_pairs * (ROWS // SHORT), block, 0)
            at = (slice(None), slice(None), slice(None), pl.ds(0, SHORT))
            copies.append(pltpu.make_async_copy(es.at[at], e.at[at], sems.at[0]))
            copies[-1].start()
            for c in copies:
                c.wait()
            return

        ready = {0: project(0)}

        def score(item):
            a, qb, h = item
            q, k, _ = ready[a]
            qh = jnp.where((lane < HD) == (h == 0), q[qb * QB : (qb + 1) * QB], jnp.zeros((), BF))
            return dot_nt(qh, k)

        done = {}

        def product(item, ex):
            a, qb, h = item
            qs = slice(qb * QB, (qb + 1) * QB)
            u = dot(ex, ready[a][2][h])
            r = 1.0 / pltpu.roll(u, HD, 1)
            done[h] = (u * r, r)
            if h == 1:
                o[a, qs, :] = jnp.where(lane < HD, done[0][0], done[1][0]).astype(BF)
                rl[a, qs, :] = jnp.where(lane < HD, done[0][1], done[1][1])

        items = [(a, qb, h) for a in range(n_pairs) for qb in range(ROWS // QB) for h in range(2)]
        ahead, last = score(items[0]), None
        for i, item in enumerate(items):
            s = ahead
            if i + 1 < len(items):
                if items[i + 1][0] not in ready:
                    ready[items[i + 1][0]] = project(items[i + 1][0])
                ahead = score(items[i + 1])
            ex = jnp.exp(s - jnp.max(s, axis=1, keepdims=True)).astype(BF)
            a, qb, h = item
            at = (a, h, pl.ds(qb * QB, QB))
            es[at] = ex
            copies.append(pltpu.make_async_copy(es.at[at], e.at[at], sems.at[i]))
            copies[-1].start()
            if last is not None:
                product(*last)
            last = (item, ex)
        product(*last)
        for c in copies:
            c.wait()

    pl.when(code[1] == 1)(lambda: run(False))
    pl.when(code[1] == 0)(lambda: run(True))


def attention_forward(code, x, was, wbs):
    S, n = jax.ShapeDtypeStruct, len(was)
    return pl.pallas_call(
        lambda *refs: fwd_kernel(n, *refs),
        in_specs=[SMEM, VM] + [VM] * (2 * n),
        out_specs=[HBM, VM, HBM, VM],
        out_shape=[S((n, 2, ROWS, ROWS), BF), S((n, ROWS, PAIR), BF), S((n, ROWS, 3 * PAIR), BF), S((n, ROWS, PAIR), F32)],
        scratch_shapes=[pltpu.VMEM((n, 2, ROWS, ROWS), BF), pltpu.VMEM((n, ROWS, 3 * PAIR), BF), pltpu.VMEM((n, 2, ROWS, PAIR), BF),
                        pltpu.SemaphoreType.DMA((8 * n,)), pltpu.SemaphoreType.DMA((n,))],
        compiler_params=params(0),
        cost_estimate=cost(1e6, 1 << 10),
    )(code, x, *was, *wbs)


PART, VROWS = 192, 64


def bwd_kernel(slots, at_o, last, code, x_, hg_, *refs):
    n = len(slots)
    es_, qkvs_, os_, rls_ = (refs[k * n : (k + 1) * n] for k in range(4))
    refs = refs[4 * n :]
    if last:
        (vec, vup, *bg_ins), refs = refs[:4], refs[4:]
        g_, keep, send, v_out, x, e, qkv, o, do, rl, ds, g, gsum, vrow, sva, sda, skm, sqt, sdt, sems, gsems = refs
    else:
        g_, keep, send, bg_out, x, e, qkv, o, do, rl, ds, g, gsum, vrow, sva, sda, skm, sqt, sdt, sems, gsems = refs
    lane = lax.broadcasted_iota(jnp.int32, (1, PAIR), 1)
    first, zero, one = lane < HD, jnp.zeros((), BF), jnp.ones((), BF)
    row = lax.broadcasted_iota(jnp.int32, (PAIR, PAIR), 0)
    col = lax.broadcasted_iota(jnp.int32, (PAIR, PAIR), 1)
    pick = jnp.where(((row < HD) != (col < HD)) & ((col & (HD - 1)) < 2), 1.0, 0.0).astype(BF)
    hs = [slice(h * HD, (h + 1) * HD) for h in range(2)]
    tile = 512
    items = [(t, h) for t in range(ROWS // tile) for h in range(2)]

    def small_loads(a):
        pairs = ((hg_.at[:, pl.ds(slots[a] * PAIR, PAIR)], do), (rls_[a].at[at_o[a]], rl), (os_[a].at[at_o[a]], o), (qkvs_[a].at[at_o[a]], qkv))
        return [pltpu.make_async_copy(src, dst.at[a], sems.at[8 * a + k]) for k, (src, dst) in enumerate(pairs)]

    def e_load(a, i):
        t, h = items[i]
        at = (h, pl.ds(t * tile, tile))
        return pltpu.make_async_copy(es_[a].at[(at_o[a], *at)], e.at[(a, *at)], sems.at[8 * a + 4 + i])

    def e_load_short(a):
        at = (slice(None), slice(None), pl.ds(0, SHORT))
        return pltpu.make_async_copy(es_[a].at[(at_o[a], *at)], e.at[(a, *at)], sems.at[8 * a + 4])

    def store_g(a):
        return pltpu.make_async_copy(g.at[a], g_.at[a], gsems.at[a])

    x_load = pltpu.make_async_copy(x_, x, sems.at[8 * n])

    def prepare(a):
        dof = do[a].astype(F32) * rl[a]
        dob = dof.astype(BF)
        t = dof * o[a].astype(F32)
        th = t.astype(BF)
        tl = (t - th.astype(F32)).astype(BF)
        delta = -(dot(th, pick) + dot(tl, pick))
        dh = delta.astype(BF)
        dd = jnp.where((lane & (HD - 1)) == 0, dh, (delta - dh.astype(F32)).astype(BF))
        q, k, v = qkv[a, :, :PAIR], qkv[a, :, PAIR : 2 * PAIR], qkv[a, :, 2 * PAIR :]
        own = [first == (h == 0) for h in range(2)]
        aug = [jnp.logical_not(own[h]) & ((lane & (HD - 1)) < 2) for h in range(2)]
        va = [jnp.where(own[h], v, jnp.where(aug[h], one, zero)) for h in range(2)]
        da = [jnp.where(own[h], dob, jnp.where(aug[h], dd, zero)) for h in range(2)]
        km = [jnp.where(own[h], k, zero) for h in range(2)]
        return va, da, km, q.astype(F32).T.astype(BF), dof.T.astype(BF)

    def project_back(a):
        gr = dot_tn(x[...], g[a])
        for c in range(3):
            gsum[a, c * D : (c + 1) * D, :] = gr[:, c * PAIR : (c + 1) * PAIR].astype(BF)

    def long():
        for a in range(n):
            for c in small_loads(a) + [e_load(a, i) for i in range(4)]:
                c.start()
        x_load.start()
        for a in range(n):
            for c in small_loads(a):
                c.wait()
            va, da, km, qt, dt = prepare(a)

            def weights(item):
                t, h = item
                return dot_nt(da[h][t * tile : (t + 1) * tile], va[h])

            ahead = weights(items[0])
            for i, item in enumerate(items):
                dp = ahead
                if i + 1 < len(items):
                    ahead = weights(items[i + 1])
                t, h = item
                rows = slice(t * tile, (t + 1) * tile)
                e_load(a, i).wait()
                ds[a, h, rows, :] = e[a, h, rows, :] * dp.astype(BF)
            dq = dot(ds[a, 0], km[0]) + dot(ds[a, 1], km[1])
            g[a, :, :PAIR] = (dq * SCALE).astype(BF)
            vt = [dot(dt[hs[h]], e[a, h]) for h in range(2)]
            kt = [dot(qt[hs[h]], ds[a, h]) for h in range(2)]
            g[a, :, 2 * PAIR :] = jnp.concatenate(vt, 0).T.astype(BF)
            g[a, :, PAIR : 2 * PAIR] = jnp.concatenate(kt, 0).T.astype(BF)
            store_g(a).start()
            if a == 0:
                x_load.wait()
            project_back(a)

    def short():
        for a in range(n):
            for c in small_loads(a) + [e_load_short(a)]:
                c.start()
        x_load.start()
        for a in range(n):
            for c in small_loads(a) + [e_load_short(a)]:
                c.wait()
        x_load.wait()

        def pair(a, carry):
            va, da, km, qt, dt = prepare(a)
            for h in range(2):
                sva[h], sda[h], skm[h] = va[h], da[h], km[h]
            sqt[...] = qt
            sdt[...] = dt

            def block(t, carry):
                rows = pl.ds(pl.multiple_of(t * SHORT, SHORT), SHORT)
                dq, vt, kt = 0.0, [], []
                for h in range(2):
                    ex = e[a, h, rows, 0:SHORT]
                    d = ex * dot_nt(sda[h, rows, :], sva[h, rows, :]).astype(BF)
                    dq = dq + dot(d, skm[h, rows, :])
                    vt.append(dot(sdt[hs[h], rows], ex))
                    kt.append(dot(sqt[hs[h], rows], d))
                g[a, rows, :PAIR] = (dq * SCALE).astype(BF)
                g[a, rows, 2 * PAIR :] = jnp.concatenate(vt, 0).T.astype(BF)
                g[a, rows, PAIR : 2 * PAIR] = jnp.concatenate(kt, 0).T.astype(BF)
                return carry

            lax.fori_loop(0, ROWS // SHORT, block, 0)
            store_g(a).start()
            project_back(a)
            return carry

        lax.fori_loop(0, n, pair, 0)

    pl.when(code[1] == 1)(long)
    pl.when(code[1] == 0)(short)

    def put(i, carry):
        a, j = i // 8, i % 8
        block = gsum[a, pl.ds(pl.multiple_of(j * PART, PART), PART), :]
        rel = (j % 4) ^ code[5]
        if n == 2:
            at = (rel & 1) + jnp.where(j // 4 == 0, (rel >> 1) * 4 + a * 2, (rel >> 1) * 2 + a * 4)
        else:
            at = rel
        rows = pl.ds(pl.multiple_of(at * PART, PART), PART)

        @pl.when(code[0] == j // 4)
        def _():
            keep[rows, :] = block

        @pl.when(code[0] != j // 4)
        def _():
            send[rows, :] = block

        return carry

    lax.fori_loop(0, 8 * n, put, 0)
    for a in range(n):
        store_g(a).wait()
    bgs = [jnp.concatenate([colsum(g[a, :, :PAIR].astype(F32)), colsum(g[a, :, 2 * PAIR :].astype(F32))], 0) for a in range(n)]
    if not last:
        bg_out[...] = jnp.concatenate(bgs + [jnp.zeros((8 - 2 * n, PAIR), F32)], 0)
        return
    for i in range(6):
        for c in range(4):
            vrow[i * 4 + c : i * 4 + c + 1, :] = vec[i : i + 1, c * PAIR : (c + 1) * PAIR]
    for c in range(16):
        vrow[24 + c : 25 + c, :] = vup[0:1, c * PAIR : (c + 1) * PAIR]
    known = [bg_ins[0][0:2], bg_ins[0][2:4], bg_ins[1][0:2]] + bgs
    for p in range(4):
        vrow[40 + 2 * p : 42 + 2 * p, :] = sum(jnp.where((code[4] ^ s) == p, b, 0.0) for s, b in enumerate(known))
    vrow[48:, :] = jnp.zeros((VROWS - 48, PAIR), F32)
    v_out[...] = vrow[...].astype(BF)
    send[4 * n * PART :, :] = v_out[...]


def attention_backward(code, x, hg, slots, at_o, es, qkvs, os, rls, small=None):
    S, n, last = jax.ShapeDtypeStruct, len(slots), small is not None
    ins = [code, x, hg, *es, *qkvs, *os, *rls] + list(small or ())
    rows = 4 * n * PART
    outs = [S((n, ROWS, 3 * PAIR), BF), S((rows, PAIR), BF), S((rows + VROWS * last, PAIR), BF), S((VROWS, PAIR), BF) if last else S((8, PAIR), F32)]
    scratch = [((ROWS, D), BF), ((n, 2, ROWS, ROWS), BF), ((n, ROWS, 3 * PAIR), BF), ((n, ROWS, PAIR), BF), ((n, ROWS, PAIR), BF),
               ((n, ROWS, PAIR), F32), ((n, 2, ROWS, ROWS), BF), ((n, ROWS, 3 * PAIR), BF), ((n, 3 * D, PAIR), BF), ((VROWS, PAIR), F32)]
    scratch += [((2, ROWS, PAIR), BF)] * 3 + [((PAIR, ROWS), BF)] * 2
    return pl.pallas_call(
        lambda *refs: bwd_kernel(slots, at_o, last, *refs),
        in_specs=[SMEM] + [HBM] * (2 + 4 * n) + [VM] * (4 * last),
        out_specs=[HBM, VM, VM, VM],
        out_shape=outs,
        scratch_shapes=[pltpu.VMEM(*a) for a in scratch] + [pltpu.SemaphoreType.DMA((8 * n + 1,)), pltpu.SemaphoreType.DMA((n,))],
        compiler_params=params(0, 44),
        cost_estimate=cost(n * 8e9, n * 8 << 20),
    )(*ins)


def gelu_parts(u):
    cdf = 0.5 + 0.5 * lax.erf(u * math.sqrt(0.5))
    density = jnp.exp2(u * u * (-0.5 * math.log2(math.e))) * (1.0 / math.sqrt(2.0 * math.pi))
    return u * cdf, cdf + u * density


def norm_parts(h):
    m = jnp.mean(h, -1, keepdims=True)
    c = h - m
    r = lax.rsqrt(jnp.mean(c * c, -1, keepdims=True) + 1e-5)
    return c * r, r


def norm_back(e, gain, z, r):
    eg = e * gain
    return r * (eg - jnp.mean(eg, -1, keepdims=True) - z * jnp.mean(eg * z, -1, keepdims=True))


def colsum(a):
    return jnp.sum(a, 0, keepdims=True)


BLOCKS, BLOCK = 16, 144


def place(block, size, base, first, half, code, out):
    low = code[2 + half]
    for s in range(block.shape[0] // size):
        out[(first + s) ^ low, base : base + size, :] = block[s * size : (s + 1) * size].astype(BF)


def ffn_kernel(code, x_, acc_, oa_, ob_, oc_, wo, bo, g1, s1, wu_, bu, wd_, bd, g2, s2, sc_, ac_,
               ns_, na_, fg_, hg_, keep0, keep1, send0, send1, vec, vup,
               x, acc, oa, ob, oc, od, sc, ac, wu, wd, ns, na, fg, hg, keep, send, wp, hid, bfull, lfull, pfull, ofull, afull, isem, osem):
    tiles = [slice(t * QB, (t + 1) * QB) for t in range(ROWS // QB)]
    loads, stores = {}, []

    def load(name, src, dst, t=None):
        at = pl.ds(t * QB, QB) if t is not None else pl.ds(0, src.shape[0])
        loads[name, t] = pltpu.make_async_copy(src.at[at], dst.at[at], isem.at[len(loads)])
        loads[name, t].start()

    def store(src, dst, *at):
        stores.append(pltpu.make_async_copy(src.at[at], dst.at[at], osem.at[len(stores)]))
        stores[-1].start()

    by_tile = (("oa", oa_.at[0], oa), ("ob", ob_.at[0], ob), ("oc", oc_.at[0], oc), ("od", oc_.at[1], od), ("x", x_, x), ("acc", acc_, acc), ("sc", sc_, sc), ("ac", ac_, ac))
    for t in (0, 1):
        for name, src, dst in by_tile[:5]:
            load(name, src, dst, t)
    load("wu", wu_, wu)
    load("wd", wd_, wd)
    for name, src, dst in by_tile[5:]:
        for t in (0, 1):
            load(name, src, dst, t)
    for t in (2, 3):
        for name, src, dst in by_tile:
            load(name, src, dst, t)

    for s in range(D // PAIR):
        at = pl.multiple_of((code[4] ^ s) * PAIR, PAIR)
        wp[s * PAIR : (s + 1) * PAIR, :] = wo[pl.ds(at, PAIR), :]

    def wait(t, *names):
        for name in names:
            loads[name, t].wait()

    sums, up_sum = [0.0] * 6, 0.0
    for group in ((0, 1), (2, 3)):
        att, z1, r1, first, hidden, slope, si, bgs, pgs, ags = {}, {}, {}, {}, {}, {}, {}, {}, {}, {}
        for t in group:
            wait(t, "oa", "ob", "oc", "od")
            ofull[tiles[t], :] = jnp.concatenate([oa[tiles[t]], ob[tiles[t]], oc[tiles[t]], od[tiles[t]]], axis=1)
            att[t] = dot(ofull[tiles[t], :], wp[...]) + bo[...]
        for t in group:
            wait(t, "x")
            z1[t], r1[t] = norm_parts(x[tiles[t]].astype(F32) + att[t])
            first[t] = z1[t] * g1[...] + s1[...]
            lfull[tiles[t], :] = first[t].astype(BF)
        if group[0] == 0:
            wait(None, "wu")
        ups = {t: dot(first[t].astype(BF), wu[...]) for t in group}
        for t in group:
            a, slope[t] = gelu_parts(ups[t] + bu[...])
            hidden[t] = a.astype(BF)
            hid[tiles[t], :] = hidden[t]
        if group[0] == 0:
            wait(None, "wd")
        branch = {t: dot(hidden[t], wd[...]) + bd[...] for t in group}
        for t in group:
            wait(t, "acc", "sc", "ac")
            na[tiles[t]] = acc[tiles[t]] + att[t] + branch[t]
            store(na, na_, pl.ds(t * QB, QB))
            z2, r2 = norm_parts(first[t] + branch[t])
            ns[tiles[t]] = (z2 * g2[...] + s2[...]).astype(BF)
            store(ns, ns_, pl.ds(t * QB, QB))
            e2 = sc[tiles[t]]
            si[t] = norm_back(e2, g2[...], z2, r2)
            bgs[t] = (si[t] + ac[tiles[t]]).astype(BF)
            bfull[tiles[t], :] = bgs[t]
            sums[3:] = [a + colsum(b) for a, b in zip(sums[3:], (bgs[t].astype(F32), e2 * z2, e2))]
        hgs = {t: dot_nt(bgs[t], wd[...]) for t in group}
        for t in group:
            pgs[t] = (hgs[t] * slope[t]).astype(BF)
            pfull[tiles[t], :] = pgs[t]
            up_sum += colsum(pgs[t].astype(F32))
        es = {t: dot_nt(pgs[t], wu[...]) for t in group}
        for t in group:
            e1 = es[t] + si[t]
            fi = norm_back(e1, g1[...], z1[t], r1[t])
            fg[tiles[t]] = fi
            store(fg, fg_, pl.ds(t * QB, QB))
            ags[t] = (fi + ac[tiles[t]]).astype(BF)
            afull[tiles[t], :] = ags[t]
            sums[:3] = [a + colsum(b) for a, b in zip(sums[:3], (ags[t].astype(F32), e1 * z1[t], e1))]
        for t in group:
            hg[tiles[t]] = dot_nt(ags[t], wp[...]).astype(BF)
            store(hg, hg_, pl.ds(t * QB, QB))
    for j, s in enumerate(sums):
        vec[j : j + 1, :] = s
    vec[6:8, :] = jnp.zeros((2, D), F32)
    vup[0:1, :] = up_sum
    quarter = BLOCKS // 2
    for half, out, dsts in ((1, send, (send0, send1)), (0, keep, (keep0, keep1))):

        def ship(base, size):
            for k in (1, 0):
                src = out.at[pl.ds(k * quarter, quarter), pl.ds(base, size)]
                stores.append(pltpu.make_async_copy(src, dsts[k].at[:, pl.ds(base, size)], osem.at[len(stores)]))
                stores[-1].start()

        mine = code[0] ^ half
        for b in range(4):
            at = pl.multiple_of(mine * 1024 + b * 256, 256)
            place(dot_tn(hid[:, pl.ds(at, 256)], bfull[...]), 64, 0, b * 4, half, code, out)
        ship(0, 64)
        for c in range(2):
            at = pl.multiple_of(mine * 1024 + c * 512, 512)
            place(dot_tn(lfull[...], pfull[:, pl.ds(at, 512)]), 64, 64, c * 8, half, code, out)
        ship(64, 64)
        for p in range(2):
            at = pl.multiple_of(((mine * 2 + p) ^ code[4]) * PAIR, PAIR)
            place(dot_tn(ofull[:, pl.ds(at, PAIR)], afull[...]), 16, 128, p * 8, half, code, out)
        ship(128, 16)
    for c in stores:
        c.wait()


def ffn(code, x, acc, os, wo, bo, g1, s1, wu, bu, wd, bd, g2, s2, sc, ac):
    S = jax.ShapeDtypeStruct
    bo, g1, s1, bu, bd, g2, s2 = (v.reshape(1, -1) for v in (bo, g1, s1, bu, bd, g2, s2))
    ins = (code, x, acc, *os, wo, bo, g1, s1, wu, bu, wd, bd, g2, s2, sc, ac)
    specs = [SMEM] + [HBM] * 5 + [VM] * 4 + [HBM, VM, HBM] + [VM] * 3 + [HBM] * 2
    outs = [S((ROWS, D), BF), S((ROWS, D), F32), S((ROWS, D), F32), S((ROWS, D), BF)]
    outs += [S((BLOCKS // 2, BLOCK, D), BF)] * 4 + [S((8, D), F32), S((1, FF), F32)]
    buffers = [x, acc] + [S((ROWS, PAIR), BF)] * 4 + [sc, ac, wu, wd] + outs[:4] + [S((BLOCKS, BLOCK, D), BF)] * 2
    scratch = [pltpu.VMEM(a.shape, a.dtype) for a in buffers]
    scratch += [pltpu.VMEM(s, BF) for s in ((D, D), (ROWS, FF), (ROWS, D), (ROWS, D), (ROWS, FF), (ROWS, D), (ROWS, D))]
    return pl.pallas_call(
        ffn_kernel,
        in_specs=specs,
        out_specs=[HBM] * 8 + [VM] * 2,
        out_shape=outs,
        scratch_shapes=scratch + [pltpu.SemaphoreType.DMA((34,)), pltpu.SemaphoreType.DMA((28,))],
        compiler_params=params(0),
        cost_estimate=cost(25e9, 20 << 20),
    )(*ins)


def back_stream_kernel(code, fg, ga, gb, gc, *refs):
    was, wbs, out = refs[:4], refs[4:8], refs[8]
    ca = pl.multiple_of(code[0] * HALF, HALF)
    cb = pl.multiple_of(HALF - code[0] * HALF, HALF)
    for at, ws in ((ca, was), (cb, wbs)):
        t = fg[:, pl.ds(at, HALF)]
        for s, w in enumerate(ws):
            t = t + dot_nt((ga[0], ga[1], gb[0], gc[0])[s], side(w))
        out[:, pl.ds(at, HALF)] = t


def back_stream(code, fg, gs, was, wbs):
    return pl.pallas_call(
        back_stream_kernel,
        grid=(ROWS // QB,),
        in_specs=[SMEM, pl.BlockSpec((QB, D), lambda i: (i, 0))] + [pl.BlockSpec((g.shape[0], QB, 3 * PAIR), lambda i: (0, i, 0)) for g in gs] + [whole((PACK, PAIR))] * 8,
        out_specs=pl.BlockSpec((QB, D), lambda i: (i, 0)),
        out_shape=jax.ShapeDtypeStruct((ROWS, D), F32),
        compiler_params=params(1, 56),
        cost_estimate=cost(4e9, 8 << 20),
    )(code, fg, *gs, *was, *wbs)


def general_gather(inward, inward_bias):
    full = lax.all_gather(inward, "head", axis=2, tiled=True)
    bias = lax.all_gather(inward_bias, "head", axis=1, tiled=True)
    was, wbs = [], []
    for p in range(D // PAIR):
        cols = slice(p * PAIR, (p + 1) * PAIR)
        tail = jnp.pad(bias[:, cols], ((0, 14), (0, 0)))
        was.append(jnp.concatenate([full[:, :HALF, cols].reshape(3 * HALF, PAIR), tail], 0))
        wbs.append(jnp.concatenate([full[:, HALF:, cols].reshape(3 * HALF, PAIR), tail], 0))
    return was, wbs


def general_sums(blocks, pair_parts, vectors):
    both = ("batch", "head")
    whole_half, vectors = lax.psum((blocks, vectors), both)
    wide = whole_half.astype(F32)
    dwd = wide[:, :64].reshape(FF, D)
    dwu = wide[:, 64:128].reshape(4, D, D).transpose(1, 0, 2).reshape(D, FF)
    dwo = wide[:, 128:].reshape(D, D)
    wg = []
    for k, n in pair_parts:
        if k.shape[0] == 8 * PART:
            k, n = k.reshape(2, 2, 2, PART, PAIR).swapaxes(0, 1), n.reshape(2, 2, 2, PART, PAIR)
        else:
            k, n = k.reshape(1, 2, 2, PART, PAIR), n[: 4 * PART].reshape(1, 2, 2, PART, PAIR)
        wg += [jnp.concatenate([t[a].reshape(4 * PART, PAIR) for t in (k, n)], 0).reshape(3, D, PAIR) for a in range(k.shape[0])]
    wg = lax.psum(lax.psum_scatter(jnp.concatenate(wg, 2), "head", scatter_dimension=2, tiled=True), "batch")
    rows = vectors[:48].astype(F32).reshape(-1)
    bias = rows[5120:].reshape(D // PAIR, 2, PAIR).transpose(1, 0, 2).reshape(2, D)
    width = D // lax.axis_size("head")
    bias = lax.dynamic_slice_in_dim(bias, lax.axis_index("head") * width, width, 1)
    return wg.astype(F32), bias, dwo, dwu, dwd, rows


def swap(x, masks):
    n_batch, n_head = lax.axis_size("batch"), lax.axis_size("head")
    pairs = []
    for b in range(n_batch):
        for h in range(n_head):
            axis, mask = masks[b & 1]
            to = (b ^ mask, h) if axis == "batch" else (b, h ^ mask)
            pairs.append((b * n_head + h, to[0] * n_head + to[1]))
    return lax.ppermute(x, ("batch", "head"), pairs)


CORE = (("batch", 1), ("batch", 1))
X, Y, NEAR, FAR = ("batch", 2), ("batch", 4), ("head", 1), ("head", 2)
STEPS = ((X, NEAR), (NEAR, X), (Y, FAR), (FAR, Y))
PAIR_STEPS = ((X, NEAR), (NEAR, X), (FAR, FAR))


def place_code(steps, core, index):
    code = 0
    for masks in steps:
        bits = []
        for axis, mask in masks:
            bits.append(((index[axis] & mask) > 0).astype(jnp.int32))
        code = code * 2 + jnp.where(core == 0, bits[0], bits[1])
    return code


def add(a, b):
    return (a.astype(F32) + b.astype(F32)).astype(BF)


def after(x, *others):
    return lax.optimization_barrier((x, *others))[0]


def split_sum(total, to, keep, send):
    half = keep.shape[0]
    if to < half:
        keep[to : to + total.shape[0], :] = total
    else:
        send[to - half : to - half + total.shape[0], :] = total


def first_combine_kernel(code, ka, kb, kc, ra, rb, rc, v, keep, send, v_out):
    def place_at(q, far):
        return ((q >> 1) * 4 + far * 2 + (q & 1)) * PART

    for q in range(8):
        rows = slice(q * PART, (q + 1) * PART)
        split_sum(add(ka[rows, :], ra[rows, :]), place_at(q, 0), keep, send)
    for core in range(2):

        @pl.when(code[0] == core)
        def _():
            for k, r, near in ((kb, rb, 0), (kc, rc, 1)):
                for p in range(4):
                    rows = slice(p * PART, (p + 1) * PART)
                    q = (p & 1) + ((p >> 1) * 4 + near * 2 if core == 0 else (p >> 1) * 2 + near * 4)
                    split_sum(add(k[rows, :], r[rows, :]), place_at(q, 1), keep, send)

    v_out[...] = add(v[...], rc[-VROWS:, :])
    send[keep.shape[0] :, :] = v_out[...]


def combine_kernel(k, r, v, keep, send, v_out):
    half = keep.shape[0]
    for to in (0, half):
        split_sum(add(k[to : to + half, :], r[to : to + half, :]), to, keep, send)
    v_out[...] = add(v[...], r[-VROWS:, :])
    send[half:, :] = v_out[...]


def merge_kernel(k, r, v, out):
    n = k.shape[0]
    out[:n, :] = add(k[...], r[:n, :])
    out[n:, :] = add(v[...], r[n:, :])


def merge(k, r, v):
    return pl.pallas_call(
        merge_kernel,
        in_specs=[VM] * 3,
        out_specs=VM,
        out_shape=jax.ShapeDtypeStruct(r.shape, BF),
        compiler_params=pltpu.CompilerParams(vmem_limit_bytes=16 << 20),
        cost_estimate=cost(1e6, 1 << 18),
    )(k, r, v)


def combine(kernel, half, *args):
    S = jax.ShapeDtypeStruct
    return pl.pallas_call(
        kernel,
        in_specs=[SMEM] * (len(args) - 3 > 3) + [VM] * (len(args) - (len(args) - 3 > 3)),
        out_specs=[VM] * 3,
        out_shape=[S((half, PAIR), BF), S((half + VROWS, PAIR), BF), S((VROWS, PAIR), BF)],
        compiler_params=pltpu.CompilerParams(vmem_limit_bytes=16 << 20),
        cost_estimate=cost(1e6, 2 << 20),
    )(*args)


def widen_kernel(code, src, *refs):
    dwd, dwu, dwo = refs[-3:]
    for s in range(4):
        at = (pl.program_id(0) * 4 + s) ^ (code[1] & 7)
        dwd[s * 64 : (s + 1) * 64, :] = src[at, 0:64].astype(F32)
        dwu[s * 64 : (s + 1) * 64, :] = src[at, 64:128].astype(F32)
        dwo[s * 16 : (s + 1) * 16, :] = src[at, 128:144].astype(F32)


def widen(quarter, low, src, before=()):
    S = jax.ShapeDtypeStruct
    spec = pltpu.PrefetchScalarGridSpec(
        num_scalar_prefetch=1,
        grid=(2,),
        in_specs=[VM] + [HBM] * len(before),
        out_specs=[
            pl.BlockSpec((256, D), lambda i, c: (c[0] * 2 + i, 0)),
            pl.BlockSpec((256, D), lambda i, c: (i, c[0])),
            pl.BlockSpec((64, D), lambda i, c: (c[0] * 2 + i, 0)),
        ],
    )
    return pl.pallas_call(
        widen_kernel,
        grid_spec=spec,
        out_shape=[S((FF, D), F32), S((D, FF), F32), S((D, D), F32)],
        input_output_aliases={2 + k: k for k in range(len(before))},
        compiler_params=params(1, 16),
        cost_estimate=cost(1e6, 4 << 20),
    )(jnp.stack([quarter, low]), src, *before)


def finish_kernel(code, own, other, v, wg, bg, *outs):
    for j in range(8):
        rel = (j % 4) ^ code[5]
        at = pl.multiple_of(rel * PART, PART)

        def put(src, j=j, at=at):
            block = src[pl.ds(at, PART), :].astype(F32)
            for r in range(0, PART, 64):
                to = j * PART + r
                wg[to // D, to % D : to % D + 64] = block[r : r + 64]

        pl.when(code[0] == j // 4)(lambda: put(own))
        pl.when(code[0] != j // 4)(lambda: put(other))

    rows = v[2 * PART :, :].astype(F32)
    for i in range(6):
        for c in range(4):
            outs[i][0:1, c * PAIR : (c + 1) * PAIR] = rows[i * 4 + c : i * 4 + c + 1]
    for c in range(16):
        outs[6][0:1, c * PAIR : (c + 1) * PAIR] = rows[24 + c : 25 + c]
    for p in range(4):

        @pl.when(code[4] == p)
        def _():
            bg[...] = rows[40 + 2 * p : 42 + 2 * p]


def finish(code, own, other, v):
    S = jax.ShapeDtypeStruct
    return pl.pallas_call(
        finish_kernel,
        in_specs=[SMEM, VM, VM, VM],
        out_specs=[VM] * 9,
        out_shape=[S((3, D, PAIR), F32), S((2, PAIR), F32)] + [S((1, D), F32)] * 6 + [S((1, FF), F32)],
        compiler_params=pltpu.CompilerParams(vmem_limit_bytes=16 << 20),
        cost_estimate=cost(1e6, 3 << 20),
    )(code, own, other, v)


def body(stream, accumulator, inward, inward_bias, outward, outward_bias, first_gain, first_shift, up_weight, up_bias,
         down_weight, down_bias, second_gain, second_shift, long_count, stream_cotangent, accumulator_cotangent):
    assert stream.shape == (ROWS, D)
    b, h = lax.axis_index("batch"), lax.axis_index("head")
    tuned = (lax.axis_size("batch"), lax.axis_size("head")) == (8, 4)
    flag = (h < long_count[0]).astype(jnp.int32)
    zero = jnp.zeros((), jnp.int32)
    if tuned:
        core, index = b & 1, {"batch": b, "head": h}
        low, other = (2 * place_code(STEPS[:3], c, index) for c in (core, 1 - core))
        across = 2 * place_code(((X, X),), core, index)
        code = jnp.stack([core, flag, low, other, h, across, zero, zero])
        bias = jnp.pad(inward_bias, ((0, 14), (0, 0)))
        packs = [jnp.concatenate([inward[0, r], inward[1, r], inward[2, r], bias], 0) for r in (slice(0, HALF), slice(HALF, D))]
        wa, wb = jnp.where(core == 0, packs[0], packs[1]), jnp.where(core == 0, packs[1], packs[0])
        was, wbs = [wa], [wb]
    else:
        code = jnp.stack([zero, flag] + [zero] * 6)
        was, wbs = general_gather(inward, inward_bias)

    heads = [attention_forward(code, stream, was[:1], wbs[:1])]
    if tuned:
        far, near = lax.optimization_barrier((swap(wa, (FAR, FAR)), swap(wa, (NEAR, NEAR)), heads[0][1]))[:2]
        other_far, other_near, last = swap(far, CORE), swap(near, CORE), swap(far, (NEAR, NEAR))
        heads.append(attention_forward(code, stream, [near], [other_near]))
        two = [far, after(last, heads[1][1])]
        other_two = [other_far, swap(two[1], CORE)]
        was, wbs = [wa, near, *two], [wb, other_near, *other_two]
    else:
        heads.append(attention_forward(code, stream, was[1:2], wbs[1:2]))
    heads.append(attention_forward(code, stream, was[2:], wbs[2:]))
    place_of = ((0, 0), (1, 0), (2, 0), (2, 1))
    ns, na, fg, hg, *halves, vec, vup = ffn(
        code, stream, accumulator, [t[1] for t in heads], outward, outward_bias, first_gain, first_shift, up_weight, up_bias,
        down_weight, down_bias, second_gain, second_shift, stream_cotangent, accumulator_cotangent)

    def backward(slots, code, small=None):
        t = [heads[place_of[s][0]] for s in slots]
        at = [place_of[s][1] for s in slots]
        return attention_backward(code, stream, hg, slots, at, [a[0] for a in t], [a[2] for a in t], [a[1] for a in t], [a[3] for a in t], small)

    if not tuned:
        ga, ka, sa, bga = backward((0, 1), code)
        gb, kb, sb, bgb = backward((2,), code)
        gc, kc, sc, v = backward((3,), code, (vec, vup, bga, bgb))
        wg, bias, dwo, dwu, dwd, rows = general_sums(jnp.concatenate(halves, 0), ((ka, sa), (kb, sb), (kc, sc)), v)
        sg = back_stream(code, fg, [ga, gb, gc], was, wbs)
        vecs, vup = [rows[i * D : (i + 1) * D] for i in range(6)], rows[6 * D : 6 * D + FF]
    else:
        keep0, keep1, send0, send1 = halves
        out = add(keep1, swap(send1, CORE))
        got0 = swap(send0, CORE)
        got = swap(out, STEPS[0])
        ga, ka, sa, bga = backward((0, 1), after(code, out))
        ra = swap(sa, CORE)
        cur = add(add(after(keep0, ka), got0), got)
        out = cur[4:]
        got = swap(out, STEPS[1])
        gb, kb, sb, bgb = backward((2,), after(code, out))
        rb = swap(sb, CORE)
        cur = add(after(cur[:4], kb), got)
        out = cur[2:]
        got = swap(out, STEPS[2])
        gc, kc, sc, v = backward((3,), after(code, out), (vec, vup, bga, bgb))
        rc = swap(sc, CORE)
        cur = add(after(cur[:2], kc), got)
        got = swap(cur, STEPS[3])
        k, s, v = combine(first_combine_kernel, 8 * PART, code, ka, kb, kc, ra, rb, rc, after(v, cur))
        got2 = swap(s, PAIR_STEPS[0])
        sg = back_stream(code, after(fg, s), [ga, gb, gc], was, wbs)
        cur = add(after(cur, sg), got)
        got = swap(cur, STEPS[2])
        k, s, v = combine(combine_kernel, 4 * PART, k, got2, after(v, cur))
        got2 = swap(s, PAIR_STEPS[1])
        k, s, v = combine(combine_kernel, 2 * PART, k, got2, after(v, s))
        got2 = swap(s, PAIR_STEPS[2])
        cur = jnp.concatenate([after(cur, s), got], 0)
        got = swap(cur, STEPS[1])
        got2 = after(got2, cur)
        cur = jnp.concatenate([after(cur, got2), got], 0)
        m = merge(k, got2, v)
        got2 = swap(m, (Y, Y))
        got = swap(cur, STEPS[0])
        other_cur = swap(cur, CORE)
        mine, theirs = core * 2 + (low >> 3), (1 - core) * 2 + (other >> 3)
        wide = widen(mine, low, after(cur, m))
        m = add(after(m, wide[0]), got2)
        k = m[: 2 * PART]
        got2 = swap(k, (X, X))
        wide = widen(theirs, other, after(other_cur, k), wide)
        k = jnp.concatenate([after(k, wide[0]), got2], 0)
        got = after(got, k)
        other_got, other_k = swap(got, CORE), swap(k, CORE)
        wide = widen(mine ^ 1, low, got, wide)
        wg, bias, *vecs, vup = finish(code, k, after(other_k, wide[0]), m)
        dwd, dwu, dwo = widen(theirs ^ 1, other, after(other_got, bias), wide)
        vecs, vup = [t[0] for t in vecs], vup[0]
    return (ns, na, sg, wg, bias, dwo, vecs[0], vecs[1], vecs[2], dwu, vup, dwd, vecs[3], vecs[4], vecs[5])


def solution(mesh):
    tokens = P(("batch", "head"), None)
    in_specs = (tokens, tokens, P(None, None, "head"), P(None, "head")) + (P(),) * 10 + (P("batch"), tokens, tokens)
    out_specs = (tokens,) * 3 + (P(None, None, "head"), P(None, "head")) + (P(),) * 10
    return jax.shard_map(body, mesh=mesh, in_specs=in_specs, out_specs=out_specs, check_vma=False)
```

```python
import math

import jax
import jax.numpy as jnp
from jax import lax
from jax.experimental import pallas as pl
from jax.experimental.pallas import tpu as pltpu
from jax.sharding import PartitionSpec as P

F32, BF = jnp.float32, jnp.bfloat16
ROWS, D, FF, PAIR, HD, SHORT = 1024, 512, 2048, 128, 64, 256
QB = 256
SCALE = 1.0 / math.sqrt(HD)


def dot(a, b):
    return lax.dot_general(a, b, (((1,), (0,)), ((), ())), preferred_element_type=F32)


def dot_nt(a, b):
    return lax.dot_general(a, b, (((1,), (1,)), ((), ())), preferred_element_type=F32)


def dot_tn(a, b):
    return lax.dot_general(a, b, (((0,), (0,)), ((), ())), preferred_element_type=F32)


def params(n=1, mib=60):
    return pltpu.CompilerParams(dimension_semantics=("arbitrary",) * n or None, vmem_limit_bytes=mib << 20)


def cost(flops, nbytes):
    return pl.CostEstimate(flops=int(flops), bytes_accessed=int(nbytes), transcendentals=0)


SMEM = pl.BlockSpec(memory_space=pltpu.SMEM)
VM = pl.BlockSpec(memory_space=pltpu.VMEM)
HBM = pl.BlockSpec(memory_space=pltpu.HBM)


def whole(shape):
    return pl.BlockSpec(shape, lambda *_: (0,) * len(shape))


HALF = D // 2
PACK = 3 * HALF + 16


def side(w):
    return jnp.concatenate([w[c * HALF : (c + 1) * HALF] for c in range(3)], axis=1)


def fwd_kernel(n_pairs, code, x, *refs):
    was, wbs = refs[:n_pairs], refs[n_pairs : 2 * n_pairs]
    e, o, qkv, rl, es, qs_, va, sems, qsems = refs[2 * n_pairs :]
    ca = pl.multiple_of(code[0] * HALF, HALF)
    cb = pl.multiple_of(HALF - code[0] * HALF, HALF)
    lane = lax.broadcasted_iota(jnp.int32, (1, PAIR), 1)

    def run(short):
        copies = []

        def project(a):
            wa, wb = was[a], wbs[a]
            p = dot(x[:, pl.ds(ca, HALF)], side(wa)) + dot(x[:, pl.ds(cb, HALF)], side(wb))
            bq, bv = wa[3 * HALF : 3 * HALF + 1].astype(F32), wa[3 * HALF + 1 : 3 * HALF + 2].astype(F32)
            q = ((p[:, :PAIR] + bq).astype(BF).astype(F32) * SCALE).astype(BF)
            k = p[:, PAIR : 2 * PAIR].astype(BF)
            v = (p[:, 2 * PAIR :] + bv).astype(BF)
            qs_[a, :, :PAIR] = q
            qs_[a, :, PAIR : 2 * PAIR] = k
            qs_[a, :, 2 * PAIR :] = v
            copies.append(pltpu.make_async_copy(qs_.at[a], qkv.at[a], qsems.at[a]))
            copies[-1].start()
            return q, k, [jnp.where((lane < HD) == (h == 0), v, jnp.ones((), BF)) for h in range(2)]

        if short:
            for a in range(n_pairs):
                for h, v in enumerate(project(a)[2]):
                    va[a, h] = v

            def block(a, t):
                rows = slice(t * SHORT, (t + 1) * SHORT)
                q, k = qs_[a, rows, :PAIR], qs_[a, rows, PAIR : 2 * PAIR]
                outs = []
                for h in range(2):
                    sc = dot_nt(jnp.where((lane < HD) == (h == 0), q, jnp.zeros((), BF)), k)
                    ex = jnp.exp(sc - jnp.max(sc, axis=1, keepdims=True)).astype(BF)
                    es[a, h, rows, 0:SHORT] = ex
                    u = dot(ex, va[a, h, rows, :])
                    r = 1.0 / pltpu.roll(u, HD, 1)
                    outs.append((u * r, r))
                o[a, rows, :] = jnp.where(lane < HD, outs[0][0], outs[1][0]).astype(BF)
                rl[a, rows, :] = jnp.where(lane < HD, outs[0][1], outs[1][1])

            def pair(a, carry):
                for t in range(ROWS // SHORT):
                    block(a, t)
                return carry

            lax.fori_loop(0, n_pairs, pair, 0)
            at = (slice(None), slice(None), slice(None), pl.ds(0, SHORT))
            copies.append(pltpu.make_async_copy(es.at[at], e.at[at], sems.at[0]))
            copies[-1].start()
            for c in copies:
                c.wait()
            return

        ready = {0: project(0)}

        def score(item):
            a, qb, h = item
            q, k, _ = ready[a]
            qh = jnp.where((lane < HD) == (h == 0), q[qb * QB : (qb + 1) * QB], jnp.zeros((), BF))
            return dot_nt(qh, k)

        done = {}

        def product(item, ex):
            a, qb, h = item
            qs = slice(qb * QB, (qb + 1) * QB)
            u = dot(ex, ready[a][2][h])
            r = 1.0 / pltpu.roll(u, HD, 1)
            done[h] = (u * r, r)
            if h == 1:
                o[a, qs, :] = jnp.where(lane < HD, done[0][0], done[1][0]).astype(BF)
                rl[a, qs, :] = jnp.where(lane < HD, done[0][1], done[1][1])

        items = [(a, qb, h) for a in range(n_pairs) for qb in range(ROWS // QB) for h in range(2)]
        ahead, last = score(items[0]), None
        for i, item in enumerate(items):
            s = ahead
            if i + 1 < len(items):
                if items[i + 1][0] not in ready:
                    ready[items[i + 1][0]] = project(items[i + 1][0])
                ahead = score(items[i + 1])
            ex = jnp.exp(s - jnp.max(s, axis=1, keepdims=True)).astype(BF)
            a, qb, h = item
            at = (a, h, pl.ds(qb * QB, QB))
            es[at] = ex
            copies.append(pltpu.make_async_copy(es.at[at], e.at[at], sems.at[i]))
            copies[-1].start()
            if last is not None:
                product(*last)
            last = (item, ex)
        product(*last)
        for c in copies:
            c.wait()

    pl.when(code[1] == 1)(lambda: run(False))
    pl.when(code[1] == 0)(lambda: run(True))


def attention_forward(code, x, was, wbs):
    S, n = jax.ShapeDtypeStruct, len(was)
    return pl.pallas_call(
        lambda *refs: fwd_kernel(n, *refs),
        in_specs=[SMEM, VM] + [VM] * (2 * n),
        out_specs=[HBM, VM, HBM, VM],
        out_shape=[S((n, 2, ROWS, ROWS), BF), S((n, ROWS, PAIR), BF), S((n, ROWS, 3 * PAIR), BF), S((n, ROWS, PAIR), F32)],
        scratch_shapes=[pltpu.VMEM((n, 2, ROWS, ROWS), BF), pltpu.VMEM((n, ROWS, 3 * PAIR), BF), pltpu.VMEM((n, 2, ROWS, PAIR), BF),
                        pltpu.SemaphoreType.DMA((8 * n,)), pltpu.SemaphoreType.DMA((n,))],
        compiler_params=params(0),
        cost_estimate=cost(1e6, 1 << 10),
    )(code, x, *was, *wbs)


PART, VROWS = 192, 64


def bwd_kernel(slots, at_o, last, code, x_, hg_, *refs):
    n = len(slots)
    es_, qkvs_, os_, rls_ = (refs[k * n : (k + 1) * n] for k in range(4))
    refs = refs[4 * n :]
    if last:
        (vec, vup, *bg_ins), refs = refs[:4], refs[4:]
        g_, keep, send, v_out, x, e, qkv, o, do, rl, ds, g, gsum, vrow, sva, sda, skm, sqt, sdt, sems, gsems = refs
    else:
        g_, keep, send, bg_out, x, e, qkv, o, do, rl, ds, g, gsum, vrow, sva, sda, skm, sqt, sdt, sems, gsems = refs
    lane = lax.broadcasted_iota(jnp.int32, (1, PAIR), 1)
    first, zero, one = lane < HD, jnp.zeros((), BF), jnp.ones((), BF)
    row = lax.broadcasted_iota(jnp.int32, (PAIR, PAIR), 0)
    col = lax.broadcasted_iota(jnp.int32, (PAIR, PAIR), 1)
    pick = jnp.where(((row < HD) != (col < HD)) & ((col & (HD - 1)) < 2), 1.0, 0.0).astype(BF)
    hs = [slice(h * HD, (h + 1) * HD) for h in range(2)]
    tile = 512
    items = [(t, h) for t in range(ROWS // tile) for h in range(2)]

    def small_loads(a):
        pairs = ((hg_.at[:, pl.ds(slots[a] * PAIR, PAIR)], do), (rls_[a].at[at_o[a]], rl), (os_[a].at[at_o[a]], o), (qkvs_[a].at[at_o[a]], qkv))
        return [pltpu.make_async_copy(src, dst.at[a], sems.at[8 * a + k]) for k, (src, dst) in enumerate(pairs)]

    def e_load(a, i):
        t, h = items[i]
        at = (h, pl.ds(t * tile, tile))
        return pltpu.make_async_copy(es_[a].at[(at_o[a], *at)], e.at[(a, *at)], sems.at[8 * a + 4 + i])

    def e_load_short(a):
        at = (slice(None), slice(None), pl.ds(0, SHORT))
        return pltpu.make_async_copy(es_[a].at[(at_o[a], *at)], e.at[(a, *at)], sems.at[8 * a + 4])

    def store_g(a):
        return pltpu.make_async_copy(g.at[a], g_.at[a], gsems.at[a])

    x_load = pltpu.make_async_copy(x_, x, sems.at[8 * n])

    def prepare(a):
        dof = do[a].astype(F32) * rl[a]
        dob = dof.astype(BF)
        t = dof * o[a].astype(F32)
        th = t.astype(BF)
        tl = (t - th.astype(F32)).astype(BF)
        delta = -(dot(th, pick) + dot(tl, pick))
        dh = delta.astype(BF)
        dd = jnp.where((lane & (HD - 1)) == 0, dh, (delta - dh.astype(F32)).astype(BF))
        q, k, v = qkv[a, :, :PAIR], qkv[a, :, PAIR : 2 * PAIR], qkv[a, :, 2 * PAIR :]
        own = [first == (h == 0) for h in range(2)]
        aug = [jnp.logical_not(own[h]) & ((lane & (HD - 1)) < 2) for h in range(2)]
        va = [jnp.where(own[h], v, jnp.where(aug[h], one, zero)) for h in range(2)]
        da = [jnp.where(own[h], dob, jnp.where(aug[h], dd, zero)) for h in range(2)]
        km = [jnp.where(own[h], k, zero) for h in range(2)]
        return va, da, km, q.astype(F32).T.astype(BF), dof.T.astype(BF)

    def project_back(a):
        gr = dot_tn(x[...], g[a])
        for c in range(3):
            gsum[a, c * D : (c + 1) * D, :] = gr[:, c * PAIR : (c + 1) * PAIR].astype(BF)

    def long():
        for a in range(n):
            for c in small_loads(a) + [e_load(a, i) for i in range(4)]:
                c.start()
        x_load.start()
        for a in range(n):
            for c in small_loads(a):
                c.wait()
            va, da, km, qt, dt = prepare(a)

            def weights(item):
                t, h = item
                return dot_nt(da[h][t * tile : (t + 1) * tile], va[h])

            ahead = weights(items[0])
            for i, item in enumerate(items):
                dp = ahead
                if i + 1 < len(items):
                    ahead = weights(items[i + 1])
                t, h = item
                rows = slice(t * tile, (t + 1) * tile)
                e_load(a, i).wait()
                ds[a, h, rows, :] = e[a, h, rows, :] * dp.astype(BF)
            dq = dot(ds[a, 0], km[0]) + dot(ds[a, 1], km[1])
            g[a, :, :PAIR] = (dq * SCALE).astype(BF)
            vt = [dot(dt[hs[h]], e[a, h]) for h in range(2)]
            kt = [dot(qt[hs[h]], ds[a, h]) for h in range(2)]
            g[a, :, 2 * PAIR :] = jnp.concatenate(vt, 0).T.astype(BF)
            g[a, :, PAIR : 2 * PAIR] = jnp.concatenate(kt, 0).T.astype(BF)
            store_g(a).start()
            if a == 0:
                x_load.wait()
            project_back(a)

    def short():
        for a in range(n):
            for c in small_loads(a) + [e_load_short(a)]:
                c.start()
        x_load.start()
        for a in range(n):
            for c in small_loads(a) + [e_load_short(a)]:
                c.wait()
        x_load.wait()

        def pair(a, carry):
            va, da, km, qt, dt = prepare(a)
            for h in range(2):
                sva[h], sda[h], skm[h] = va[h], da[h], km[h]
            sqt[...] = qt
            sdt[...] = dt

            def block(t, carry):
                rows = pl.ds(pl.multiple_of(t * SHORT, SHORT), SHORT)
                dq, vt, kt = 0.0, [], []
                for h in range(2):
                    ex = e[a, h, rows, 0:SHORT]
                    d = ex * dot_nt(sda[h, rows, :], sva[h, rows, :]).astype(BF)
                    dq = dq + dot(d, skm[h, rows, :])
                    vt.append(dot(sdt[hs[h], rows], ex))
                    kt.append(dot(sqt[hs[h], rows], d))
                g[a, rows, :PAIR] = (dq * SCALE).astype(BF)
                g[a, rows, 2 * PAIR :] = jnp.concatenate(vt, 0).T.astype(BF)
                g[a, rows, PAIR : 2 * PAIR] = jnp.concatenate(kt, 0).T.astype(BF)
                return carry

            lax.fori_loop(0, ROWS // SHORT, block, 0)
            store_g(a).start()
            project_back(a)
            return carry

        lax.fori_loop(0, n, pair, 0)

    pl.when(code[1] == 1)(long)
    pl.when(code[1] == 0)(short)

    def put(i, carry):
        a, j = i // 8, i % 8
        block = gsum[a, pl.ds(pl.multiple_of(j * PART, PART), PART), :]
        rel = (j % 4) ^ code[5]
        if n == 2:
            at = (rel & 1) + jnp.where(j // 4 == 0, (rel >> 1) * 4 + a * 2, (rel >> 1) * 2 + a * 4)
        else:
            at = rel
        rows = pl.ds(pl.multiple_of(at * PART, PART), PART)

        @pl.when(code[0] == j // 4)
        def _():
            keep[rows, :] = block

        @pl.when(code[0] != j // 4)
        def _():
            send[rows, :] = block

        return carry

    lax.fori_loop(0, 8 * n, put, 0)
    for a in range(n):
        store_g(a).wait()
    bgs = [jnp.concatenate([colsum(g[a, :, :PAIR].astype(F32)), colsum(g[a, :, 2 * PAIR :].astype(F32))], 0) for a in range(n)]
    if not last:
        bg_out[...] = jnp.concatenate(bgs + [jnp.zeros((8 - 2 * n, PAIR), F32)], 0)
        return
    for i in range(6):
        for c in range(4):
            vrow[i * 4 + c : i * 4 + c + 1, :] = vec[i : i + 1, c * PAIR : (c + 1) * PAIR]
    for c in range(16):
        vrow[24 + c : 25 + c, :] = vup[0:1, c * PAIR : (c + 1) * PAIR]
    known = [bg_ins[0][0:2], bg_ins[0][2:4], bg_ins[1][0:2]] + bgs
    for p in range(4):
        vrow[40 + 2 * p : 42 + 2 * p, :] = sum(jnp.where((code[4] ^ s) == p, b, 0.0) for s, b in enumerate(known))
    vrow[48:, :] = jnp.zeros((VROWS - 48, PAIR), F32)
    v_out[...] = vrow[...].astype(BF)
    send[4 * n * PART :, :] = v_out[...]


def attention_backward(code, x, hg, slots, at_o, es, qkvs, os, rls, small=None):
    S, n, last = jax.ShapeDtypeStruct, len(slots), small is not None
    ins = [code, x, hg, *es, *qkvs, *os, *rls] + list(small or ())
    rows = 4 * n * PART
    outs = [S((n, ROWS, 3 * PAIR), BF), S((rows, PAIR), BF), S((rows + VROWS * last, PAIR), BF), S((VROWS, PAIR), BF) if last else S((8, PAIR), F32)]
    scratch = [((ROWS, D), BF), ((n, 2, ROWS, ROWS), BF), ((n, ROWS, 3 * PAIR), BF), ((n, ROWS, PAIR), BF), ((n, ROWS, PAIR), BF),
               ((n, ROWS, PAIR), F32), ((n, 2, ROWS, ROWS), BF), ((n, ROWS, 3 * PAIR), BF), ((n, 3 * D, PAIR), BF), ((VROWS, PAIR), F32)]
    scratch += [((2, ROWS, PAIR), BF)] * 3 + [((PAIR, ROWS), BF)] * 2
    return pl.pallas_call(
        lambda *refs: bwd_kernel(slots, at_o, last, *refs),
        in_specs=[SMEM] + [HBM] * (2 + 4 * n) + [VM] * (4 * last),
        out_specs=[HBM, VM, VM, VM],
        out_shape=outs,
        scratch_shapes=[pltpu.VMEM(*a) for a in scratch] + [pltpu.SemaphoreType.DMA((8 * n + 1,)), pltpu.SemaphoreType.DMA((n,))],
        compiler_params=params(0, 44),
        cost_estimate=cost(n * 8e9, n * 8 << 20),
    )(*ins)


def gelu_parts(u):
    cdf = 0.5 + 0.5 * lax.erf(u * math.sqrt(0.5))
    density = jnp.exp2(u * u * (-0.5 * math.log2(math.e))) * (1.0 / math.sqrt(2.0 * math.pi))
    return u * cdf, cdf + u * density


def norm_parts(h):
    m = jnp.mean(h, -1, keepdims=True)
    c = h - m
    r = lax.rsqrt(jnp.mean(c * c, -1, keepdims=True) + 1e-5)
    return c * r, r


def norm_back(e, gain, z, r):
    eg = e * gain
    return r * (eg - jnp.mean(eg, -1, keepdims=True) - z * jnp.mean(eg * z, -1, keepdims=True))


def colsum(a):
    return jnp.sum(a, 0, keepdims=True)


BLOCKS, BLOCK = 16, 144


def place(block, size, base, first, half, code, out):
    low = code[2 + half]
    for s in range(block.shape[0] // size):
        out[(first + s) ^ low, base : base + size, :] = block[s * size : (s + 1) * size].astype(BF)


def ffn_kernel(code, x_, acc_, oa_, ob_, oc_, wo, bo, g1, s1, wu_, bu, wd_, bd, g2, s2, sc_, ac_,
               ns_, na_, fg_, hg_, keep0, keep1, send0, send1, vec, vup,
               x, acc, oa, ob, oc, od, sc, ac, wu, wd, ns, na, fg, hg, keep, send, wp, hid, bfull, lfull, pfull, ofull, afull, isem, osem):
    tiles = [slice(t * QB, (t + 1) * QB) for t in range(ROWS // QB)]
    loads, stores = {}, []

    def load(name, src, dst, t=None):
        at = pl.ds(t * QB, QB) if t is not None else pl.ds(0, src.shape[0])
        loads[name, t] = pltpu.make_async_copy(src.at[at], dst.at[at], isem.at[len(loads)])
        loads[name, t].start()

    def store(src, dst, *at):
        stores.append(pltpu.make_async_copy(src.at[at], dst.at[at], osem.at[len(stores)]))
        stores[-1].start()

    by_tile = (("oa", oa_.at[0], oa), ("ob", ob_.at[0], ob), ("oc", oc_.at[0], oc), ("od", oc_.at[1], od), ("x", x_, x), ("acc", acc_, acc), ("sc", sc_, sc), ("ac", ac_, ac))
    for t in (0, 1):
        for name, src, dst in by_tile[:5]:
            load(name, src, dst, t)
    load("wu", wu_, wu)
    load("wd", wd_, wd)
    for name, src, dst in by_tile[5:]:
        for t in (0, 1):
            load(name, src, dst, t)
    for t in (2, 3):
        for name, src, dst in by_tile:
            load(name, src, dst, t)

    for s in range(D // PAIR):
        at = pl.multiple_of((code[4] ^ s) * PAIR, PAIR)
        wp[s * PAIR : (s + 1) * PAIR, :] = wo[pl.ds(at, PAIR), :]

    def wait(t, *names):
        for name in names:
            loads[name, t].wait()

    sums, up_sum = [0.0] * 6, 0.0
    for group in ((0, 1), (2, 3)):
        att, z1, r1, first, hidden, slope, si, bgs, pgs, ags = {}, {}, {}, {}, {}, {}, {}, {}, {}, {}
        for t in group:
            wait(t, "oa", "ob", "oc", "od")
            ofull[tiles[t], :] = jnp.concatenate([oa[tiles[t]], ob[tiles[t]], oc[tiles[t]], od[tiles[t]]], axis=1)
            att[t] = dot(ofull[tiles[t], :], wp[...]) + bo[...]
        for t in group:
            wait(t, "x")
            z1[t], r1[t] = norm_parts(x[tiles[t]].astype(F32) + att[t])
            first[t] = z1[t] * g1[...] + s1[...]
            lfull[tiles[t], :] = first[t].astype(BF)
        if group[0] == 0:
            wait(None, "wu")
        ups = {t: dot(first[t].astype(BF), wu[...]) for t in group}
        for t in group:
            a, slope[t] = gelu_parts(ups[t] + bu[...])
            hidden[t] = a.astype(BF)
            hid[tiles[t], :] = hidden[t]
        if group[0] == 0:
            wait(None, "wd")
        branch = {t: dot(hidden[t], wd[...]) + bd[...] for t in group}
        for t in group:
            wait(t, "acc", "sc", "ac")
            na[tiles[t]] = acc[tiles[t]] + att[t] + branch[t]
            store(na, na_, pl.ds(t * QB, QB))
            z2, r2 = norm_parts(first[t] + branch[t])
            ns[tiles[t]] = (z2 * g2[...] + s2[...]).astype(BF)
            store(ns, ns_, pl.ds(t * QB, QB))
            e2 = sc[tiles[t]]
            si[t] = norm_back(e2, g2[...], z2, r2)
            bgs[t] = (si[t] + ac[tiles[t]]).astype(BF)
            bfull[tiles[t], :] = bgs[t]
            sums[3:] = [a + colsum(b) for a, b in zip(sums[3:], (bgs[t].astype(F32), e2 * z2, e2))]
        hgs = {t: dot_nt(bgs[t], wd[...]) for t in group}
        for t in group:
            pgs[t] = (hgs[t] * slope[t]).astype(BF)
            pfull[tiles[t], :] = pgs[t]
            up_sum += colsum(pgs[t].astype(F32))
        es = {t: dot_nt(pgs[t], wu[...]) for t in group}
        for t in group:
            e1 = es[t] + si[t]
            fi = norm_back(e1, g1[...], z1[t], r1[t])
            fg[tiles[t]] = fi
            store(fg, fg_, pl.ds(t * QB, QB))
            ags[t] = (fi + ac[tiles[t]]).astype(BF)
            afull[tiles[t], :] = ags[t]
            sums[:3] = [a + colsum(b) for a, b in zip(sums[:3], (ags[t].astype(F32), e1 * z1[t], e1))]
        for t in group:
            hg[tiles[t]] = dot_nt(ags[t], wp[...]).astype(BF)
            store(hg, hg_, pl.ds(t * QB, QB))
    for j, s in enumerate(sums):
        vec[j : j + 1, :] = s
    vec[6:8, :] = jnp.zeros((2, D), F32)
    vup[0:1, :] = up_sum
    quarter = BLOCKS // 2
    for half, out, dsts in ((1, send, (send0, send1)), (0, keep, (keep0, keep1))):

        def ship(base, size):
            for k in (1, 0):
                src = out.at[pl.ds(k * quarter, quarter), pl.ds(base, size)]
                stores.append(pltpu.make_async_copy(src, dsts[k].at[:, pl.ds(base, size)], osem.at[len(stores)]))
                stores[-1].start()

        mine = code[0] ^ half
        for b in range(4):
            at = pl.multiple_of(mine * 1024 + b * 256, 256)
            place(dot_tn(hid[:, pl.ds(at, 256)], bfull[...]), 64, 0, b * 4, half, code, out)
        ship(0, 64)
        for c in range(2):
            at = pl.multiple_of(mine * 1024 + c * 512, 512)
            place(dot_tn(lfull[...], pfull[:, pl.ds(at, 512)]), 64, 64, c * 8, half, code, out)
        ship(64, 64)
        for p in range(2):
            at = pl.multiple_of(((mine * 2 + p) ^ code[4]) * PAIR, PAIR)
            place(dot_tn(ofull[:, pl.ds(at, PAIR)], afull[...]), 16, 128, p * 8, half, code, out)
        ship(128, 16)
    for c in stores:
        c.wait()


def ffn(code, x, acc, os, wo, bo, g1, s1, wu, bu, wd, bd, g2, s2, sc, ac):
    S = jax.ShapeDtypeStruct
    bo, g1, s1, bu, bd, g2, s2 = (v.reshape(1, -1) for v in (bo, g1, s1, bu, bd, g2, s2))
    ins = (code, x, acc, *os, wo, bo, g1, s1, wu, bu, wd, bd, g2, s2, sc, ac)
    specs = [SMEM] + [HBM] * 5 + [VM] * 4 + [HBM, VM, HBM] + [VM] * 3 + [HBM] * 2
    outs = [S((ROWS, D), BF), S((ROWS, D), F32), S((ROWS, D), F32), S((ROWS, D), BF)]
    outs += [S((BLOCKS // 2, BLOCK, D), BF)] * 4 + [S((8, D), F32), S((1, FF), F32)]
    buffers = [x, acc] + [S((ROWS, PAIR), BF)] * 4 + [sc, ac, wu, wd] + outs[:4] + [S((BLOCKS, BLOCK, D), BF)] * 2
    scratch = [pltpu.VMEM(a.shape, a.dtype) for a in buffers]
    scratch += [pltpu.VMEM(s, BF) for s in ((D, D), (ROWS, FF), (ROWS, D), (ROWS, D), (ROWS, FF), (ROWS, D), (ROWS, D))]
    return pl.pallas_call(
        ffn_kernel,
        in_specs=specs,
        out_specs=[HBM] * 8 + [VM] * 2,
        out_shape=outs,
        scratch_shapes=scratch + [pltpu.SemaphoreType.DMA((34,)), pltpu.SemaphoreType.DMA((28,))],
        compiler_params=params(0),
        cost_estimate=cost(25e9, 20 << 20),
    )(*ins)


def back_stream_kernel(code, fg, ga, gb, gc, *refs):
    was, wbs, out = refs[:4], refs[4:8], refs[8]
    ca = pl.multiple_of(code[0] * HALF, HALF)
    cb = pl.multiple_of(HALF - code[0] * HALF, HALF)
    for at, ws in ((ca, was), (cb, wbs)):
        t = fg[:, pl.ds(at, HALF)]
        for s, w in enumerate(ws):
            t = t + dot_nt((ga[0], ga[1], gb[0], gc[0])[s], side(w))
        out[:, pl.ds(at, HALF)] = t


def back_stream(code, fg, gs, was, wbs):
    return pl.pallas_call(
        back_stream_kernel,
        grid=(ROWS // QB,),
        in_specs=[SMEM, pl.BlockSpec((QB, D), lambda i: (i, 0))] + [pl.BlockSpec((g.shape[0], QB, 3 * PAIR), lambda i: (0, i, 0)) for g in gs] + [whole((PACK, PAIR))] * 8,
        out_specs=pl.BlockSpec((QB, D), lambda i: (i, 0)),
        out_shape=jax.ShapeDtypeStruct((ROWS, D), F32),
        compiler_params=params(1, 56),
        cost_estimate=cost(4e9, 8 << 20),
    )(code, fg, *gs, *was, *wbs)


def general_gather(inward, inward_bias):
    full = lax.all_gather(inward, "head", axis=2, tiled=True)
    bias = lax.all_gather(inward_bias, "head", axis=1, tiled=True)
    was, wbs = [], []
    for p in range(D // PAIR):
        cols = slice(p * PAIR, (p + 1) * PAIR)
        tail = jnp.pad(bias[:, cols], ((0, 14), (0, 0)))
        was.append(jnp.concatenate([full[:, :HALF, cols].reshape(3 * HALF, PAIR), tail], 0))
        wbs.append(jnp.concatenate([full[:, HALF:, cols].reshape(3 * HALF, PAIR), tail], 0))
    return was, wbs


def general_sums(blocks, pair_parts, vectors):
    both = ("batch", "head")
    whole_half, vectors = lax.psum((blocks, vectors), both)
    wide = whole_half.astype(F32)
    dwd = wide[:, :64].reshape(FF, D)
    dwu = wide[:, 64:128].reshape(4, D, D).transpose(1, 0, 2).reshape(D, FF)
    dwo = wide[:, 128:].reshape(D, D)
    wg = []
    for k, n in pair_parts:
        if k.shape[0] == 8 * PART:
            k, n = k.reshape(2, 2, 2, PART, PAIR).swapaxes(0, 1), n.reshape(2, 2, 2, PART, PAIR)
        else:
            k, n = k.reshape(1, 2, 2, PART, PAIR), n[: 4 * PART].reshape(1, 2, 2, PART, PAIR)
        wg += [jnp.concatenate([t[a].reshape(4 * PART, PAIR) for t in (k, n)], 0).reshape(3, D, PAIR) for a in range(k.shape[0])]
    wg = lax.psum(lax.psum_scatter(jnp.concatenate(wg, 2), "head", scatter_dimension=2, tiled=True), "batch")
    rows = vectors[:48].astype(F32).reshape(-1)
    bias = rows[5120:].reshape(D // PAIR, 2, PAIR).transpose(1, 0, 2).reshape(2, D)
    width = D // lax.axis_size("head")
    bias = lax.dynamic_slice_in_dim(bias, lax.axis_index("head") * width, width, 1)
    return wg.astype(F32), bias, dwo, dwu, dwd, rows


def swap(x, masks):
    n_batch, n_head = lax.axis_size("batch"), lax.axis_size("head")
    pairs = []
    for b in range(n_batch):
        for h in range(n_head):
            axis, mask = masks[b & 1]
            to = (b ^ mask, h) if axis == "batch" else (b, h ^ mask)
            pairs.append((b * n_head + h, to[0] * n_head + to[1]))
    return lax.ppermute(x, ("batch", "head"), pairs)


CORE = (("batch", 1), ("batch", 1))
X, Y, NEAR, FAR = ("batch", 2), ("batch", 4), ("head", 1), ("head", 2)
STEPS = ((X, NEAR), (NEAR, X), (Y, FAR), (FAR, Y))
PAIR_STEPS = ((X, NEAR), (NEAR, X), (FAR, FAR))


def place_code(steps, core, index):
    code = 0
    for masks in steps:
        bits = []
        for axis, mask in masks:
            bits.append(((index[axis] & mask) > 0).astype(jnp.int32))
        code = code * 2 + jnp.where(core == 0, bits[0], bits[1])
    return code


def add(a, b):
    return (a.astype(F32) + b.astype(F32)).astype(BF)


def after(x, *others):
    return lax.optimization_barrier((x, *others))[0]


def split_sum(total, to, keep, send):
    half = keep.shape[0]
    if to < half:
        keep[to : to + total.shape[0], :] = total
    else:
        send[to - half : to - half + total.shape[0], :] = total


def first_combine_kernel(code, ka, kb, kc, ra, rb, rc, v, keep, send, v_out):
    def place_at(q, far):
        return ((q >> 1) * 4 + far * 2 + (q & 1)) * PART

    for q in range(8):
        rows = slice(q * PART, (q + 1) * PART)
        split_sum(add(ka[rows, :], ra[rows, :]), place_at(q, 0), keep, send)
    for core in range(2):

        @pl.when(code[0] == core)
        def _():
            for k, r, near in ((kb, rb, 0), (kc, rc, 1)):
                for p in range(4):
                    rows = slice(p * PART, (p + 1) * PART)
                    q = (p & 1) + ((p >> 1) * 4 + near * 2 if core == 0 else (p >> 1) * 2 + near * 4)
                    split_sum(add(k[rows, :], r[rows, :]), place_at(q, 1), keep, send)

    v_out[...] = add(v[...], rc[-VROWS:, :])
    send[keep.shape[0] :, :] = v_out[...]


def combine_kernel(k, r, v, keep, send, v_out):
    half = keep.shape[0]
    for to in (0, half):
        split_sum(add(k[to : to + half, :], r[to : to + half, :]), to, keep, send)
    v_out[...] = add(v[...], r[-VROWS:, :])
    send[half:, :] = v_out[...]


def merge_kernel(k, r, v, out):
    n = k.shape[0]
    out[:n, :] = add(k[...], r[:n, :])
    out[n:, :] = add(v[...], r[n:, :])


def merge(k, r, v):
    return pl.pallas_call(
        merge_kernel,
        in_specs=[VM] * 3,
        out_specs=VM,
        out_shape=jax.ShapeDtypeStruct(r.shape, BF),
        compiler_params=pltpu.CompilerParams(vmem_limit_bytes=16 << 20),
        cost_estimate=cost(1e6, 1 << 18),
    )(k, r, v)


def combine(kernel, half, *args):
    S = jax.ShapeDtypeStruct
    return pl.pallas_call(
        kernel,
        in_specs=[SMEM] * (len(args) - 3 > 3) + [VM] * (len(args) - (len(args) - 3 > 3)),
        out_specs=[VM] * 3,
        out_shape=[S((half, PAIR), BF), S((half + VROWS, PAIR), BF), S((VROWS, PAIR), BF)],
        compiler_params=pltpu.CompilerParams(vmem_limit_bytes=16 << 20),
        cost_estimate=cost(1e6, 2 << 20),
    )(*args)


def widen_kernel(code, src, *refs):
    dwd, dwu, dwo = refs[-3:]
    for s in range(4):
        at = (pl.program_id(0) * 4 + s) ^ (code[1] & 7)
        dwd[s * 64 : (s + 1) * 64, :] = src[at, 0:64].astype(F32)
        dwu[s * 64 : (s + 1) * 64, :] = src[at, 64:128].astype(F32)
        dwo[s * 16 : (s + 1) * 16, :] = src[at, 128:144].astype(F32)


def widen(quarter, low, src, before=()):
    S = jax.ShapeDtypeStruct
    spec = pltpu.PrefetchScalarGridSpec(
        num_scalar_prefetch=1,
        grid=(2,),
        in_specs=[VM] + [HBM] * len(before),
        out_specs=[
            pl.BlockSpec((256, D), lambda i, c: (c[0] * 2 + i, 0)),
            pl.BlockSpec((256, D), lambda i, c: (i, c[0])),
            pl.BlockSpec((64, D), lambda i, c: (c[0] * 2 + i, 0)),
        ],
    )
    return pl.pallas_call(
        widen_kernel,
        grid_spec=spec,
        out_shape=[S((FF, D), F32), S((D, FF), F32), S((D, D), F32)],
        input_output_aliases={2 + k: k for k in range(len(before))},
        compiler_params=params(1, 16),
        cost_estimate=cost(1e6, 4 << 20),
    )(jnp.stack([quarter, low]), src, *before)


def finish_kernel(code, own, other, v, wg, bg, *outs):
    for j in range(8):
        rel = (j % 4) ^ code[5]
        at = pl.multiple_of(rel * PART, PART)

        def put(src, j=j, at=at):
            block = src[pl.ds(at, PART), :].astype(F32)
            for r in range(0, PART, 64):
                to = j * PART + r
                wg[to // D, to % D : to % D + 64] = block[r : r + 64]

        pl.when(code[0] == j // 4)(lambda: put(own))
        pl.when(code[0] != j // 4)(lambda: put(other))

    rows = v[2 * PART :, :].astype(F32)
    for i in range(6):
        for c in range(4):
            outs[i][0:1, c * PAIR : (c + 1) * PAIR] = rows[i * 4 + c : i * 4 + c + 1]
    for c in range(16):
        outs[6][0:1, c * PAIR : (c + 1) * PAIR] = rows[24 + c : 25 + c]
    for p in range(4):

        @pl.when(code[4] == p)
        def _():
            bg[...] = rows[40 + 2 * p : 42 + 2 * p]


def finish(code, own, other, v):
    S = jax.ShapeDtypeStruct
    return pl.pallas_call(
        finish_kernel,
        in_specs=[SMEM, VM, VM, VM],
        out_specs=[VM] * 9,
        out_shape=[S((3, D, PAIR), F32), S((2, PAIR), F32)] + [S((1, D), F32)] * 6 + [S((1, FF), F32)],
        compiler_params=pltpu.CompilerParams(vmem_limit_bytes=16 << 20),
        cost_estimate=cost(1e6, 3 << 20),
    )(code, own, other, v)


def body(stream, accumulator, inward, inward_bias, outward, outward_bias, first_gain, first_shift, up_weight, up_bias,
         down_weight, down_bias, second_gain, second_shift, long_count, stream_cotangent, accumulator_cotangent):
    assert stream.shape == (ROWS, D)
    b, h = lax.axis_index("batch"), lax.axis_index("head")
    tuned = (lax.axis_size("batch"), lax.axis_size("head")) == (8, 4)
    flag = (h < long_count[0]).astype(jnp.int32)
    zero = jnp.zeros((), jnp.int32)
    if tuned:
        core, index = b & 1, {"batch": b, "head": h}
        low, other = (2 * place_code(STEPS[:3], c, index) for c in (core, 1 - core))
        across = 2 * place_code(((X, X),), core, index)
        code = jnp.stack([core, flag, low, other, h, across, zero, zero])
        bias = jnp.pad(inward_bias, ((0, 14), (0, 0)))
        packs = [jnp.concatenate([inward[0, r], inward[1, r], inward[2, r], bias], 0) for r in (slice(0, HALF), slice(HALF, D))]
        wa, wb = jnp.where(core == 0, packs[0], packs[1]), jnp.where(core == 0, packs[1], packs[0])
        was, wbs = [wa], [wb]
    else:
        code = jnp.stack([zero, flag] + [zero] * 6)
        was, wbs = general_gather(inward, inward_bias)

    heads = [attention_forward(code, stream, was[:1], wbs[:1])]
    if tuned:
        far, near = lax.optimization_barrier((swap(wa, (FAR, FAR)), swap(wa, (NEAR, NEAR)), heads[0][1]))[:2]
        other_far, other_near, last = swap(far, CORE), swap(near, CORE), swap(far, (NEAR, NEAR))
        heads.append(attention_forward(code, stream, [near], [other_near]))
        two = [far, after(last, heads[1][1])]
        other_two = [other_far, swap(two[1], CORE)]
        was, wbs = [wa, near, *two], [wb, other_near, *other_two]
    else:
        heads.append(attention_forward(code, stream, was[1:2], wbs[1:2]))
    heads.append(attention_forward(code, stream, was[2:], wbs[2:]))
    place_of = ((0, 0), (1, 0), (2, 0), (2, 1))
    ns, na, fg, hg, *halves, vec, vup = ffn(
        code, stream, accumulator, [t[1] for t in heads], outward, outward_bias, first_gain, first_shift, up_weight, up_bias,
        down_weight, down_bias, second_gain, second_shift, stream_cotangent, accumulator_cotangent)

    def backward(slots, code, small=None):
        t = [heads[place_of[s][0]] for s in slots]
        at = [place_of[s][1] for s in slots]
        return attention_backward(code, stream, hg, slots, at, [a[0] for a in t], [a[2] for a in t], [a[1] for a in t], [a[3] for a in t], small)

    if not tuned:
        ga, ka, sa, bga = backward((0, 1), code)
        gb, kb, sb, bgb = backward((2,), code)
        gc, kc, sc, v = backward((3,), code, (vec, vup, bga, bgb))
        wg, bias, dwo, dwu, dwd, rows = general_sums(jnp.concatenate(halves, 0), ((ka, sa), (kb, sb), (kc, sc)), v)
        sg = back_stream(code, fg, [ga, gb, gc], was, wbs)
        vecs, vup = [rows[i * D : (i + 1) * D] for i in range(6)], rows[6 * D : 6 * D + FF]
    else:
        keep0, keep1, send0, send1 = halves
        out = add(keep1, swap(send1, CORE))
        got0 = swap(send0, CORE)
        got = swap(out, STEPS[0])
        ga, ka, sa, bga = backward((0, 1), after(code, out))
        ra = swap(sa, CORE)
        cur = add(add(after(keep0, ka), got0), got)
        out = cur[4:]
        got = swap(out, STEPS[1])
        gb, kb, sb, bgb = backward((2,), after(code, out))
        rb = swap(sb, CORE)
        cur = add(after(cur[:4], kb), got)
        out = cur[2:]
        got = swap(out, STEPS[2])
        gc, kc, sc, v = backward((3,), after(code, out), (vec, vup, bga, bgb))
        rc = swap(sc, CORE)
        cur = add(after(cur[:2], kc), got)
        got = swap(cur, STEPS[3])
        k, s, v = combine(first_combine_kernel, 8 * PART, code, ka, kb, kc, ra, rb, rc, after(v, cur))
        got2 = swap(s, PAIR_STEPS[0])
        sg = back_stream(code, after(fg, s), [ga, gb, gc], was, wbs)
        cur = add(after(cur, sg), got)
        got = swap(cur, STEPS[2])
        k, s, v = combine(combine_kernel, 4 * PART, k, got2, after(v, cur))
        got2 = swap(s, PAIR_STEPS[1])
        k, s, v = combine(combine_kernel, 2 * PART, k, got2, after(v, s))
        got2 = swap(s, PAIR_STEPS[2])
        cur = jnp.concatenate([after(cur, s), got], 0)
        got = swap(cur, STEPS[1])
        got2 = after(got2, cur)
        cur = jnp.concatenate([after(cur, got2), got], 0)
        m = merge(k, got2, v)
        got2 = swap(m, (Y, Y))
        got = swap(cur, STEPS[0])
        other_cur = swap(cur, CORE)
        mine, theirs = core * 2 + (low >> 3), (1 - core) * 2 + (other >> 3)
        wide = widen(mine, low, after(cur, m))
        m = add(after(m, wide[0]), got2)
        k = m[: 2 * PART]
        got2 = swap(k, (X, X))
        wide = widen(theirs, other, after(other_cur, k), wide)
        k = jnp.concatenate([after(k, wide[0]), got2], 0)
        got = after(got, k)
        other_got, other_k = swap(got, CORE), swap(k, CORE)
        wide = widen(mine ^ 1, low, got, wide)
        wg, bias, *vecs, vup = finish(code, k, after(other_k, wide[0]), m)
        dwd, dwu, dwo = widen(theirs ^ 1, other, after(other_got, bias), wide)
        vecs, vup = [t[0] for t in vecs], vup[0]
    return (ns, na, sg, wg, bias, dwo, vecs[0], vecs[1], vecs[2], dwu, vup, dwd, vecs[3], vecs[4], vecs[5])


def solution(mesh):
    tokens = P(("batch", "head"), None)
    in_specs = (tokens, tokens, P(None, None, "head"), P(None, "head")) + (P(),) * 10 + (P("batch"), tokens, tokens)
    out_specs = (tokens,) * 3 + (P(None, None, "head"), P(None, "head")) + (P(),) * 10
    return jax.shard_map(body, mesh=mesh, in_specs=in_specs, out_specs=out_specs, check_vma=False)
```
